32 devices in a mesh: dp: 4 (over y, x), seq: 8 (over z, core).
Axes of the slice: x: 2, y: 2, z: 4, core: 2. Of those that a mesh axis runs over, the one named last changes fastest.
Arguments:
- hidden_in: bfloat16 [8, 4096, 1024], P('dp', 'seq'), may hold values from -6 to 6
- segment_ids: int32 [8, 4096], P('dp'), may hold values from 0 to 256, as said below
- query_weight: bfloat16 [1024, 1024], P(('dp', 'seq')), may hold values from -0.1875 to 0.1875
- query_bias: bfloat16 [1024], P(('dp', 'seq')), may hold values from -3 to 3
- key_weight: bfloat16 [1024, 1024], P(('dp', 'seq')), may hold values from -0.1875 to 0.1875
- value_weight: bfloat16 [1024, 1024], P(('dp', 'seq')), may hold values from -0.1875 to 0.1875
- value_bias: bfloat16 [1024], P(('dp', 'seq')), may hold values from -3 to 3
- output_weight: bfloat16 [1024, 1024], P(('dp', 'seq')), may hold values from -0.5 to 0.5
- output_bias: bfloat16 [1024], P(('dp', 'seq')), may hold values from -3 to 3
- first_gain: bfloat16 [1024], P(('dp', 'seq')), may hold values from 0.5 to 1.5
- first_shift: bfloat16 [1024], P(('dp', 'seq')), may hold values from -3 to 3
- inner_weight: bfloat16 [1024, 4096], P(('dp', 'seq')), may hold values from -0.1875 to 0.1875
- inner_bias: bfloat16 [4096], P(('dp', 'seq')), may hold values from -3 to 3
- outer_weight: bfloat16 [4096, 1024], P(('dp', 'seq')), may hold values from -0.09375 to 0.09375
- outer_bias: bfloat16 [1024], P(('dp', 'seq')), may hold values from -3 to 3
- second_gain: bfloat16 [1024], P(('dp', 'seq')), may hold values from 0.5 to 1.5
- second_shift: bfloat16 [1024], P(('dp', 'seq')), may hold values from -3 to 3
- cotangent: bfloat16 [8, 4096, 1024], P('dp', 'seq'), may hold values from -6 to 6
Outputs:
- layer_out: bfloat16 [8, 4096, 1024], P('dp', 'seq')
- grad_hidden: float32 [8, 4096, 1024], P('dp', 'seq')
- query_weight_grad: float32 [1024, 1024], P(('dp', 'seq'))
- query_bias_grad: float32 [1024], P(('dp', 'seq'))
- key_weight_grad: float32 [1024, 1024], P(('dp', 'seq'))
- value_weight_grad: float32 [1024, 1024], P(('dp', 'seq'))
- value_bias_grad: float32 [1024], P(('dp', 'seq'))
- output_weight_grad: float32 [1024, 1024], P(('dp', 'seq'))
- output_bias_grad: float32 [1024], P(('dp', 'seq'))
- first_gain_grad: float32 [1024], P(('dp', 'seq'))
- first_shift_grad: float32 [1024], P(('dp', 'seq'))
- inner_weight_grad: float32 [1024, 4096], P(('dp', 'seq'))
- inner_bias_grad: float32 [4096], P(('dp', 'seq'))
- outer_weight_grad: float32 [4096, 1024], P(('dp', 'seq'))
- outer_bias_grad: float32 [1024], P(('dp', 'seq'))
- second_gain_grad: float32 [1024], P(('dp', 'seq'))
- second_shift_grad: float32 [1024], P(('dp', 'seq'))
The draws below stay inside these ranges and needn't reach their ends.
Inputs may be any that keep to these rules, and one draw needn't show every extreme that they name: `segment_ids`: ids never fall along a row and restart for each row; the tokens of a segment are contiguous and its id is positive; 0 marks padding at a row's end, and every row ends in padding. Each segment holds 16 to 256 tokens, a row's first exactly 256, and no segment other than a row's first starts at a position divisible by 512. A row's last segment has the id 4096 // 16.
All inputs are finite; a program needn't handle non-finite values.
Results may differ from the reference program's by a relative error of at most 0.014.
Values may be sent and summed in bfloat16 or wider, within the bound.
A program may use at most 256 MiB of HBM per device.

```python
import jax
import jax.numpy as jnp
from jax import lax

D = 1024
H = 16
HD = 64
FF = 4096
TOK_DEV = 512
SEGMAX = 256
SEGMIN = 16
ROW = 4096
ROWS = 8


def draw_segment_ids(key, part):
    key = jax.random.fold_in(key, 11)
    count = ROW // SEGMIN + 1
    lengths = jax.random.randint(key, (ROWS, count), SEGMIN, SEGMAX // 2 + 1)
    lengths = lengths.at[:, 0].set(SEGMAX)
    ends = jnp.cumsum(lengths, axis=1)
    starts = ends - lengths
    keep = (starts % TOK_DEV != 0) | (starts == 0)
    marks = jnp.zeros((ROWS, ROW + 1), jnp.int32)
    row_index = jnp.broadcast_to(jnp.arange(ROWS)[:, None], (ROWS, count))
    marks = marks.at[row_index, jnp.minimum(starts, ROW)].add(keep.astype(jnp.int32))
    numbers = jnp.cumsum(marks[:, :ROW], axis=1)
    complete = jnp.max(jnp.where(ends < ROW, ends, 0), axis=1)
    position = jnp.arange(ROW)
    inside = position[None, :] < complete[:, None]
    numbers = jnp.where(inside, numbers, 0)
    last = jnp.max(numbers, axis=1)
    numbers = jnp.where(inside & (numbers == last[:, None]), ROW // SEGMIN, numbers)
    return numbers.astype(jnp.int32)


def levels(key, shape, split, smallest, high):
    loudness = 1.0
    for dim, blocks in split:
        steps = jax.random.uniform(jax.random.fold_in(jax.random.fold_in(key, 6), dim), (blocks,), jnp.float32, smallest / len(split), high / len(split))
        loudness = loudness * jnp.repeat(jnp.exp(steps), shape[dim] // blocks).reshape((-1,) + (1,) * (len(shape) - 1 - dim))
    return loudness


def scatter_about(stream_key, dims, deviation, limit, split=(), kind=jnp.bfloat16):
    values = deviation * jax.random.normal(stream_key, dims, jnp.float32)
    if split:
        values = values * levels(stream_key, dims, split, -0.22, 0.18)
    return jnp.clip(values, -limit, limit).astype(kind)


def setup_inputs(seed: int = 0) -> dict:
    key_of = jax.random.split(jax.random.key(seed), 19)
    return {
        "hidden_in": scatter_about(key_of[0], (ROWS, ROW, D), 1.0, 6.0, ((0, 4), (1, 8))),
        "segment_ids": draw_segment_ids(jax.random.fold_in(key_of[18], 71), 0),
        "query_weight": scatter_about(key_of[2], (D, D), D ** -0.5, 0.1875, ((0, 32),)),
        "query_bias": scatter_about(key_of[3], (D,), 0.5, 3.0, ((0, 32),)),
        "key_weight": scatter_about(key_of[4], (D, D), D ** -0.5, 0.1875, ((0, 32),)),
        "value_weight": scatter_about(key_of[5], (D, D), D ** -0.5, 0.1875, ((0, 32),)),
        "value_bias": scatter_about(key_of[6], (D,), 0.5, 3.0, ((0, 32),)),
        "output_weight": scatter_about(key_of[7], (D, D), (D // 8) ** -0.5, 0.5, ((0, 32),)),
        "output_bias": scatter_about(key_of[8], (D,), 0.5, 3.0, ((0, 32),)),
        "first_gain": jnp.clip(1.0 + 0.1 * jax.random.normal(key_of[9], (D,), jnp.float32), 0.5, 1.5).astype(jnp.bfloat16),
        "first_shift": scatter_about(key_of[10], (D,), 0.5, 3.0, ((0, 32),)),
        "inner_weight": scatter_about(key_of[11], (D, FF), D ** -0.5, 0.1875, ((0, 32),)),
        "inner_bias": scatter_about(key_of[12], (FF,), 0.5, 3.0, ((0, 32),)),
        "outer_weight": scatter_about(key_of[13], (FF, D), FF ** -0.5, 0.09375, ((0, 32),)),
        "outer_bias": scatter_about(key_of[14], (D,), 0.5, 3.0, ((0, 32),)),
        "second_gain": jnp.clip(1.0 + 0.1 * jax.random.normal(key_of[15], (D,), jnp.float32), 0.5, 1.5).astype(jnp.bfloat16),
        "second_shift": scatter_about(key_of[16], (D,), 0.5, 3.0, ((0, 32),)),
        "cotangent": scatter_about(key_of[17], (ROWS, ROW, D), 1.0, 6.0, ((0, 4), (1, 8))),
    }


@jax.custom_vjp
def low(v):
    return lax.optimization_barrier(v.astype(jnp.bfloat16)).astype(jnp.float32)

@jax.custom_vjp
def low_back(v):
    return v

def low_keep(v):
    return (low(v), None)

def low_pass(kept, grad):
    return (grad,)

def back_keep(v):
    return (v, None)

def back_low(kept, grad):
    return (low(grad),)
low.defvjp(low_keep, low_pass)
low_back.defvjp(back_keep, back_low)

def matmul(left, right):
    return jnp.dot(left, right, precision=lax.Precision.HIGHEST)

def normalize(hidden, gain, shift):
    center = hidden - lax.optimization_barrier(jnp.mean(hidden, axis=-1, keepdims=True))
    spread = lax.optimization_barrier(jnp.mean(center * center, axis=-1, keepdims=True))
    return center * lax.rsqrt(spread + 1e-05) * gain + shift

def layer(row_in, params, row_ids):
    query_w, query_b, key_w, value_w, value_b, output_w, output_b, first_g, first_b, inner_w, inner_b, outer_w, outer_b, second_g, second_b = params
    queries = low_back(low(matmul(row_in, query_w) + query_b))
    keys = low_back(low(matmul(row_in, key_w)))
    values = low_back(low(matmul(row_in, value_w) + value_b))
    window = TOK_DEV + SEGMAX
    blocks = ROW // TOK_DEV
    key_pad = jnp.concatenate([jnp.zeros((SEGMAX, D), keys.dtype), keys], axis=0)
    value_pad = jnp.concatenate([jnp.zeros((SEGMAX, D), values.dtype), values], axis=0)
    ids_pad = jnp.concatenate([jnp.full((SEGMAX,), -1, jnp.int32), row_ids.astype(jnp.int32)], axis=0)
    query_blocks = queries.reshape(blocks, TOK_DEV, H, HD)
    query_ids = row_ids.astype(jnp.int32).reshape(blocks, TOK_DEV)
    starts = (jnp.arange(blocks) * TOK_DEV).astype(jnp.int32)
    diagonal = jnp.arange(window)[None, :] == jnp.arange(TOK_DEV)[:, None] + SEGMAX

    def one_block(items):
        block_q, block_ids, start = items
        block_k = lax.dynamic_slice_in_dim(key_pad, start, window, 0).reshape(window, H, HD)
        block_v = lax.dynamic_slice_in_dim(value_pad, start, window, 0).reshape(window, H, HD)
        key_ids = lax.dynamic_slice_in_dim(ids_pad, start, window, 0)
        visible = (block_ids[:, None] == key_ids[None, :]) & (block_ids[:, None] > 0) | diagonal
        scores = low_back(jnp.einsum('qhd,khd->hqk', block_q, block_k, precision=lax.Precision.HIGHEST) * 0.125)
        scores = jnp.where(visible[None], scores, -1e+30)
        probs = low(jax.nn.softmax(scores, axis=-1))
        mixed = jnp.einsum('hqk,khd->qhd', probs, block_v, precision=lax.Precision.HIGHEST)
        return mixed.reshape(TOK_DEV, D)
    mixed = lax.map(jax.checkpoint(one_block), (query_blocks, query_ids, starts)).reshape(ROW, D)
    mixed = low_back(low(mixed))
    attended = low_back(matmul(mixed, output_w) + output_b)
    normed = normalize(row_in + attended, first_g, first_b)
    inner = low_back(matmul(low(normed), inner_w) + inner_b)
    active = low(jax.nn.gelu(inner, approximate=False))
    outer = low_back(matmul(active, outer_w) + outer_b)
    return normalize(normed + outer, second_g, second_b)

def reference(hidden_in, segment_ids, query_weight, query_bias, key_weight, value_weight, value_bias, output_weight, output_bias, first_gain, first_shift, inner_weight, inner_bias, outer_weight, outer_bias, second_gain, second_shift, cotangent):
    params = tuple((weight.astype(jnp.float32) for weight in (query_weight, query_bias, key_weight, value_weight, value_bias, output_weight, output_bias, first_gain, first_shift, inner_weight, inner_bias, outer_weight, outer_bias, second_gain, second_shift)))

    def per_row(totals, items):
        row_in, row_cot, row_ids = items
        result, pull = jax.vjp(lambda first, second: layer(first, second, row_ids), row_in, params)
        row_grad, param_grads = pull(row_cot)
        totals = jax.tree.map(lambda left, right: left + right, totals, param_grads)
        return (totals, (result.astype(jnp.bfloat16), row_grad))
    zeros = tuple((jnp.zeros_like(weight) for weight in params))
    totals, (outputs, grads) = lax.scan(per_row, zeros, (hidden_in.astype(jnp.float32), cotangent.astype(jnp.float32), segment_ids))
    return (outputs, grads, totals[0], totals[1], totals[2], totals[3], totals[4], totals[5], totals[6], totals[7], totals[8], totals[9], totals[10], totals[11], totals[12], totals[13], totals[14])
```

```python
import functools

import jax
import jax.numpy as jnp
from jax import lax
from jax.experimental import pallas as pl
from jax.experimental.pallas import tpu as pltpu
from jax.sharding import PartitionSpec as P

HD = 64
SEGMAX = 256
EPS = 1e-05
LOG2E = 1.4426950408889634
SCORE_SCALE = 0.125 * LOG2E
HIDDEN = -1e30
PAIR = 2 * HD
MESH = pl.DeviceIdType.MESH
BF16 = jnp.bfloat16
F32 = jnp.float32
MIB = 2**20


group_heads = 4


def passed_along(block, axis, distance):
    devices = range(lax.axis_size(axis))
    route = [(i - distance, i) for i in devices if i - distance in devices]
    return lax.ppermute(block, axis, route)


def normalize(hidden, gain, shift):
    center = hidden - jnp.mean(hidden, axis=-1, keepdims=True)
    spread = jnp.mean(center * center, axis=-1, keepdims=True)
    return center * lax.rsqrt(spread + 1e-05) * gain + shift


def contract_rows(left, right):
    return lax.dot_general(
        left, right, (((0,), (0,)), ((), ())), preferred_element_type=jnp.float32
    )


def times_transposed(left, right):
    return lax.dot_general(
        left, right, (((1,), (1,)), ((), ())), preferred_element_type=jnp.float32
    )


def column_sum(values):
    return jnp.sum(values.astype(jnp.float32), axis=0)


def plain(
    hidden_in,
    segment_ids,
    query_weight,
    query_bias,
    key_weight,
    value_weight,
    value_bias,
    output_weight,
    output_bias,
    first_gain,
    first_shift,
    inner_weight,
    inner_bias,
    outer_weight,
    outer_bias,
    second_gain,
    second_shift,
    cotangent,
):
    rows_here, tokens, width = hidden_in.shape
    window = tokens + SEGMAX
    span = group_heads * HD
    groups = width // span
    items = jnp.arange(rows_here * groups, dtype=jnp.int32)
    (
        query_matrix,
        query_offset,
        key_matrix,
        value_matrix,
        value_offset,
        output_matrix,
        output_offset,
        first_scale,
        first_offset,
    ) = (
        lax.all_gather(query_weight, ("dp", "seq"), axis=0, tiled=True),
        lax.all_gather(query_bias, ("dp", "seq"), axis=0, tiled=True),
        lax.all_gather(key_weight, ("dp", "seq"), axis=0, tiled=True),
        lax.all_gather(value_weight, ("dp", "seq"), axis=0, tiled=True),
        lax.all_gather(value_bias, ("dp", "seq"), axis=0, tiled=True),
        lax.all_gather(output_weight, ("dp", "seq"), axis=0, tiled=True),
        lax.all_gather(output_bias, ("dp", "seq"), axis=0, tiled=True),
        lax.all_gather(first_gain, ("dp", "seq"), axis=0, tiled=True),
        lax.all_gather(first_shift, ("dp", "seq"), axis=0, tiled=True),
    )
    flat = hidden_in.reshape(rows_here * tokens, width)
    offset = lax.axis_index("seq") * tokens
    padded_ids = jnp.concatenate(
        [jnp.full((rows_here, SEGMAX), -1, jnp.int32), segment_ids], axis=1
    )
    key_ids = lax.dynamic_slice_in_dim(padded_ids, offset, window, 1)
    query_ids = key_ids[:, SEGMAX:]
    diagonal = jnp.arange(window)[None, :] == jnp.arange(tokens)[:, None] + SEGMAX
    visible = (query_ids[:, :, None] == key_ids[:, None, :]) & (
        query_ids[:, :, None] > 0
    ) | diagonal[None]
    queries = (
        (
            jnp.dot(flat, query_matrix, preferred_element_type=jnp.float32)
            + query_offset.astype(jnp.float32)
        )
        .astype(jnp.bfloat16)
        .reshape(rows_here, tokens, width)
    )
    keys_own = (
        jnp.dot(flat, key_matrix, preferred_element_type=jnp.float32)
        .astype(jnp.bfloat16)
        .reshape(rows_here, tokens, width)
    )
    values_own = (
        (
            jnp.dot(flat, value_matrix, preferred_element_type=jnp.float32)
            + value_offset.astype(jnp.float32)
        )
        .astype(jnp.bfloat16)
        .reshape(rows_here, tokens, width)
    )
    tails = passed_along(
        (keys_own[:, tokens - SEGMAX :], values_own[:, tokens - SEGMAX :]), "seq", 1
    )
    keys_all = jnp.concatenate([tails[0], keys_own], axis=1)
    values_all = jnp.concatenate([tails[1], values_own], axis=1)

    def pieces(item):
        row = item // groups
        column = item % groups * span
        query_part = lax.dynamic_slice(queries, (row, 0, column), (1, tokens, span))[0].reshape(
            tokens, group_heads, HD
        )
        key_part = lax.dynamic_slice(keys_all, (row, 0, column), (1, window, span))[0].reshape(
            window, group_heads, HD
        )
        value_part = lax.dynamic_slice(values_all, (row, 0, column), (1, window, span))[0].reshape(
            window, group_heads, HD
        )
        mask_row = lax.dynamic_index_in_dim(visible, row, 0, keepdims=False)
        scores = (
            jnp.einsum("qhd,khd->hqk", query_part, key_part, preferred_element_type=jnp.float32)
            * 0.125
        )
        scores = jnp.where(mask_row[None], scores, -1e30)
        return (row, column, query_part, key_part, value_part, scores)

    def attend(item):
        row, column, query_part, key_part, value_part, scores = pieces(item)
        highest = jnp.max(scores, axis=-1, keepdims=True)
        expo = jnp.exp(scores - highest)
        total = jnp.sum(expo, axis=-1, keepdims=True)
        probs = (expo / total).astype(jnp.bfloat16)
        mixed_part = jnp.einsum(
            "hqk,khd->qhd", probs, value_part, preferred_element_type=jnp.float32
        )
        return (
            mixed_part.astype(jnp.bfloat16).reshape(tokens, span),
            highest[..., 0] + jnp.log(total[..., 0]),
        )

    mixed_parts, logsums = lax.map(attend, items)
    mixed = (
        mixed_parts.reshape(rows_here, groups, tokens, span)
        .transpose(0, 2, 1, 3)
        .reshape(rows_here * tokens, width)
    )
    first_sum = (
        flat.astype(jnp.float32)
        + jnp.dot(mixed, output_matrix, preferred_element_type=jnp.float32)
        + output_offset.astype(jnp.float32)
    )
    normed = normalize(first_sum, first_scale.astype(jnp.float32), first_offset.astype(jnp.float32))
    normed_low = normed.astype(jnp.bfloat16)
    inner_matrix, inner_offset, outer_matrix, outer_offset, second_scale, second_offset = (
        lax.all_gather(inner_weight, ("dp", "seq"), axis=0, tiled=True),
        lax.all_gather(inner_bias, ("dp", "seq"), axis=0, tiled=True),
        lax.all_gather(outer_weight, ("dp", "seq"), axis=0, tiled=True),
        lax.all_gather(outer_bias, ("dp", "seq"), axis=0, tiled=True),
        lax.all_gather(second_gain, ("dp", "seq"), axis=0, tiled=True),
        lax.all_gather(second_shift, ("dp", "seq"), axis=0, tiled=True),
    )
    inner = jnp.dot(
        normed_low, inner_matrix, preferred_element_type=jnp.float32
    ) + inner_offset.astype(jnp.float32)
    active_low = jax.nn.gelu(inner, approximate=False).astype(jnp.bfloat16)
    second_sum = (
        normed
        + jnp.dot(active_low, outer_matrix, preferred_element_type=jnp.float32)
        + outer_offset.astype(jnp.float32)
    )
    layer_out = normalize(
        second_sum, second_scale.astype(jnp.float32), second_offset.astype(jnp.float32)
    )
    layer_out = layer_out.astype(jnp.bfloat16).reshape(rows_here, tokens, width)
    inner_matrix, inner_offset, outer_matrix, outer_offset, second_scale, second_offset = (
        lax.all_gather(inner_weight, ("dp", "seq"), axis=0, tiled=True),
        lax.all_gather(inner_bias, ("dp", "seq"), axis=0, tiled=True),
        lax.all_gather(outer_weight, ("dp", "seq"), axis=0, tiled=True),
        lax.all_gather(outer_bias, ("dp", "seq"), axis=0, tiled=True),
        lax.all_gather(second_gain, ("dp", "seq"), axis=0, tiled=True),
        lax.all_gather(second_shift, ("dp", "seq"), axis=0, tiled=True),
    )
    upstream = cotangent.reshape(rows_here * tokens, width).astype(jnp.float32)
    _, pull_second = jax.vjp(
        normalize, second_sum, second_scale.astype(jnp.float32), second_offset.astype(jnp.float32)
    )
    grad_second, second_gain_grad, second_shift_grad = pull_second(upstream)
    outer_grad = grad_second.astype(jnp.bfloat16)
    outer_weight_grad = contract_rows(active_low, outer_grad)
    outer_bias_grad = column_sum(outer_grad)
    _, pull_gelu = jax.vjp(lambda value: jax.nn.gelu(value, approximate=False), inner)
    (inner_grad_full,) = pull_gelu(times_transposed(outer_grad, outer_matrix))
    inner_grad = inner_grad_full.astype(jnp.bfloat16)
    inner_weight_grad = contract_rows(normed_low, inner_grad)
    inner_bias_grad = column_sum(inner_grad)
    grad_normed = grad_second + times_transposed(inner_grad, inner_matrix)
    (
        query_matrix,
        query_offset,
        key_matrix,
        value_matrix,
        value_offset,
        output_matrix,
        output_offset,
        first_scale,
        first_offset,
    ) = (
        lax.all_gather(query_weight, ("dp", "seq"), axis=0, tiled=True),
        lax.all_gather(query_bias, ("dp", "seq"), axis=0, tiled=True),
        lax.all_gather(key_weight, ("dp", "seq"), axis=0, tiled=True),
        lax.all_gather(value_weight, ("dp", "seq"), axis=0, tiled=True),
        lax.all_gather(value_bias, ("dp", "seq"), axis=0, tiled=True),
        lax.all_gather(output_weight, ("dp", "seq"), axis=0, tiled=True),
        lax.all_gather(output_bias, ("dp", "seq"), axis=0, tiled=True),
        lax.all_gather(first_gain, ("dp", "seq"), axis=0, tiled=True),
        lax.all_gather(first_shift, ("dp", "seq"), axis=0, tiled=True),
    )
    _, pull_first = jax.vjp(
        normalize, first_sum, first_scale.astype(jnp.float32), first_offset.astype(jnp.float32)
    )
    grad_first, first_gain_grad, first_shift_grad = pull_first(grad_normed)
    attn_grad = grad_first.astype(jnp.bfloat16)
    output_weight_grad = contract_rows(mixed, attn_grad)
    output_bias_grad = column_sum(attn_grad)
    grad_mixed = (
        times_transposed(attn_grad, output_matrix)
        .astype(jnp.bfloat16)
        .reshape(rows_here, tokens, width)
    )

    def attend_back(item):
        row, column, query_part, key_part, value_part, scores = pieces(item)
        logsum = lax.dynamic_index_in_dim(logsums, item, 0, keepdims=False)
        grad_part = lax.dynamic_slice(grad_mixed, (row, 0, column), (1, tokens, span))[0].reshape(
            tokens, group_heads, HD
        )
        probs = jnp.exp(scores - logsum[..., None])
        dprob = jnp.einsum(
            "qhd,khd->hqk", grad_part, value_part, preferred_element_type=jnp.float32
        )
        delta = jnp.sum(probs * dprob, axis=-1, keepdims=True)
        score_grad = (probs * (dprob - delta)).astype(jnp.bfloat16)
        query_part_grad = (
            jnp.einsum("hqk,khd->qhd", score_grad, key_part, preferred_element_type=jnp.float32)
            * 0.125
        )
        key_part_grad = (
            jnp.einsum("hqk,qhd->khd", score_grad, query_part, preferred_element_type=jnp.float32)
            * 0.125
        )
        value_part_grad = jnp.einsum(
            "hqk,qhd->khd",
            probs.astype(jnp.bfloat16),
            grad_part,
            preferred_element_type=jnp.float32,
        )
        return (
            query_part_grad.reshape(tokens, span),
            key_part_grad.reshape(window, span),
            value_part_grad.reshape(window, span),
        )

    query_parts, key_parts, value_parts = lax.map(attend_back, items)
    query_full = (
        query_parts.reshape(rows_here, groups, tokens, span)
        .transpose(0, 2, 1, 3)
        .reshape(rows_here * tokens, width)
    )
    key_window = (
        key_parts.reshape(rows_here, groups, window, span)
        .transpose(0, 2, 1, 3)
        .reshape(rows_here, window, width)
    )
    value_window = (
        value_parts.reshape(rows_here, groups, window, span)
        .transpose(0, 2, 1, 3)
        .reshape(rows_here, window, width)
    )
    returned = (
        passed_along(key_window[:, :SEGMAX].astype(jnp.bfloat16), "seq", -1).astype(jnp.float32),
        passed_along(value_window[:, :SEGMAX].astype(jnp.bfloat16), "seq", -1).astype(jnp.float32),
    )
    key_own = key_window[:, SEGMAX:]
    value_own = value_window[:, SEGMAX:]
    key_total = jnp.concatenate(
        [key_own[:, : tokens - SEGMAX], key_own[:, tokens - SEGMAX :] + returned[0]], axis=1
    )
    value_total = jnp.concatenate(
        [value_own[:, : tokens - SEGMAX], value_own[:, tokens - SEGMAX :] + returned[1]], axis=1
    )
    query_grad = query_full.astype(jnp.bfloat16)
    key_grad = key_total.reshape(rows_here * tokens, width).astype(jnp.bfloat16)
    value_grad = value_total.reshape(rows_here * tokens, width).astype(jnp.bfloat16)
    query_weight_grad = contract_rows(flat, query_grad)
    query_bias_grad = column_sum(query_grad)
    key_weight_grad = contract_rows(flat, key_grad)
    value_weight_grad = contract_rows(flat, value_grad)
    value_bias_grad = column_sum(value_grad)
    grad_hidden = (
        grad_first
        + times_transposed(query_grad, query_matrix)
        + times_transposed(key_grad, key_matrix)
        + times_transposed(value_grad, value_matrix)
    ).reshape(rows_here, tokens, width)
    shards = (
        lax.psum_scatter(query_weight_grad, ("dp", "seq"), scatter_dimension=0, tiled=True),
        lax.psum_scatter(query_bias_grad, ("dp", "seq"), scatter_dimension=0, tiled=True),
        lax.psum_scatter(key_weight_grad, ("dp", "seq"), scatter_dimension=0, tiled=True),
        lax.psum_scatter(value_weight_grad, ("dp", "seq"), scatter_dimension=0, tiled=True),
        lax.psum_scatter(value_bias_grad, ("dp", "seq"), scatter_dimension=0, tiled=True),
        lax.psum_scatter(output_weight_grad, ("dp", "seq"), scatter_dimension=0, tiled=True),
        lax.psum_scatter(output_bias_grad, ("dp", "seq"), scatter_dimension=0, tiled=True),
        lax.psum_scatter(first_gain_grad, ("dp", "seq"), scatter_dimension=0, tiled=True),
        lax.psum_scatter(first_shift_grad, ("dp", "seq"), scatter_dimension=0, tiled=True),
        lax.psum_scatter(inner_weight_grad, ("dp", "seq"), scatter_dimension=0, tiled=True),
        lax.psum_scatter(inner_bias_grad, ("dp", "seq"), scatter_dimension=0, tiled=True),
        lax.psum_scatter(outer_weight_grad, ("dp", "seq"), scatter_dimension=0, tiled=True),
        lax.psum_scatter(outer_bias_grad, ("dp", "seq"), scatter_dimension=0, tiled=True),
        lax.psum_scatter(second_gain_grad, ("dp", "seq"), scatter_dimension=0, tiled=True),
        lax.psum_scatter(second_shift_grad, ("dp", "seq"), scatter_dimension=0, tiled=True),
    )
    return (
        layer_out,
        grad_hidden,
        shards[0],
        shards[1],
        shards[2],
        shards[3],
        shards[4],
        shards[5],
        shards[6],
        shards[7],
        shards[8],
        shards[9],
        shards[10],
        shards[11],
        shards[12],
        shards[13],
        shards[14],
    )


GRID = (2, 2, 4, 2)
FF_PARTS = 8


class Place:
    def __init__(self):
        dp = lax.axis_index("dp")
        seq = lax.axis_index("seq")
        self.x = lax.rem(dp, 2)
        self.y = lax.div(dp, 2)
        self.z = lax.div(seq, 2)
        self.c = lax.rem(seq, 2)
        self.seq = seq

    def device(self, x=None, y=None, z=None, c=None):
        x = self.x if x is None else x
        y = self.y if y is None else y
        z = self.z if z is None else z
        c = self.c if c is None else c
        return (y * 2 + x, z * 2 + c)

    def peer(self, dim):
        if dim == "x":
            return self.device(x=1 - self.x)
        if dim == "y":
            return self.device(y=1 - self.y)
        if dim == "c":
            return self.device(c=1 - self.c)
        return self.device(z=lax.rem(self.z + dim, 4))


def signal(semaphore, device):
    pl.semaphore_signal(semaphore, inc=1, device_id=device, device_id_type=MESH)


def meet(place, along=0):
    barrier = pltpu.get_barrier_semaphore()
    for dim in ("x", "y", "c", 1, 2, 3):
        signal(barrier, place.peer(dim))
    extra = 0
    if along:
        up = (place.c == 1) & (place.z < 3)
        down = (place.c == 0) & (place.z > 0)
        receives, sends = (down, up) if along > 0 else (up, down)
        other = lax.rem(place.z + (3 if along > 0 else 1), 4)

        @pl.when(receives)
        def _():
            signal(barrier, place.device(z=other, c=1 - place.c))

        extra = sends.astype(jnp.int32)
    pl.semaphore_wait(barrier, 6 + extra)


def remote(src, dst, send, recv, device):
    return pltpu.make_async_remote_copy(
        src_ref=src, dst_ref=dst, send_sem=send, recv_sem=recv, device_id=device, device_id_type=MESH
    )


class Gather:
    def __init__(self, place, order, source, target, send, recv):
        held = {"x": False, "y": False, "z": False}

        def region():
            index = []
            for name, size in (("y", 2), ("x", 2), ("z", 4)):
                index.append(pl.ds(0, size) if held[name] else pl.ds(getattr(place, name), 1))
            return target(index[0], index[1], index[2], pl.ds(place.c, 1))

        self.own = pltpu.make_async_copy(source, region(), recv.at[6])
        self.phases = []
        for number, dim in enumerate(order):
            here = region()
            copies = []
            for partner in (1, 2, 3) if dim == "z" else (dim,):
                slot = partner - 1 if dim == "z" else {"x": 3, "y": 4}[dim]
                copies.append(
                    remote(
                        source if number == 0 else here,
                        here,
                        send.at[slot],
                        recv.at[slot],
                        place.peer(partner),
                    )
                )
            self.phases.append(copies)
            held[dim] = True
        here = region()
        self.phases.append([remote(here, here, send.at[5], recv.at[5], place.peer("c"))])

    def start(self, phase):
        if phase == 0:
            self.own.start()
        for copy in self.phases[phase]:
            copy.start()

    def arrive(self, phase):
        for copy in self.phases[phase]:
            copy.wait_recv()
        if phase == 0:
            self.own.wait()

    def step(self, phase):
        if phase > 0:
            self.arrive(phase - 1)
        if phase < 4:
            self.start(phase)

    def finish(self):
        for copies in self.phases:
            for copy in copies:
                copy.wait_send()


class Scatter:
    def __init__(self, place, order, stage, own, store, bufs, send, recv):
        r0, r1, r2, r3 = bufs
        self.place, self.order, self.own, self.store = place, order, own, store
        self.bufs = bufs
        self.copies = [[remote(stage(1 - place.c), r0, send.at[0], recv.at[0], place.peer("c"))]]
        y, x, z = place.y, place.x, place.z
        if order == "yx":
            first, second = (r0.at[1 - y], "y"), (r1.at[1 - x], "x")
        else:
            first, second = (r0.at[:, 1 - x], "x"), (r1.at[1 - y], "y")
        self.copies.append([remote(first[0], r1, send.at[1], recv.at[1], place.peer(first[1]))])
        self.copies.append([remote(second[0], r2, send.at[2], recv.at[2], place.peer(second[1]))])
        self.copies.append(
            [
                remote(r2.at[lax.rem(z + k, 4)], r3.at[k - 1], send.at[2 + k], recv.at[2 + k], place.peer(k))
                for k in (1, 2, 3)
            ]
        )

    def step(self, phase):
        place = self.place
        r0, r1, r2, r3 = self.bufs
        if phase > 0:
            for copy in self.copies[phase - 1]:
                copy.wait_recv()
        if phase == 1:
            r0[...] = (r0[...].astype(F32) + self.own().astype(F32)).astype(BF16)
        elif phase == 2:
            mine = r0[place.y] if self.order == "yx" else r0[:, place.x]
            r1[...] = (r1[...].astype(F32) + mine.astype(F32)).astype(BF16)
        elif phase == 3:
            mine = r1[place.x] if self.order == "yx" else r1[place.y]
            r2[...] = (r2[...].astype(F32) + mine.astype(F32)).astype(BF16)
        elif phase == 4:
            total = r2[place.z].astype(F32)
            for k in range(3):
                total = total + r3[k].astype(F32)
            self.store(total)
        if phase < 4:
            for copy in self.copies[phase]:
                copy.start()

    def finish(self):
        for copies in self.copies:
            for copy in copies:
                copy.wait_send()


def advance(slots, tick, phases=5):
    for phase in range(phases):
        number = tick - phase
        if 0 <= number < len(slots):
            for part in slots[number]:
                part.step(phase)


def dot(left, right):
    return jnp.dot(left, right, preferred_element_type=F32)


def dot_nt(left, right):
    return lax.dot_general(left, right, (((1,), (1,)), ((), ())), preferred_element_type=F32)


def dot_tn(left, right):
    return lax.dot_general(left, right, (((0,), (0,)), ((), ())), preferred_element_type=F32)


def spread(blocks, row, base, width, count):
    flat = blocks.reshape(32 * 16, 128)
    lane = lax.broadcasted_iota(jnp.int32, (128, count), 0)
    column = lax.broadcasted_iota(jnp.int32, (128, count), 1)
    pick = jnp.where(lane == base + lax.rem(column, width), 1.0, 0.0).astype(BF16)
    wide = dot(flat, pick)
    at = lax.broadcasted_iota(jnp.int32, (32 * 16, count), 0)
    column = lax.broadcasted_iota(jnp.int32, (32 * 16, count), 1)
    keep = at == lax.div(column, width) * 16 + row
    return jnp.sum(jnp.where(keep, wide, 0.0), axis=0, keepdims=True)


def project_kernel(
    x_in, small_in, wq_in, wk_in, wv_in, wo_in,
    q_out, k_out, v_out, xt_out, w_out, vec_out, ib_out,
    weights, smalls, xt, q_buf, k_buf, v_buf, send, recv, tail_sem, local_sem,
):
    place = Place()
    tokens = x_in.shape[1]
    own_x = pltpu.make_async_copy(x_in, xt.at[:, pl.ds(SEGMAX, tokens)], local_sem.at[0])
    own_x.start()
    meet(place, 1)
    width = x_in.shape[2]
    half = width // 2
    slots = [[Gather(place, "zxy", small_in, lambda y, x, z, c: smalls.at[y, x, z, c], send.at[16], recv.at[16])]]
    number = 0
    for matrix, source in enumerate((wq_in, wk_in, wv_in, wo_in)):
        for part in range(2):
            pair = []
            for piece, order in enumerate(("zxy", "zyx")):
                columns = pl.ds(part * half + piece * half // 2, half // 2)
                pair.append(
                    Gather(
                        place,
                        order,
                        source.at[:, :, :, :, :, columns],
                        lambda y, x, z, c, m=matrix, cols=columns: weights.at[m, y, x, z, c, :, cols],
                        send.at[number],
                        recv.at[number],
                    )
                )
                number += 1
            slots.append(pair)

    tail = remote(
        x_in.at[:, pl.ds(tokens - SEGMAX, SEGMAX)],
        xt.at[:, pl.ds(0, SEGMAX)],
        tail_sem.at[0],
        tail_sem.at[1],
        place.device(z=lax.rem(place.z + place.c, 4), c=1 - place.c),
    )
    has_next, has_last = place.seq < 7, place.seq > 0

    saves = []

    def save(source, target):
        copy = pltpu.make_async_copy(source, target, local_sem.at[1 + len(saves)])
        copy.start()
        saves.append(copy)

    def project(matrix, target, bias, rows_from):
        def body(step, carry):
            row, part = lax.div(step, 2), lax.rem(step, 2)
            columns = pl.ds(pl.multiple_of(part * half, half), half)
            block = weights[matrix, :, :, :, :, :, columns].reshape(width, half)
            out = dot(xt[row, rows_from:, :], block)
            if bias is not None:
                out = out + vec_out[bias : bias + 1, columns]
            target[row, :, columns] = out.astype(BF16)
            return carry

        lax.fori_loop(0, 4, body, 0)

    for tick in range(len(slots) + 4):
        if tick == 2:
            pl.when(has_next)(tail.start)
        if tick == 3:
            xt_zero = jnp.zeros((2, SEGMAX, width), BF16)

            @pl.when(place.seq == 0)
            def _():
                xt[:, :SEGMAX, :] = xt_zero

            own_x.wait()
        advance(slots, tick)
        if tick == 4:
            for vector in range(8):
                vec_out[vector : vector + 1, :] = spread(smalls[...], vector // 4, vector % 4 * 32, 32, width)
            vec_out[8:, :] = jnp.zeros((8, width), F32)
            for part in range(FF_PARTS):
                ib_out[part : part + 1, :] = spread(smalls[...], 2, part * 16, 16, 512)
        if tick == 6:
            save(weights.at[0], w_out.at[0])
            project(0, q_buf, 0, SEGMAX)
            save(q_buf, q_out)
        if tick == 8:
            save(weights.at[1], w_out.at[1])
            pl.when(has_last)(tail.wait_recv)
            save(xt, xt_out)
            project(1, k_buf, None, 0)
            save(k_buf, k_out)
        if tick == 10:
            save(weights.at[2], w_out.at[2])
            project(2, v_buf, 1, 0)
            save(v_buf, v_out)
        if tick == 12:
            save(weights.at[3], w_out.at[3])
    for slot in slots:
        for part in slot:
            part.finish()
    pl.when(has_next)(tail.wait_send)
    for copy in saves:
        copy.wait()


def project(hidden, small, wq, wk, wv, wo):
    rows, tokens, width = hidden.shape
    window = tokens + SEGMAX
    hbm = pl.BlockSpec(memory_space=pl.ANY)
    vmem = pl.BlockSpec(memory_space=pltpu.VMEM)
    lead = lambda a: a.reshape((1, 1, 1, 1) + a.shape)
    block = wq.shape
    return pl.pallas_call(
        project_kernel,
        out_shape=[
            jax.ShapeDtypeStruct((rows, tokens, width), BF16),
            jax.ShapeDtypeStruct((rows, window, width), BF16),
            jax.ShapeDtypeStruct((rows, window, width), BF16),
            jax.ShapeDtypeStruct((rows, window, width), BF16),
            jax.ShapeDtypeStruct((4,) + GRID + block, BF16),
            jax.ShapeDtypeStruct((16, width), F32),
            jax.ShapeDtypeStruct((FF_PARTS, 512), F32),
        ],
        in_specs=[hbm] * 6,
        out_specs=[hbm] * 5 + [vmem] * 2,
        scratch_shapes=[
            pltpu.VMEM((4,) + GRID + block, BF16),
            pltpu.VMEM(GRID + (16, 128), BF16),
            pltpu.VMEM((rows, window, width), BF16),
            pltpu.VMEM((rows, tokens, width), BF16),
            pltpu.VMEM((rows, window, width), BF16),
            pltpu.VMEM((rows, window, width), BF16),
            pltpu.SemaphoreType.DMA((17, 8)),
            pltpu.SemaphoreType.DMA((17, 8)),
            pltpu.SemaphoreType.DMA((2,)),
            pltpu.SemaphoreType.DMA((10,)),
        ],
        compiler_params=pltpu.CompilerParams(
            collective_id=0, has_side_effects=True, vmem_limit_bytes=48 * MIB
        ),
        name="gather_project",
    )(hidden, lead(small), lead(wq), lead(wk), lead(wv), lead(wo))


def mask_scores(key_ids, query_ids):
    keys, queries = key_ids.shape[0], query_ids.shape[1]
    key_at = lax.broadcasted_iota(jnp.int32, (keys, queries), 0)
    query_at = lax.broadcasted_iota(jnp.int32, (keys, queries), 1)
    visible = ((key_ids == query_ids) & (query_ids > 0)) | (key_at == query_at + SEGMAX)
    return jnp.where(visible, 0.0, HIDDEN).astype(F32)


def one_head(block, head):
    lane = lax.broadcasted_iota(jnp.int32, block.shape, 1)
    return jnp.where(lax.div(lane, HD) == head, block, jnp.zeros_like(block))


def layer_norm(value):
    center = value - jnp.mean(value, axis=-1, keepdims=True)
    scale = lax.rsqrt(jnp.mean(center * center, axis=-1, keepdims=True) + EPS)
    return center * scale, scale


def layer_norm_back(grad, unit, scale):
    return scale * (
        grad
        - jnp.mean(grad, axis=-1, keepdims=True)
        - unit * jnp.mean(grad * unit, axis=-1, keepdims=True)
    )


def attend_kernel(q, k, v, key_ids, query_ids, x, wo, vec, mixed, lse, low, unit, scale, bias):
    pair = pl.program_id(1)
    tokens = q.shape[1]

    @pl.when(pair == 0)
    def _():
        bias[...] = mask_scores(key_ids[0], query_ids[0])

    columns = pl.ds(pl.multiple_of(pair * PAIR, PAIR), PAIR)
    v_t = v[0].T
    for start in range(0, tokens, 256):
        low_key = 0 if start == 0 else start
        queries = q[0, start : start + 256, :]
        keys = k[0, low_key:, :]
        parts = []
        for head in range(2):
            s = dot_nt(keys, one_head(queries, head)) * SCORE_SCALE + bias[low_key:, start : start + 256]
            highest = jnp.max(s, axis=0, keepdims=True)
            expo = jnp.exp2(s - highest)
            total = jnp.sum(expo, axis=0, keepdims=True)
            out = dot(v_t[head * HD : head * HD + HD, low_key:], expo.astype(BF16))
            parts.append(out * (1.0 / total))
            lse[0, 0, head : head + 1, start : start + 256] = highest + jnp.log2(total)
        mixed[0, start : start + 256, columns] = jnp.concatenate(parts, axis=0).T.astype(BF16)

    @pl.when(pair == pl.num_programs(1) - 1)
    def _():
        for start in range(0, tokens, 256):
            rows = pl.ds(start, 256)
            total = dot(mixed[0, rows, :], wo[...]) + x[0, rows, :].astype(F32) + vec[2:3, :]
            centered, spread_ = layer_norm(total)
            unit[0, rows, :] = centered
            scale[0, rows, :] = spread_
            low[0, rows, :] = (centered * vec[3:4, :] + vec[4:5, :]).astype(BF16)


def attend(q, k, v, key_ids, query_ids, x, wo, vec):
    rows, tokens, width = q.shape
    window = k.shape[1]
    pairs = width // PAIR
    whole = lambda shape: pl.BlockSpec(shape, lambda r, p: (0,) * len(shape))
    per_pair = lambda n: pl.BlockSpec((1, n, PAIR), lambda r, p: (r, 0, p))
    per_row = lambda *s: pl.BlockSpec((1,) + s, lambda r, p: (r, 0, 0))
    return pl.pallas_call(
        attend_kernel,
        grid=(rows, pairs),
        out_shape=[
            jax.ShapeDtypeStruct((rows, tokens, width), BF16),
            jax.ShapeDtypeStruct((rows, pairs, 8, tokens), F32),
            jax.ShapeDtypeStruct((rows, tokens, width), BF16),
            jax.ShapeDtypeStruct((rows, tokens, width), F32),
            jax.ShapeDtypeStruct((rows, tokens, 1), F32),
        ],
        in_specs=[
            per_pair(tokens), per_pair(window), per_pair(window),
            per_row(window, 1), per_row(1, tokens), per_row(tokens, width),
            whole(wo.shape), whole(vec.shape),
        ],
        out_specs=[
            per_row(tokens, width),
            pl.BlockSpec((1, 1, 8, tokens), lambda r, p: (r, p, 0, 0)),
            per_row(tokens, width),
            per_row(tokens, width),
            per_row(tokens, 1),
        ],
        scratch_shapes=[pltpu.VMEM((window, tokens), F32)],
        compiler_params=pltpu.CompilerParams(vmem_limit_bytes=48 * MIB),
        name="attend",
    )(q, k, v, key_ids, query_ids, x, wo, vec)


def gelu_both(value):
    bell = jnp.exp2(value * value * (-0.5 * LOG2E)) * 0.3989422804014327
    below = 0.5 + 0.5 * lax.erf(value * 0.7071067811865476)
    return value * below, below + value * bell


def forward_kernel(low, unit, cot, inner_w, inner_b, outer_w, vec, active, slope, layer_out, og, grad_second, sums, total):
    part = pl.program_id(0)
    tokens, width = low.shape
    w1 = inner_w[...].reshape(width, 512)
    w2 = outer_w[...].reshape(512, width)
    for start in range(0, tokens, 256):
        rows = pl.ds(start, 256)
        inner = dot(low[rows, :], w1) + inner_b[0]
        act, der = gelu_both(inner)
        act = act.astype(BF16)
        active[rows, :] = act
        slope[rows, :] = der.astype(BF16)
        out = dot(act, w2)

        @pl.when(part == 0)
        def _():
            total[rows, :] = out

        @pl.when(part > 0)
        def _():
            total[rows, :] += out

    @pl.when(part == pl.num_programs(0) - 1)
    def _():
        sums[...] = jnp.zeros_like(sums)
        for start in range(0, tokens, 256):
            rows = pl.ds(start, 256)
            normed = unit[rows, :] * vec[3:4, :] + vec[4:5, :]
            centered, scale = layer_norm(total[rows, :] + normed + vec[5:6, :])
            layer_out[rows, :] = (centered * vec[6:7, :] + vec[7:8, :]).astype(BF16)
            up = cot[rows, :].astype(F32)
            grad = layer_norm_back(up * vec[6:7, :], centered, scale)
            grad_second[rows, :] = grad
            rounded = grad.astype(BF16)
            og[rows, :] = rounded
            sums[0:1, :] += jnp.sum(rounded.astype(F32), axis=0, keepdims=True)
            sums[1:2, :] += jnp.sum(up * centered, axis=0, keepdims=True)
            sums[2:3, :] += jnp.sum(up, axis=0, keepdims=True)


def feed_forward(low, unit, cot, gathered, inner_b, vec):
    tokens, width = low.shape
    ff = FF_PARTS * 512
    whole = lambda shape: pl.BlockSpec(shape, lambda q: (0,) * len(shape))
    column = pl.BlockSpec((tokens, 512), lambda q: (0, q))
    return pl.pallas_call(
        forward_kernel,
        grid=(FF_PARTS,),
        out_shape=[
            jax.ShapeDtypeStruct((tokens, ff), BF16),
            jax.ShapeDtypeStruct((tokens, ff), BF16),
            jax.ShapeDtypeStruct((tokens, width), BF16),
            jax.ShapeDtypeStruct((tokens, width), BF16),
            jax.ShapeDtypeStruct((tokens, width), F32),
            jax.ShapeDtypeStruct((8, width), F32),
        ],
        in_specs=[
            whole(low.shape), whole(unit.shape), whole(cot.shape),
            pl.BlockSpec((32, 32, 512), lambda q: (0, q // 2, q % 2)),
            pl.BlockSpec((1, 1, 512), lambda q: (q, 0, 0)),
            pl.BlockSpec((32, 16, width), lambda q: (0, 8 + q, 0)),
            whole(vec.shape),
        ],
        out_specs=[column, column, whole((tokens, width)), whole((tokens, width)), whole((tokens, width)), whole((8, width))],
        scratch_shapes=[pltpu.VMEM((tokens, width), F32)],
        compiler_params=pltpu.CompilerParams(vmem_limit_bytes=56 * MIB),
        name="feed_forward",
    )(low, unit, cot, gathered, inner_b.reshape(FF_PARTS, 1, 512), gathered, vec)


def backward_kernel(
    active, slope, og, low, inner_w, outer_w, grad_second, unit, scale, mixed, wo, vec,
    outer_grad, inner_grad, ib_grad, grad_first, grad_mixed, wo_grad, sums, total, ig,
):
    part = pl.program_id(0)
    tokens, width = og.shape
    w1 = inner_w[...].reshape(width, 512)
    w2 = outer_w[...].reshape(512, width)
    outer_grad[...] = dot_tn(active[...], og[...]).astype(BF16).reshape(outer_grad.shape)
    ib_grad[...] = jnp.zeros_like(ib_grad)
    for start in range(0, tokens, 256):
        rows = pl.ds(start, 256)
        piece = (dot_nt(og[rows, :], w2) * slope[rows, :].astype(F32)).astype(BF16)
        ig[rows, :] = piece
        ib_grad[0] += jnp.sum(piece.astype(F32), axis=0, keepdims=True)
    inner_grad[...] = dot_tn(low[...], ig[...]).astype(BF16).reshape(inner_grad.shape)
    for start in range(0, tokens, 256):
        rows = pl.ds(start, 256)
        back = dot_nt(ig[rows, :], w1)

        @pl.when(part == 0)
        def _():
            total[rows, :] = grad_second[rows, :] + back

        @pl.when(part > 0)
        def _():
            total[rows, :] += back

    @pl.when(part == pl.num_programs(0) - 1)
    def _():
        sums[...] = jnp.zeros_like(sums)
        for start in range(0, tokens, 256):
            rows = pl.ds(start, 256)
            up = total[rows, :]
            centered = unit[rows, :]
            grad = layer_norm_back(up * vec[3:4, :], centered, scale[rows, :])
            grad_first[rows, :] = grad
            rounded = grad.astype(BF16)
            og[rows, :] = rounded
            sums[0:1, :] += jnp.sum(rounded.astype(F32), axis=0, keepdims=True)
            sums[1:2, :] += jnp.sum(up * centered, axis=0, keepdims=True)
            sums[2:3, :] += jnp.sum(up, axis=0, keepdims=True)
            grad_mixed[rows, :] = dot_nt(rounded, wo[...]).astype(BF16)
        wo_grad[...] = dot_tn(mixed[...], og[...]).astype(BF16).reshape(wo_grad.shape)


def feed_backward(active, slope, og, low, gathered, grad_second, unit, scale, mixed, wo, vec):
    tokens, width = og.shape
    whole = lambda shape: pl.BlockSpec(shape, lambda q: (0,) * len(shape))
    column = pl.BlockSpec((tokens, 512), lambda q: (0, q))
    per_part = lambda shape: pl.BlockSpec((1,) + shape, lambda q: (q,) + (0,) * len(shape))
    outer_shape, inner_shape, wo_shape = GRID + (16, width), GRID + (32, 512), GRID + (32, width)
    return pl.pallas_call(
        backward_kernel,
        grid=(FF_PARTS,),
        out_shape=[
            jax.ShapeDtypeStruct((FF_PARTS,) + outer_shape, BF16),
            jax.ShapeDtypeStruct((FF_PARTS,) + inner_shape, BF16),
            jax.ShapeDtypeStruct((FF_PARTS, 1, 512), F32),
            jax.ShapeDtypeStruct((tokens, width), F32),
            jax.ShapeDtypeStruct((tokens, width), BF16),
            jax.ShapeDtypeStruct(wo_shape, BF16),
            jax.ShapeDtypeStruct((8, width), F32),
        ],
        in_specs=[
            column, column, whole(og.shape), whole(low.shape),
            pl.BlockSpec((32, 32, 512), lambda q: (0, q // 2, q % 2)),
            pl.BlockSpec((32, 16, width), lambda q: (0, 8 + q, 0)),
            whole(grad_second.shape), whole(unit.shape), whole(scale.shape), whole(mixed.shape),
            whole(wo.shape), whole(vec.shape),
        ],
        out_specs=[
            per_part(outer_shape), per_part(inner_shape), per_part((1, 512)),
            whole((tokens, width)), whole((tokens, width)), whole(wo_shape), whole((8, width)),
        ],
        scratch_shapes=[pltpu.VMEM((tokens, width), F32), pltpu.VMEM((tokens, 512), BF16)],
        compiler_params=pltpu.CompilerParams(vmem_limit_bytes=60 * MIB),
        name="feed_backward",
    )(active, slope, og, low, gathered, gathered, grad_second, unit, scale, mixed, wo, vec)


def attend_back_kernel(
    q, k, v, gm, mixed, lse, key_ids, query_ids, xt,
    dq_out, dk_out, dv_out, weight_grad, sums, bias, dq_all, dk_all, dv_all, dk_sum, dv_sum,
):
    group, row, inner = pl.program_id(0), pl.program_id(1), pl.program_id(2)
    tokens = q.shape[1]

    @pl.when((group == 0) & (inner == 0))
    def _():
        bias[row] = mask_scores(key_ids[0], query_ids[0])

    k_t = k[0].T
    for start in range(0, tokens, 256):
        low_key = 0 if start == 0 else start
        queries = q[0, start : start + 256, :]
        grads = gm[0, start : start + 256, :]
        product = (grads.astype(F32) * mixed[0, start : start + 256, :].astype(F32)).T
        keys, values = k[0, low_key:, :], v[0, low_key:, :]
        parts = []
        dk, dv = 0.0, 0.0
        for head in range(2):
            one_q, one_g = one_head(queries, head), one_head(grads, head)
            delta = jnp.sum(product[head * HD : head * HD + HD, :], axis=0, keepdims=True)
            s = dot_nt(keys, one_q) * SCORE_SCALE + bias[row, low_key:, start : start + 256]
            probs = jnp.exp2(s - lse[0, 0, head : head + 1, start : start + 256])
            dprob = dot_nt(values, one_g)
            score_grad = (probs * (dprob - delta)).astype(BF16)
            dv = dv + dot(probs.astype(BF16), one_g)
            dk = dk + dot(score_grad, one_q)
            parts.append(dot(k_t[head * HD : head * HD + HD, low_key:], score_grad))
        dq = (jnp.concatenate(parts, axis=0) * 0.125).T.astype(BF16)
        dq_out[0, start : start + 256, :] = dq
        if start == 0:
            dk_sum[...] = dk
            dv_sum[...] = dv
        else:
            dk_sum[low_key:, :] += dk
            dv_sum[low_key:, :] += dv
    dk_out[0] = (dk_sum[...] * 0.125).astype(BF16)
    dv_out[0] = dv_sum[...].astype(BF16)
    columns = pl.ds(pl.multiple_of(inner * PAIR, PAIR), PAIR)
    dq_all[row, :, columns] = dq_out[0]
    dk_all[row, :, columns] = dk_out[0]
    dv_all[row, :, columns] = dv_out[0]

    @pl.when((row == 1) & (inner == 1))
    def _():
        for number, source in enumerate((dq_all, dk_all, dv_all)):
            first = SEGMAX if number == 0 else 0
            grad = dot_tn(xt[0, first:, :], source[0]) + dot_tn(xt[1, first:, :], source[1])
            span = grad.shape[1]
            weight_grad[0, :, :, :, :, :, number * span : number * span + span] = grad.astype(BF16).reshape(
                GRID + (32, span)
            )
        sums[...] = jnp.zeros_like(sums)
        for number, source in enumerate((dq_all, dv_all)):
            added = jnp.sum(source[0].astype(F32), axis=0, keepdims=True) + jnp.sum(
                source[1].astype(F32), axis=0, keepdims=True
            )
            sums[number : number + 1, :] = added


def attend_back(q, k, v, gm, mixed, lse, key_ids, query_ids, xt):
    rows, tokens, width = q.shape
    window = k.shape[1]
    groups = width // (2 * PAIR)
    whole = lambda shape: pl.BlockSpec(shape, lambda g, r, i: (0,) * len(shape))
    per_pair = lambda n: pl.BlockSpec((1, n, PAIR), lambda g, r, i: (r, 0, g * 2 + i))
    per_row = lambda *s: pl.BlockSpec((1,) + s, lambda g, r, i: (r, 0, 0))
    out_block = GRID + (32, 6 * PAIR)
    return pl.pallas_call(
        attend_back_kernel,
        grid=(groups, rows, 2),
        out_shape=[
            jax.ShapeDtypeStruct((rows, tokens, width), BF16),
            jax.ShapeDtypeStruct((rows, window, width), BF16),
            jax.ShapeDtypeStruct((rows, window, width), BF16),
            jax.ShapeDtypeStruct((groups,) + out_block, BF16),
            jax.ShapeDtypeStruct((8, width), F32),
        ],
        in_specs=[
            per_pair(tokens), per_pair(window), per_pair(window), per_pair(tokens), per_pair(tokens),
            pl.BlockSpec((1, 1, 8, tokens), lambda g, r, i: (r, g * 2 + i, 0, 0)),
            per_row(window, 1), per_row(1, tokens), whole(xt.shape),
        ],
        out_specs=[
            per_pair(tokens), per_pair(window), per_pair(window),
            pl.BlockSpec((1,) + out_block, lambda g, r, i: (g,) + (0,) * len(out_block)),
            pl.BlockSpec((8, 2 * PAIR), lambda g, r, i: (0, g)),
        ],
        scratch_shapes=[
            pltpu.VMEM((rows, window, tokens), F32),
            pltpu.VMEM((rows, tokens, 2 * PAIR), BF16),
            pltpu.VMEM((rows, window, 2 * PAIR), BF16),
            pltpu.VMEM((rows, window, 2 * PAIR), BF16),
            pltpu.VMEM((window, PAIR), F32),
            pltpu.VMEM((window, PAIR), F32),
        ],
        compiler_params=pltpu.CompilerParams(vmem_limit_bytes=48 * MIB),
        name="attend_back",
    )(q, k, v, gm, mixed, lse, key_ids, query_ids, xt)


def scatter_buffers(count, rows, columns):
    block = (rows, columns)
    return [
        pltpu.VMEM((count, 2, 2, 4) + block, BF16),
        pltpu.VMEM((count, 2, 4) + block, BF16),
        pltpu.VMEM((count, 4) + block, BF16),
        pltpu.VMEM((count, 3) + block, BF16),
        pltpu.SemaphoreType.DMA((count, 6)),
        pltpu.SemaphoreType.DMA((count, 6)),
    ]


def finish_kernel(
    outer_in, inner_in, wo_in, qkv_in, small_in, dq, dk, dv, weights, grad_first,
    outer_out, inner_out, wo_out, qkv_out, small_out, gh_out,
    own_sem, tail_sem, tail_here, tail_there, gh, *bufs,
):
    place = Place()
    meet(place, -1)
    kinds = {}
    for number, name in enumerate(("outer", "inner", "qkv", "small")):
        kinds[name] = bufs[number * 7 : number * 7 + 7]
    used = {name: 0 for name in kinds}

    def make(name, order, source, store):
        r0, r1, r2, r3, send, recv, own = kinds[name]
        number = used[name]
        used[name] += 1
        fetch = pltpu.make_async_copy(source(place.c), own.at[number % 4], own_sem.at[make.fetches])
        make.fetches += 1
        scatter = Scatter(
            place, order, source, lambda: own[number % 4], store,
            tuple(b.at[number] for b in (r0, r1, r2, r3)), send.at[number], recv.at[number],
        )
        step = scatter.step

        def fetched(phase):
            if phase == 0:
                fetch.start()
            if phase == 1:
                fetch.wait()
            step(phase)

        scatter.step = fetched
        return scatter

    make.fetches = 0

    def halves(name, ref, out, columns):
        pair = []
        for half, order in enumerate(("yx", "xy")):
            cols = pl.ds(half * columns // 2, columns // 2)

            def store(total, cols=cols):
                out[:, cols] = total

            pair.append(make(name, order, lambda c, cols=cols: ref.at[:, :, :, c, :, cols], store))
        return pair

    width = wo_in.shape[-1]
    slots = []
    for part in range(FF_PARTS):
        slots.append(halves("outer", outer_in.at[part], outer_out.at[pl.ds(part * 16, 16)], width))
    for part in range(FF_PARTS):
        slots.append(halves("inner", inner_in.at[part], inner_out.at[part], 512))
    for part in range(2):
        cols = pl.ds(part * 512, 512)
        slots.append(halves("inner", wo_in.at[:, :, :, :, :, cols], wo_out.at[:, cols], 512))
    for part in range(qkv_in.shape[0]):
        slots.append(halves("qkv", qkv_in.at[part], qkv_out.at[part], qkv_in.shape[-1]))

    def store_small(total):
        small_out[...] = total

    slots.append([make("small", "yx", lambda c: small_in.at[:, :, :, c], store_small)])

    half = width // 2
    tokens = dq.shape[1]
    matrix = lambda m, cols: weights[m, :, :, :, :, cols, :].reshape(-1, width)
    full = [weights.at[m] for m in range(3)]

    def tail_rows(row):
        return dot_nt(dk[row, :SEGMAX, :], full[1][...].reshape(width, width)) + dot_nt(
            dv[row, :SEGMAX, :], full[2][...].reshape(width, width)
        )

    send_tail, recv_tail = place.seq > 0, place.seq < 7
    tail = remote(
        tail_here, tail_there, tail_sem.at[0], tail_sem.at[1],
        place.device(z=lax.rem(place.z + 3 + place.c, 4), c=1 - place.c),
    )

    def own_rows(row, start):
        rows = pl.ds(start, 256)
        total = grad_first[row, rows, :] + dot_nt(dq[row, rows, :], full[0][...].reshape(width, width))
        rows_k = pl.ds(start + SEGMAX, 256)
        total = total + dot_nt(dk[row, rows_k, :], full[1][...].reshape(width, width))
        total = total + dot_nt(dv[row, rows_k, :], full[2][...].reshape(width, width))
        gh[row, rows, :] = total

    work = {0: lambda: tail_rows_both(), 1: lambda: own_rows(0, 0), 2: lambda: own_rows(0, 256), 3: lambda: own_rows(1, 0), 4: lambda: own_rows(1, 256)}

    def tail_rows_both():
        for row in range(2):
            tail_here[row] = tail_rows(row).astype(BF16)
        pl.when(send_tail)(tail.start)

    for tick in range(len(slots) + 4):
        advance(slots, tick)
        if tick in work:
            work[tick]()

    @pl.when(place.seq == 7)
    def _():
        tail_there[...] = jnp.zeros_like(tail_there)

    pl.when(recv_tail)(tail.wait_recv)
    for row in range(2):
        gh[row, tokens - SEGMAX :, :] += tail_there[row].astype(F32)
    save = pltpu.make_async_copy(gh, gh_out, own_sem.at[make.fetches])
    save.start()
    for slot in slots:
        for part in slot:
            part.finish()
    pl.when(send_tail)(tail.wait_send)
    save.wait()


def finish(outer_in, inner_in, wo_in, qkv_in, small_in, dq, dk, dv, weights, grad_first):
    rows, tokens, width = dq.shape
    hbm = pl.BlockSpec(memory_space=pl.ANY)
    vmem = pl.BlockSpec(memory_space=pltpu.VMEM)
    groups = qkv_in.shape[0]
    span = qkv_in.shape[-1]
    bufs = []
    for count, block_rows, columns in (
        (2 * FF_PARTS, 16, width // 2),
        (2 * (FF_PARTS + 2), 32, 256),
        (2 * groups, 32, span // 2),
        (1, 16, 128),
    ):
        bufs += scatter_buffers(count, block_rows, columns)
        bufs.append(pltpu.VMEM((min(count, 4), 2, 2, 4, block_rows, columns), BF16))
    return pl.pallas_call(
        finish_kernel,
        out_shape=[
            jax.ShapeDtypeStruct((FF_PARTS * 16, width), F32),
            jax.ShapeDtypeStruct((FF_PARTS, 32, 512), F32),
            jax.ShapeDtypeStruct((32, width), F32),
            jax.ShapeDtypeStruct((groups, 32, span), F32),
            jax.ShapeDtypeStruct((16, 128), F32),
            jax.ShapeDtypeStruct((rows, tokens, width), F32),
        ],
        in_specs=[hbm] * 5 + [vmem] * 5,
        out_specs=[vmem] * 5 + [hbm],
        scratch_shapes=[
            pltpu.SemaphoreType.DMA((64,)),
            pltpu.SemaphoreType.DMA((2,)),
            pltpu.VMEM((rows, SEGMAX, width), BF16),
            pltpu.VMEM((rows, SEGMAX, width), BF16),
            pltpu.VMEM((rows, tokens, width), F32),
        ]
        + bufs,
        compiler_params=pltpu.CompilerParams(
            collective_id=1, has_side_effects=True, vmem_limit_bytes=62 * MIB
        ),
        name="sum_gradients",
    )(outer_in, inner_in, wo_in, qkv_in, small_in, dq, dk, dv, weights, grad_first)


def local(
    hidden_in, segment_ids, query_weight, query_bias, key_weight, value_weight, value_bias, output_weight,
    output_bias, first_gain, first_shift, inner_weight, inner_bias, outer_weight, outer_bias, second_gain,
    second_shift, cotangent,
):
    rows, tokens, width = hidden_in.shape
    window = tokens + SEGMAX
    ff = inner_weight.shape[1]
    inner_mine = inner_weight.reshape(32, 32, FF_PARTS, 16).transpose(0, 2, 1, 3).reshape(32, ff)
    inner_mine = inner_mine.reshape(32, 4, 1024).transpose(1, 0, 2).reshape(128, 1024)
    ff_mine = jnp.concatenate([inner_mine, outer_weight], axis=0)
    gathered = lax.all_gather(ff_mine, ("dp", "seq"), axis=0, tiled=True).reshape(32, 256, 1024)
    vectors = (query_bias, value_bias, output_bias, first_gain, first_shift, outer_bias, second_gain, second_shift)
    small = jnp.concatenate(list(vectors) + [inner_bias, jnp.zeros((13 * 128,), BF16)]).reshape(16, 128)

    q, k, v, xt, weights, vec, inner_b = project(
        hidden_in, small, query_weight, key_weight, value_weight, output_weight
    )
    padded = jnp.concatenate([jnp.full((rows, SEGMAX), -1, jnp.int32), segment_ids], axis=1)
    key_ids = lax.dynamic_slice_in_dim(padded, lax.axis_index("seq") * tokens, window, 1)
    query_ids = key_ids[:, None, SEGMAX:]
    key_ids = key_ids[:, :, None]
    wo = weights[3].reshape(width, width)
    mixed, lse, low, unit, scale = attend(q, k, v, key_ids, query_ids, hidden_in, wo, vec)
    flat = lambda a: a.reshape(rows * tokens, a.shape[-1])
    active, slope, layer_out, og, grad_second, sums2 = feed_forward(
        flat(low), flat(unit), flat(cotangent), gathered, inner_b, vec
    )
    outer_grad, inner_grad, ib_grad, grad_first, gm, wo_grad, sums1 = feed_backward(
        active, slope, og, flat(low), gathered, grad_second, flat(unit), flat(scale), flat(mixed), wo, vec
    )
    dq, dk, dv, qkv_grad, sums0 = attend_back(
        q, k, v, gm.reshape(rows, tokens, width), mixed, lse, key_ids, query_ids, xt
    )
    listed = jnp.stack(
        [sums0[0], sums0[1], sums1[0], sums1[1], sums1[2], sums2[0], sums2[1], sums2[2]]
    )
    small_grad = listed.reshape(8, 32, 32).transpose(1, 0, 2).reshape(32, 2, 128)
    ib_mine = ib_grad.reshape(FF_PARTS, 32, 16).transpose(1, 0, 2).reshape(32, 1, 128)
    small_grad = jnp.concatenate([small_grad, ib_mine, jnp.zeros((32, 13, 128), F32)], axis=1)
    small_grad = small_grad.astype(BF16).reshape(GRID + (16, 128))
    outer_sum, inner_sum, wo_sum, qkv_sum, small_sum, grad_hidden = finish(
        outer_grad, inner_grad, wo_grad, qkv_grad, small_grad, dq, dk, dv, weights[:3],
        grad_first.reshape(rows, tokens, width),
    )
    inner_sum = inner_sum.reshape(FF_PARTS, 32, 32, 16).transpose(1, 2, 0, 3).reshape(32, ff)
    qkv_sum = qkv_sum.reshape(4, 32, 3, 256).transpose(2, 1, 0, 3).reshape(3, 32, width)
    vector = small_sum[:2].reshape(8, 32)
    return (
        layer_out.reshape(rows, tokens, width),
        grad_hidden,
        qkv_sum[0],
        vector[0],
        qkv_sum[1],
        qkv_sum[2],
        vector[1],
        wo_sum,
        vector[2],
        vector[3],
        vector[4],
        inner_sum,
        small_sum[2],
        outer_sum,
        vector[5],
        vector[6],
        vector[7],
    )


def solution(mesh):
    in_specs = (
        P("dp", "seq", None),
        P("dp", None),
        P(("dp", "seq"), None),
        P(("dp", "seq")),
        P(("dp", "seq"), None),
        P(("dp", "seq"), None),
        P(("dp", "seq")),
        P(("dp", "seq"), None),
        P(("dp", "seq")),
        P(("dp", "seq")),
        P(("dp", "seq")),
        P(("dp", "seq"), None),
        P(("dp", "seq")),
        P(("dp", "seq"), None),
        P(("dp", "seq")),
        P(("dp", "seq")),
        P(("dp", "seq")),
        P("dp", "seq", None),
    )
    out_specs = (
        P("dp", "seq", None),
        P("dp", "seq", None),
        P(("dp", "seq"), None),
        P(("dp", "seq")),
        P(("dp", "seq"), None),
        P(("dp", "seq"), None),
        P(("dp", "seq")),
        P(("dp", "seq"), None),
        P(("dp", "seq")),
        P(("dp", "seq")),
        P(("dp", "seq")),
        P(("dp", "seq"), None),
        P(("dp", "seq")),
        P(("dp", "seq"), None),
        P(("dp", "seq")),
        P(("dp", "seq")),
        P(("dp", "seq")),
    )
    fits = dict(mesh.shape) == {"dp": 4, "seq": 8}
    body = local if fits else plain
    return jax.shard_map(body, mesh=mesh, in_specs=in_specs, out_specs=out_specs, check_vma=False)
```

```python
import functools

import jax
import jax.numpy as jnp
from jax import lax
from jax.experimental import pallas as pl
from jax.experimental.pallas import tpu as pltpu
from jax.sharding import PartitionSpec as P

HD = 64
SEGMAX = 256
EPS = 1e-05
LOG2E = 1.4426950408889634
SCORE_SCALE = 0.125 * LOG2E
HIDDEN = -1e30
PAIR = 2 * HD
MESH = pl.DeviceIdType.MESH
BF16 = jnp.bfloat16
F32 = jnp.float32
VMEM = 64 * 2**20


group_heads = 4


def passed_along(block, axis, distance):
    devices = range(lax.axis_size(axis))
    route = [(i - distance, i) for i in devices if i - distance in devices]
    return lax.ppermute(block, axis, route)


def normalize(hidden, gain, shift):
    center = hidden - jnp.mean(hidden, axis=-1, keepdims=True)
    spread = jnp.mean(center * center, axis=-1, keepdims=True)
    return center * lax.rsqrt(spread + 1e-05) * gain + shift


def contract_rows(left, right):
    return lax.dot_general(
        left, right, (((0,), (0,)), ((), ())), preferred_element_type=jnp.float32
    )


def times_transposed(left, right):
    return lax.dot_general(
        left, right, (((1,), (1,)), ((), ())), preferred_element_type=jnp.float32
    )


def column_sum(values):
    return jnp.sum(values.astype(jnp.float32), axis=0)


def plain(
    hidden_in,
    segment_ids,
    query_weight,
    query_bias,
    key_weight,
    value_weight,
    value_bias,
    output_weight,
    output_bias,
    first_gain,
    first_shift,
    inner_weight,
    inner_bias,
    outer_weight,
    outer_bias,
    second_gain,
    second_shift,
    cotangent,
):
    rows_here, tokens, width = hidden_in.shape
    window = tokens + SEGMAX
    span = group_heads * HD
    groups = width // span
    items = jnp.arange(rows_here * groups, dtype=jnp.int32)
    (
        query_matrix,
        query_offset,
        key_matrix,
        value_matrix,
        value_offset,
        output_matrix,
        output_offset,
        first_scale,
        first_offset,
    ) = (
        lax.all_gather(query_weight, ("dp", "seq"), axis=0, tiled=True),
        lax.all_gather(query_bias, ("dp", "seq"), axis=0, tiled=True),
        lax.all_gather(key_weight, ("dp", "seq"), axis=0, tiled=True),
        lax.all_gather(value_weight, ("dp", "seq"), axis=0, tiled=True),
        lax.all_gather(value_bias, ("dp", "seq"), axis=0, tiled=True),
        lax.all_gather(output_weight, ("dp", "seq"), axis=0, tiled=True),
        lax.all_gather(output_bias, ("dp", "seq"), axis=0, tiled=True),
        lax.all_gather(first_gain, ("dp", "seq"), axis=0, tiled=True),
        lax.all_gather(first_shift, ("dp", "seq"), axis=0, tiled=True),
    )
    flat = hidden_in.reshape(rows_here * tokens, width)
    offset = lax.axis_index("seq") * tokens
    padded_ids = jnp.concatenate(
        [jnp.full((rows_here, SEGMAX), -1, jnp.int32), segment_ids], axis=1
    )
    key_ids = lax.dynamic_slice_in_dim(padded_ids, offset, window, 1)
    query_ids = key_ids[:, SEGMAX:]
    diagonal = jnp.arange(window)[None, :] == jnp.arange(tokens)[:, None] + SEGMAX
    visible = (query_ids[:, :, None] == key_ids[:, None, :]) & (
        query_ids[:, :, None] > 0
    ) | diagonal[None]
    queries = (
        (
            jnp.dot(flat, query_matrix, preferred_element_type=jnp.float32)
            + query_offset.astype(jnp.float32)
        )
        .astype(jnp.bfloat16)
        .reshape(rows_here, tokens, width)
    )
    keys_own = (
        jnp.dot(flat, key_matrix, preferred_element_type=jnp.float32)
        .astype(jnp.bfloat16)
        .reshape(rows_here, tokens, width)
    )
    values_own = (
        (
            jnp.dot(flat, value_matrix, preferred_element_type=jnp.float32)
            + value_offset.astype(jnp.float32)
        )
        .astype(jnp.bfloat16)
        .reshape(rows_here, tokens, width)
    )
    tails = passed_along(
        (keys_own[:, tokens - SEGMAX :], values_own[:, tokens - SEGMAX :]), "seq", 1
    )
    keys_all = jnp.concatenate([tails[0], keys_own], axis=1)
    values_all = jnp.concatenate([tails[1], values_own], axis=1)

    def pieces(item):
        row = item // groups
        column = item % groups * span
        query_part = lax.dynamic_slice(queries, (row, 0, column), (1, tokens, span))[0].reshape(
            tokens, group_heads, HD
        )
        key_part = lax.dynamic_slice(keys_all, (row, 0, column), (1, window, span))[0].reshape(
            window, group_heads, HD
        )
        value_part = lax.dynamic_slice(values_all, (row, 0, column), (1, window, span))[0].reshape(
            window, group_heads, HD
        )
        mask_row = lax.dynamic_index_in_dim(visible, row, 0, keepdims=False)
        scores = (
            jnp.einsum("qhd,khd->hqk", query_part, key_part, preferred_element_type=jnp.float32)
            * 0.125
        )
        scores = jnp.where(mask_row[None], scores, -1e30)
        return (row, column, query_part, key_part, value_part, scores)

    def attend(item):
        row, column, query_part, key_part, value_part, scores = pieces(item)
        highest = jnp.max(scores, axis=-1, keepdims=True)
        expo = jnp.exp(scores - highest)
        total = jnp.sum(expo, axis=-1, keepdims=True)
        probs = (expo / total).astype(jnp.bfloat16)
        mixed_part = jnp.einsum(
            "hqk,khd->qhd", probs, value_part, preferred_element_type=jnp.float32
        )
        return (
            mixed_part.astype(jnp.bfloat16).reshape(tokens, span),
            highest[..., 0] + jnp.log(total[..., 0]),
        )

    mixed_parts, logsums = lax.map(attend, items)
    mixed = (
        mixed_parts.reshape(rows_here, groups, tokens, span)
        .transpose(0, 2, 1, 3)
        .reshape(rows_here * tokens, width)
    )
    first_sum = (
        flat.astype(jnp.float32)
        + jnp.dot(mixed, output_matrix, preferred_element_type=jnp.float32)
        + output_offset.astype(jnp.float32)
    )
    normed = normalize(first_sum, first_scale.astype(jnp.float32), first_offset.astype(jnp.float32))
    normed_low = normed.astype(jnp.bfloat16)
    inner_matrix, inner_offset, outer_matrix, outer_offset, second_scale, second_offset = (
        lax.all_gather(inner_weight, ("dp", "seq"), axis=0, tiled=True),
        lax.all_gather(inner_bias, ("dp", "seq"), axis=0, tiled=True),
        lax.all_gather(outer_weight, ("dp", "seq"), axis=0, tiled=True),
        lax.all_gather(outer_bias, ("dp", "seq"), axis=0, tiled=True),
        lax.all_gather(second_gain, ("dp", "seq"), axis=0, tiled=True),
        lax.all_gather(second_shift, ("dp", "seq"), axis=0, tiled=True),
    )
    inner = jnp.dot(
        normed_low, inner_matrix, preferred_element_type=jnp.float32
    ) + inner_offset.astype(jnp.float32)
    active_low = jax.nn.gelu(inner, approximate=False).astype(jnp.bfloat16)
    second_sum = (
        normed
        + jnp.dot(active_low, outer_matrix, preferred_element_type=jnp.float32)
        + outer_offset.astype(jnp.float32)
    )
    layer_out = normalize(
        second_sum, second_scale.astype(jnp.float32), second_offset.astype(jnp.float32)
    )
    layer_out = layer_out.astype(jnp.bfloat16).reshape(rows_here, tokens, width)
    inner_matrix, inner_offset, outer_matrix, outer_offset, second_scale, second_offset = (
        lax.all_gather(inner_weight, ("dp", "seq"), axis=0, tiled=True),
        lax.all_gather(inner_bias, ("dp", "seq"), axis=0, tiled=True),
        lax.all_gather(outer_weight, ("dp", "seq"), axis=0, tiled=True),
        lax.all_gather(outer_bias, ("dp", "seq"), axis=0, tiled=True),
        lax.all_gather(second_gain, ("dp", "seq"), axis=0, tiled=True),
        lax.all_gather(second_shift, ("dp", "seq"), axis=0, tiled=True),
    )
    upstream = cotangent.reshape(rows_here * tokens, width).astype(jnp.float32)
    _, pull_second = jax.vjp(
        normalize, second_sum, second_scale.astype(jnp.float32), second_offset.astype(jnp.float32)
    )
    grad_second, second_gain_grad, second_shift_grad = pull_second(upstream)
    outer_grad = grad_second.astype(jnp.bfloat16)
    outer_weight_grad = contract_rows(active_low, outer_grad)
    outer_bias_grad = column_sum(outer_grad)
    _, pull_gelu = jax.vjp(lambda value: jax.nn.gelu(value, approximate=False), inner)
    (inner_grad_full,) = pull_gelu(times_transposed(outer_grad, outer_matrix))
    inner_grad = inner_grad_full.astype(jnp.bfloat16)
    inner_weight_grad = contract_rows(normed_low, inner_grad)
    inner_bias_grad = column_sum(inner_grad)
    grad_normed = grad_second + times_transposed(inner_grad, inner_matrix)
    (
        query_matrix,
        query_offset,
        key_matrix,
        value_matrix,
        value_offset,
        output_matrix,
        output_offset,
        first_scale,
        first_offset,
    ) = (
        lax.all_gather(query_weight, ("dp", "seq"), axis=0, tiled=True),
        lax.all_gather(query_bias, ("dp", "seq"), axis=0, tiled=True),
        lax.all_gather(key_weight, ("dp", "seq"), axis=0, tiled=True),
        lax.all_gather(value_weight, ("dp", "seq"), axis=0, tiled=True),
        lax.all_gather(value_bias, ("dp", "seq"), axis=0, tiled=True),
        lax.all_gather(output_weight, ("dp", "seq"), axis=0, tiled=True),
        lax.all_gather(output_bias, ("dp", "seq"), axis=0, tiled=True),
        lax.all_gather(first_gain, ("dp", "seq"), axis=0, tiled=True),
        lax.all_gather(first_shift, ("dp", "seq"), axis=0, tiled=True),
    )
    _, pull_first = jax.vjp(
        normalize, first_sum, first_scale.astype(jnp.float32), first_offset.astype(jnp.float32)
    )
    grad_first, first_gain_grad, first_shift_grad = pull_first(grad_normed)
    attn_grad = grad_first.astype(jnp.bfloat16)
    output_weight_grad = contract_rows(mixed, attn_grad)
    output_bias_grad = column_sum(attn_grad)
    grad_mixed = (
        times_transposed(attn_grad, output_matrix)
        .astype(jnp.bfloat16)
        .reshape(rows_here, tokens, width)
    )

    def attend_back(item):
        row, column, query_part, key_part, value_part, scores = pieces(item)
        logsum = lax.dynamic_index_in_dim(logsums, item, 0, keepdims=False)
        grad_part = lax.dynamic_slice(grad_mixed, (row, 0, column), (1, tokens, span))[0].reshape(
            tokens, group_heads, HD
        )
        probs = jnp.exp(scores - logsum[..., None])
        dprob = jnp.einsum(
            "qhd,khd->hqk", grad_part, value_part, preferred_element_type=jnp.float32
        )
        delta = jnp.sum(probs * dprob, axis=-1, keepdims=True)
        score_grad = (probs * (dprob - delta)).astype(jnp.bfloat16)
        query_part_grad = (
            jnp.einsum("hqk,khd->qhd", score_grad, key_part, preferred_element_type=jnp.float32)
            * 0.125
        )
        key_part_grad = (
            jnp.einsum("hqk,qhd->khd", score_grad, query_part, preferred_element_type=jnp.float32)
            * 0.125
        )
        value_part_grad = jnp.einsum(
            "hqk,qhd->khd",
            probs.astype(jnp.bfloat16),
            grad_part,
            preferred_element_type=jnp.float32,
        )
        return (
            query_part_grad.reshape(tokens, span),
            key_part_grad.reshape(window, span),
            value_part_grad.reshape(window, span),
        )

    query_parts, key_parts, value_parts = lax.map(attend_back, items)
    query_full = (
        query_parts.reshape(rows_here, groups, tokens, span)
        .transpose(0, 2, 1, 3)
        .reshape(rows_here * tokens, width)
    )
    key_window = (
        key_parts.reshape(rows_here, groups, window, span)
        .transpose(0, 2, 1, 3)
        .reshape(rows_here, window, width)
    )
    value_window = (
        value_parts.reshape(rows_here, groups, window, span)
        .transpose(0, 2, 1, 3)
        .reshape(rows_here, window, width)
    )
    returned = (
        passed_along(key_window[:, :SEGMAX].astype(jnp.bfloat16), "seq", -1).astype(jnp.float32),
        passed_along(value_window[:, :SEGMAX].astype(jnp.bfloat16), "seq", -1).astype(jnp.float32),
    )
    key_own = key_window[:, SEGMAX:]
    value_own = value_window[:, SEGMAX:]
    key_total = jnp.concatenate(
        [key_own[:, : tokens - SEGMAX], key_own[:, tokens - SEGMAX :] + returned[0]], axis=1
    )
    value_total = jnp.concatenate(
        [value_own[:, : tokens - SEGMAX], value_own[:, tokens - SEGMAX :] + returned[1]], axis=1
    )
    query_grad = query_full.astype(jnp.bfloat16)
    key_grad = key_total.reshape(rows_here * tokens, width).astype(jnp.bfloat16)
    value_grad = value_total.reshape(rows_here * tokens, width).astype(jnp.bfloat16)
    query_weight_grad = contract_rows(flat, query_grad)
    query_bias_grad = column_sum(query_grad)
    key_weight_grad = contract_rows(flat, key_grad)
    value_weight_grad = contract_rows(flat, value_grad)
    value_bias_grad = column_sum(value_grad)
    grad_hidden = (
        grad_first
        + times_transposed(query_grad, query_matrix)
        + times_transposed(key_grad, key_matrix)
        + times_transposed(value_grad, value_matrix)
    ).reshape(rows_here, tokens, width)
    shards = (
        lax.psum_scatter(query_weight_grad, ("dp", "seq"), scatter_dimension=0, tiled=True),
        lax.psum_scatter(query_bias_grad, ("dp", "seq"), scatter_dimension=0, tiled=True),
        lax.psum_scatter(key_weight_grad, ("dp", "seq"), scatter_dimension=0, tiled=True),
        lax.psum_scatter(value_weight_grad, ("dp", "seq"), scatter_dimension=0, tiled=True),
        lax.psum_scatter(value_bias_grad, ("dp", "seq"), scatter_dimension=0, tiled=True),
        lax.psum_scatter(output_weight_grad, ("dp", "seq"), scatter_dimension=0, tiled=True),
        lax.psum_scatter(output_bias_grad, ("dp", "seq"), scatter_dimension=0, tiled=True),
        lax.psum_scatter(first_gain_grad, ("dp", "seq"), scatter_dimension=0, tiled=True),
        lax.psum_scatter(first_shift_grad, ("dp", "seq"), scatter_dimension=0, tiled=True),
        lax.psum_scatter(inner_weight_grad, ("dp", "seq"), scatter_dimension=0, tiled=True),
        lax.psum_scatter(inner_bias_grad, ("dp", "seq"), scatter_dimension=0, tiled=True),
        lax.psum_scatter(outer_weight_grad, ("dp", "seq"), scatter_dimension=0, tiled=True),
        lax.psum_scatter(outer_bias_grad, ("dp", "seq"), scatter_dimension=0, tiled=True),
        lax.psum_scatter(second_gain_grad, ("dp", "seq"), scatter_dimension=0, tiled=True),
        lax.psum_scatter(second_shift_grad, ("dp", "seq"), scatter_dimension=0, tiled=True),
    )
    return (
        layer_out,
        grad_hidden,
        shards[0],
        shards[1],
        shards[2],
        shards[3],
        shards[4],
        shards[5],
        shards[6],
        shards[7],
        shards[8],
        shards[9],
        shards[10],
        shards[11],
        shards[12],
        shards[13],
        shards[14],
    )


GRID = (2, 2, 4, 2)
FF_PARTS = 8
PART = 512
EARLY = 5
PIECE = GRID + (32, PART)


class Place:
    def __init__(self):
        dp = lax.axis_index("dp")
        seq = lax.axis_index("seq")
        self.x = lax.rem(dp, 2)
        self.y = lax.div(dp, 2)
        self.z = lax.div(seq, 2)
        self.c = lax.rem(seq, 2)
        self.seq = seq

    def device(self, x=None, y=None, z=None, c=None):
        x = self.x if x is None else x
        y = self.y if y is None else y
        z = self.z if z is None else z
        c = self.c if c is None else c
        return (y * 2 + x, z * 2 + c)

    def peer(self, dim):
        if dim == "x":
            return self.device(x=1 - self.x)
        if dim == "y":
            return self.device(y=1 - self.y)
        if dim == "c":
            return self.device(c=1 - self.c)
        return self.device(z=lax.rem(self.z + dim, 4))


def signal(semaphore, device):
    pl.semaphore_signal(semaphore, inc=1, device_id=device, device_id_type=MESH)


def meet(place, along=0):
    barrier = pltpu.get_barrier_semaphore()
    for dim in ("x", "y", "c", 1, 2, 3):
        signal(barrier, place.peer(dim))
    extra = 0
    if along:
        up = (place.c == 1) & (place.z < 3)
        down = (place.c == 0) & (place.z > 0)
        receives, sends = (down, up) if along > 0 else (up, down)
        other = lax.rem(place.z + (3 if along > 0 else 1), 4)

        @pl.when(receives)
        def _():
            signal(barrier, place.device(z=other, c=1 - place.c))

        extra = sends.astype(jnp.int32)
    pl.semaphore_wait(barrier, 6 + extra)


def remote(src, dst, send, recv, device):
    return pltpu.make_async_remote_copy(
        src_ref=src, dst_ref=dst, send_sem=send, recv_sem=recv, device_id=device, device_id_type=MESH
    )


class Gather:
    def __init__(self, place, order, source, target, send, recv):
        held = {"x": False, "y": False, "z": False}

        def region():
            index = []
            for name, size in (("y", 2), ("x", 2), ("z", 4)):
                index.append(pl.ds(0, size) if held[name] else pl.ds(getattr(place, name), 1))
            return target(index[0], index[1], index[2], pl.ds(place.c, 1))

        self.own = pltpu.make_async_copy(source, region(), recv.at[6])
        self.phases = []
        for number, dim in enumerate(order):
            here = region()
            copies = []
            for partner in (1, 2, 3) if dim == "z" else (dim,):
                slot = partner - 1 if dim == "z" else {"x": 3, "y": 4}[dim]
                copies.append(
                    remote(
                        source if number == 0 else here,
                        here,
                        send.at[slot],
                        recv.at[slot],
                        place.peer(partner),
                    )
                )
            self.phases.append(copies)
            held[dim] = True
        here = region()
        self.phases.append([remote(here, here, send.at[5], recv.at[5], place.peer("c"))])

    def start(self, phase):
        if phase == 0:
            self.own.start()
        for copy in self.phases[phase]:
            copy.start()

    def arrive(self, phase):
        for copy in self.phases[phase]:
            copy.wait_recv()
        if phase == 0:
            self.own.wait()

    def step(self, phase):
        if phase > 0:
            self.arrive(phase - 1)
        if phase < 4:
            self.start(phase)

    def finish(self):
        for copies in self.phases:
            for copy in copies:
                copy.wait_send()


class Sums:
    def __init__(self, place, count, stage, slot, bufs, store, halves=2, ready=None, order=None, offsets=(0, 1, 3, 5, 7)):
        self.place, self.count, self.stage, self.slot = place, count, stage, slot
        self.order, self.offsets = order, offsets
        self.r0, self.r1, self.r2, self.r3, self.send, self.recv = bufs
        self.store, self.halves, self.ready = store, halves, ready

    def copies(self, j, half, phase):
        place = self.place
        send, recv = self.send.at[j, half], self.recv.at[j, half]
        r0, r1, r2, r3 = (ref.at[j, half] for ref in (self.r0, self.r1, self.r2, self.r3))
        if phase == 0:
            source = self.stage.at[self.slot(j), :, :, :, 1 - place.c, pl.ds(16 * half, 16)]
            return [remote(source, r0, send.at[0], recv.at[0], place.peer("c"))]
        if phase == 1:
            source, dim = (r0.at[1 - place.y], "y") if half == 0 else (r0.at[:, 1 - place.x], "x")
            return [remote(source, r1, send.at[1], recv.at[1], place.peer(dim))]
        if phase == 2:
            source, dim = (r1.at[1 - place.x], "x") if half == 0 else (r1.at[1 - place.y], "y")
            return [remote(source, r2, send.at[2], recv.at[2], place.peer(dim))]
        return [
            remote(r2.at[lax.rem(place.z + k, 4)], r3.at[k - 1], send.at[2 + k], recv.at[2 + k], place.peer(k))
            for k in (1, 2, 3)
        ]

    def step(self, j, phase):
        place = self.place
        if phase == 0 and self.ready is not None:
            self.ready(j)
        for half in range(self.halves):
            if phase > 0:
                for copy in self.copies(j, half, phase - 1):
                    copy.wait_recv()
            if phase == 1:
                self.copies(j, half, 0)[0].wait_send()
                mine = self.stage[self.slot(j), :, :, :, place.c, 16 * half : 16 * half + 16, :]
                self.r0[j, half] = self.r0[j, half] + mine
            elif phase == 2:
                mine = self.r0[j, half, place.y] if half == 0 else self.r0[j, half, :, place.x]
                self.r1[j, half] = self.r1[j, half] + mine
            elif phase == 3:
                mine = self.r1[j, half, place.x] if half == 0 else self.r1[j, half, place.y]
                self.r2[j, half] = self.r2[j, half] + mine
            elif phase == 4:
                total = self.r2[j, half, place.z].astype(F32)
                for k in range(3):
                    total = total + self.r3[j, half, k].astype(F32)
                self.store(j, half, total)
            if phase < 4:
                for copy in self.copies(j, half, phase):
                    copy.start()

    def tick(self, time):
        for phase, offset in enumerate(self.offsets):
            j = time - offset
            valid = (j >= 0) & (j < self.count)
            if self.order is not None:
                j, valid = self.order(j)
            if isinstance(valid, bool):
                if valid:
                    self.step(j, phase)
            else:
                pl.when(valid)(functools.partial(self.step, j, phase))

    def finish(self):
        def body(j, carry):
            for half in range(self.halves):
                for phase in (1, 2, 3):
                    for copy in self.copies(j, half, phase):
                        copy.wait_send()
            return carry

        lax.fori_loop(0, self.count, body, 0)


def sums_buffers(count, columns=512, halves=2):
    block = (16, columns)
    return [
        pltpu.VMEM((count, halves, 2, 2, 4) + block, BF16),
        pltpu.VMEM((count, halves, 2, 4) + block, BF16),
        pltpu.VMEM((count, halves, 4) + block, BF16),
        pltpu.VMEM((count, halves, 3) + block, BF16),
        pltpu.SemaphoreType.DMA((count, halves, 6)),
        pltpu.SemaphoreType.DMA((count, halves, 6)),
    ]


def advance(slots, time, offsets):
    for phase, offset in enumerate(offsets):
        number = time - offset
        if 0 <= number < len(slots):
            for part in slots[number]:
                part.step(phase)


def dot(left, right):
    return jnp.dot(left, right, preferred_element_type=F32)


def dot_nt(left, right):
    return lax.dot_general(left, right, (((1,), (1,)), ((), ())), preferred_element_type=F32)


def dot_tn(left, right):
    return lax.dot_general(left, right, (((0,), (0,)), ((), ())), preferred_element_type=F32)


def spread(blocks, row, base, width, count):
    flat = blocks.reshape(32 * 16, 128)
    lane = lax.broadcasted_iota(jnp.int32, (128, count), 0)
    column = lax.broadcasted_iota(jnp.int32, (128, count), 1)
    pick = jnp.where(lane == base + lax.rem(column, width), 1.0, 0.0).astype(BF16)
    wide = dot(flat, pick)
    at = lax.broadcasted_iota(jnp.int32, (32 * 16, count), 0)
    column = lax.broadcasted_iota(jnp.int32, (32 * 16, count), 1)
    keep = at == lax.div(column, width) * 16 + row
    return jnp.sum(jnp.where(keep, wide, 0.0), axis=0, keepdims=True)


BEATS = (0, 1, 3, 5, 6)


def gather_slots(place, source, target, pieces, send, recv):
    slots = []
    number = 0
    for rows, first, columns in pieces:
        pair = []
        for half, order in enumerate(("zxy", "zyx")):
            cols = pl.ds(first + half * columns // 2, columns // 2)
            pair.append(
                Gather(
                    place,
                    order,
                    source.at[:, :, :, :, rows, cols],
                    lambda y, x, z, c, rows=rows, cols=cols: target.at[y, x, z, c, rows, cols],
                    send.at[number],
                    recv.at[number],
                )
            )
            number += 1
        slots.append(pair)
    return slots


def finish_slots(slots):
    for slot in slots:
        for part in slot:
            part.finish()


def mask_scores(key_ids, query_ids):
    keys, queries = key_ids.shape[0], query_ids.shape[1]
    key_at = lax.broadcasted_iota(jnp.int32, (keys, queries), 0)
    query_at = lax.broadcasted_iota(jnp.int32, (keys, queries), 1)
    visible = ((key_ids == query_ids) & (query_ids > 0)) | (key_at == query_at + SEGMAX)
    return jnp.where(visible, 0.0, HIDDEN).astype(F32)


def one_head(block, head):
    lane = lax.broadcasted_iota(jnp.int32, block.shape, 1)
    return jnp.where(lax.div(lane, HD) == head, block, jnp.zeros_like(block))


def layer_norm(value):
    center = value - jnp.mean(value, axis=-1, keepdims=True)
    scale = lax.rsqrt(jnp.mean(center * center, axis=-1, keepdims=True) + EPS)
    return center * scale, scale


def layer_norm_back(grad, unit, scale):
    return scale * (
        grad
        - jnp.mean(grad, axis=-1, keepdims=True)
        - unit * jnp.mean(grad * unit, axis=-1, keepdims=True)
    )


def encode_kernel(
    x_in, key_ids, query_ids, v0, v1, v2, v3, v4, v5, v6, v7, v8, wq_in, wk_in, wv_in, wo_in, inner_in, outer_in,
    q_out, k_out, v_out, xt_out, w_out, mixed_out, unit_out, low_out, inner_out, outer_out, lse, scale, vec, ib_out,
    weights, small, smalls, xt, q, k, v, mixed, unit, low, bias, inner_own, outer_own, send, recv, tail_sem, local_sem,
):
    place = Place()
    tokens, width = x_in.shape[1], x_in.shape[2]
    own_x = pltpu.make_async_copy(x_in, xt.at[:, pl.ds(SEGMAX, tokens)], local_sem.at[0])
    own_x.start()
    own_ff = [
        pltpu.make_async_copy(inner_in, inner_own, local_sem.at[14]),
        pltpu.make_async_copy(outer_in, outer_own, local_sem.at[15]),
    ]
    for copy in own_ff:
        copy.start()
    at = lax.broadcasted_iota(jnp.int32, (16, 128), 0)
    block = jnp.zeros((16, 128), F32)
    for number, vector in enumerate((v0, v1, v2, v3, v4, v5, v6, v7, v8)):
        size = vector.shape[1]
        base, row = (number % 4 * 32, number // 4) if number < 8 else (0, 2)
        lane = lax.broadcasted_iota(jnp.int32, (size, 128), 1)
        index = lax.broadcasted_iota(jnp.int32, (size, 128), 0)
        pick = jnp.where(lane == base + index, 1.0, 0.0).astype(BF16)
        wide = dot(jnp.broadcast_to(vector[...], (16, size)), pick)
        block = block + jnp.where(at == row, wide, 0.0)
    small[0, 0, 0, 0] = block.astype(BF16)
    meet(place, 1)
    half = width // 2
    slots = [[Gather(place, "zxy", small, lambda y, x, z, c: smalls.at[y, x, z, c], send.at[48], recv.at[48])]]
    everything, used = slice(None), 0

    def add(source, target, pieces):
        nonlocal used, slots
        sems = pl.ds(used, 2 * len(pieces))
        used += 2 * len(pieces)
        slots += gather_slots(place, source, target, pieces, send.at[sems], recv.at[sems])

    for matrix, source in enumerate((wq_in, wk_in, wv_in, wo_in)):
        add(source, weights.at[matrix], [(everything, part * half, half) for part in range(2)])
    add(inner_own, inner_out, [(everything, part * PART, PART) for part in range(FF_PARTS)])
    add(outer_own, outer_out, [(pl.ds(part * 16, 16), 0, width) for part in range(8)])

    tail = remote(
        x_in.at[:, pl.ds(tokens - SEGMAX, SEGMAX)],
        xt.at[:, pl.ds(0, SEGMAX)],
        tail_sem.at[0],
        tail_sem.at[1],
        place.device(z=lax.rem(place.z + place.c, 4), c=1 - place.c),
    )
    has_next, has_last = place.seq < 7, place.seq > 0
    saves = []

    def save(source, target):
        copy = pltpu.make_async_copy(source, target, local_sem.at[1 + len(saves)])
        copy.start()
        saves.append(copy)

    def project(matrix, part):
        target, bias_row, first = ((q, 0, SEGMAX), (k, None, 0), (v, 1, 0))[matrix]
        columns = slice(part * half, part * half + half)
        for row in range(2):
            out = dot(xt[row, first:, :], weights[matrix, :, :, :, :, :, columns].reshape(width, half))
            if bias_row is not None:
                out = out + vec[bias_row : bias_row + 1, columns]
            target[row, :, columns] = out.astype(BF16)

    last = BEATS[-1]
    first_beats = last + 7
    for time in range(first_beats):
        if time == 3:
            pl.when(has_next)(tail.start)
            xt_zero = jnp.zeros((2, SEGMAX, width), BF16)

            @pl.when(place.seq == 0)
            def _():
                xt[:, :SEGMAX, :] = xt_zero

            own_x.wait()
            for copy in own_ff:
                copy.wait()
        advance(slots, time, BEATS)
        done = time - last
        if done == 0:
            for vector in range(8):
                vec[vector : vector + 1, :] = spread(smalls[...], vector // 4, vector % 4 * 32, 32, width)
            vec[8:, :] = jnp.zeros((8, width), F32)
            for part in range(FF_PARTS):
                for device in range(4):
                    index = part * 4 + device
                    row = smalls[index // 16, index // 8 % 2, index // 2 % 4, index % 2]
                    ib_out[part : part + 1, device * 128 : device * 128 + 128] = row[2:3, :].astype(F32)
        if 1 <= done <= 6:
            matrix, part = (done - 1) // 2, (done - 1) % 2
            if matrix == 1 and part == 0:
                pl.when(has_last)(tail.wait_recv)
                save(xt, xt_out)
            project(matrix, part)
            if part == 1:
                save(weights.at[matrix], w_out.at[matrix])
                save((q, k, v)[matrix], (q_out, k_out, v_out)[matrix])

    pairs = width // PAIR
    count = 2 * pairs
    rest = len(slots) + last - first_beats

    def beats(times):
        for time in times:
            advance(slots, time, BEATS)

    def attend(item, carry):
        row, pair = lax.div(item, pairs), lax.rem(item, pairs)
        for number in range(count):
            times = range(first_beats + number * rest // count, first_beats + (number + 1) * rest // count)
            if times:
                pl.when(item == number)(functools.partial(beats, times))

        @pl.when(pair == 0)
        def _():
            bias[...] = mask_scores(key_ids[row], query_ids[row])

        columns = pl.ds(pl.multiple_of(pair * PAIR, PAIR), PAIR)
        v_t = v[row, :, columns].T
        for start in range(0, tokens, 256):
            low_key = 0 if start == 0 else start
            queries = q[row, start : start + 256, columns]
            keys = k[row, low_key:, columns]
            parts = []
            for head in range(2):
                s = dot_nt(keys, one_head(queries, head)) * SCORE_SCALE + bias[low_key:, start : start + 256]
                highest = jnp.max(s, axis=0, keepdims=True)
                expo = jnp.exp2(s - highest)
                total = jnp.sum(expo, axis=0, keepdims=True)
                out = dot(v_t[head * HD : head * HD + HD, low_key:], expo.astype(BF16))
                parts.append(out * (1.0 / total))
                lse[row, pair, head : head + 1, start : start + 256] = highest + jnp.log2(total)
            mixed[row, start : start + 256, columns] = jnp.concatenate(parts, axis=0).T.astype(BF16)

        @pl.when(pair == pairs - 1)
        def _():
            matrix = weights[3].reshape(width, width)
            for start in range(0, tokens, 256):
                rows = pl.ds(start, 256)
                residual = xt[row, SEGMAX + start : SEGMAX + start + 256, :].astype(F32)
                total = dot(mixed[row, rows, :], matrix) + residual + vec[2:3, :]
                centered, spread_ = layer_norm(total)
                unit[row, rows, :] = centered
                scale[row, rows, :] = spread_
                low[row, rows, :] = (centered * vec[3:4, :] + vec[4:5, :]).astype(BF16)

        return carry

    lax.fori_loop(0, count, attend, 0)
    save(weights.at[3], w_out.at[3])
    for source, target in ((mixed, mixed_out), (unit, unit_out), (low, low_out)):
        save(source, target)
    finish_slots(slots)
    pl.when(has_next)(tail.wait_send)
    for copy in saves:
        copy.wait()


def encode(hidden, key_ids, query_ids, vectors, wq, wk, wv, wo, inner, outer):
    rows, tokens, width = hidden.shape
    window = tokens + SEGMAX
    hbm = pl.BlockSpec(memory_space=pltpu.HBM)
    vmem = pl.BlockSpec(memory_space=pltpu.VMEM)
    lead = lambda a: a.reshape((1, 1, 1, 1) + a.shape)
    block = wq.shape
    own, wide = (rows, tokens, width), (rows, window, width)
    return pl.pallas_call(
        encode_kernel,
        out_shape=[
            jax.ShapeDtypeStruct(own, BF16),
            jax.ShapeDtypeStruct(wide, BF16),
            jax.ShapeDtypeStruct(wide, BF16),
            jax.ShapeDtypeStruct(wide, BF16),
            jax.ShapeDtypeStruct((4,) + GRID + block, BF16),
            jax.ShapeDtypeStruct(own, BF16),
            jax.ShapeDtypeStruct(own, F32),
            jax.ShapeDtypeStruct(own, BF16),
            jax.ShapeDtypeStruct(GRID + inner.shape, BF16),
            jax.ShapeDtypeStruct(GRID + outer.shape, BF16),
            jax.ShapeDtypeStruct((rows, width // PAIR, 8, tokens), F32),
            jax.ShapeDtypeStruct((rows, tokens, 1), F32),
            jax.ShapeDtypeStruct((16, width), F32),
            jax.ShapeDtypeStruct((FF_PARTS, PART), F32),
        ],
        in_specs=[hbm] + [vmem] * 11 + [hbm] * 6,
        out_specs=[hbm] * 10 + [vmem] * 4,
        scratch_shapes=[
            pltpu.VMEM((4,) + GRID + block, BF16),
            pltpu.VMEM((1, 1, 1, 1, 16, 128), BF16),
            pltpu.VMEM(GRID + (16, 128), BF16),
            pltpu.VMEM(wide, BF16),
            pltpu.VMEM(own, BF16),
            pltpu.VMEM(wide, BF16),
            pltpu.VMEM(wide, BF16),
            pltpu.VMEM(own, BF16),
            pltpu.VMEM(own, F32),
            pltpu.VMEM(own, BF16),
            pltpu.VMEM((window, tokens), F32),
            pltpu.VMEM((1, 1, 1, 1) + inner.shape, BF16),
            pltpu.VMEM((1, 1, 1, 1) + outer.shape, BF16),
            pltpu.SemaphoreType.DMA((49, 8)),
            pltpu.SemaphoreType.DMA((49, 8)),
            pltpu.SemaphoreType.DMA((2,)),
            pltpu.SemaphoreType.DMA((16,)),
        ],
        compiler_params=pltpu.CompilerParams(collective_id=0, has_side_effects=True, vmem_limit_bytes=VMEM),
        name="gather_encode",
    )(
        hidden, key_ids, query_ids, *[v.reshape(1, -1) for v in vectors],
        lead(wq), lead(wk), lead(wv), lead(wo), lead(inner), lead(outer),
    )


def gelu_both(value):
    bell = jnp.exp2(value * value * (-0.5 * LOG2E)) * 0.3989422804014327
    below = 0.5 + 0.5 * lax.erf(value * 0.7071067811865476)
    return value * below, below + value * bell


def forward_kernel(
    low, unit, cot, inner_w, inner_b, outer_in, vec,
    active, slope, layer_out, og, grad_second, sums,
    acts, outer, total, load_sem,
):
    step = pl.program_id(0)
    tokens, width = low.shape
    load = pltpu.make_async_copy(outer_in, outer, load_sem)
    pl.when(step == 0)(load.start)

    @pl.when(step < FF_PARTS)
    def _():
        w1 = inner_w[...].reshape(width, PART)
        for start in range(0, tokens, 512):
            rows = pl.ds(start, 512)
            inner = dot(low[rows, :], w1) + inner_b[0]
            act, der = gelu_both(inner)
            act = act.astype(BF16)
            active[rows, :] = act
            slope[rows, :] = der.astype(BF16)
            acts[rows, pl.ds(pl.multiple_of(step * PART, PART), PART)] = act

    @pl.when(step == FF_PARTS)
    def _():
        load.wait()
        sums[...] = jnp.zeros_like(sums)

    @pl.when(step >= FF_PARTS)
    def _():
        rows = pl.ds(pl.multiple_of((step - FF_PARTS) * 512, 512), 512)
        for column in range(0, width, 512):
            w2 = outer[:, :, :, :, :, column : column + 512].reshape(-1, 512)
            total[:, column : column + 512] = dot(acts[rows, :], w2)
        for start in range(0, 512, 128):
            rows = pl.ds(start, 128)
            normed = unit[rows, :] * vec[3:4, :] + vec[4:5, :]
            centered, scale = layer_norm(total[rows, :] + normed + vec[5:6, :])
            layer_out[rows, :] = (centered * vec[6:7, :] + vec[7:8, :]).astype(BF16)
            up = cot[rows, :].astype(F32)
            grad = layer_norm_back(up * vec[6:7, :], centered, scale)
            grad_second[rows, :] = grad
            rounded = grad.astype(BF16)
            og[rows, :] = rounded
            sums[0:1, :] += jnp.sum(rounded.astype(F32), axis=0, keepdims=True)
            sums[1:2, :] += jnp.sum(up * centered, axis=0, keepdims=True)
            sums[2:3, :] += jnp.sum(up, axis=0, keepdims=True)


def feed_forward(low, unit, cot, inner, inner_b, outer, vec):
    tokens, width = low.shape
    ff = FF_PARTS * PART
    first = lambda s: jnp.minimum(s, FF_PARTS - 1)
    second = lambda s: jnp.maximum(s - FF_PARTS, 0)
    whole = lambda shape: pl.BlockSpec(shape, lambda s: (0,) * len(shape))
    column = pl.BlockSpec((tokens, PART), lambda s: (0, first(s)))
    rows = pl.BlockSpec((512, width), lambda s: (second(s), 0))
    hbm = pl.BlockSpec(memory_space=pltpu.HBM)
    return pl.pallas_call(
        forward_kernel,
        grid=(FF_PARTS + tokens // 512,),
        out_shape=[
            jax.ShapeDtypeStruct((tokens, ff), BF16),
            jax.ShapeDtypeStruct((tokens, ff), BF16),
            jax.ShapeDtypeStruct((tokens, width), BF16),
            jax.ShapeDtypeStruct((tokens, width), BF16),
            jax.ShapeDtypeStruct((tokens, width), F32),
            jax.ShapeDtypeStruct((8, width), F32),
        ],
        in_specs=[
            whole(low.shape), rows, rows,
            pl.BlockSpec(GRID + (inner.shape[4], PART), lambda s: (0, 0, 0, 0, 0, first(s))),
            pl.BlockSpec((1, 1, PART), lambda s: (first(s), 0, 0)),
            hbm, whole(vec.shape),
        ],
        out_specs=[column, column, rows, rows, rows, whole((8, width))],
        scratch_shapes=[
            pltpu.VMEM((tokens, ff), BF16),
            pltpu.VMEM(outer.shape, BF16),
            pltpu.VMEM((512, width), F32),
            pltpu.SemaphoreType.DMA,
        ],
        compiler_params=pltpu.CompilerParams(vmem_limit_bytes=VMEM),
        name="feed_forward",
    )(low, unit, cot, inner, inner_b.reshape(FF_PARTS, 1, PART), outer, vec)


def backward_kernel(
    active_in, slope, og, low, inner_w, outer_w, second_in, unit_in, scale, mixed_in, weights_in, vec,
    outer_sum, inner_sum, rest, ib_grad, first_out, gm_out, sums,
    acts, total, unit, mixed, wo, ig, stage, load_sem, save_sem, *bufs,
):
    step = pl.program_id(0)
    chunks = 4
    part = step - chunks
    tokens, width = og.shape
    place = Place()

    def store(j, half, value):
        @pl.when(j < FF_PARTS)
        def _():
            for group in range(4):
                outer_sum[
                    group * 32 + half * 16 : group * 32 + half * 16 + 16,
                    pl.ds(pl.multiple_of(j * 128, 128), 128),
                ] = value[:, group * 128 : group * 128 + 128]

        @pl.when(j >= FF_PARTS)
        def _():
            columns = pl.ds(pl.multiple_of((j - FF_PARTS) * PART, PART), PART)
            inner_sum[half * 16 : half * 16 + 16, columns] = value

    queue = Sums(place, FF_PARTS + EARLY, stage, lambda j: lax.rem(j, FF_PARTS), bufs, store)
    loads = [
        pltpu.make_async_copy(source, target, load_sem.at[number])
        for number, (source, target) in enumerate(
            ((active_in, acts), (second_in, total), (unit_in, unit), (mixed_in, mixed), (weights_in.at[3], wo))
        )
    ]

    def keep(number):
        return pltpu.make_async_copy(
            stage.at[number + EARLY if number < FF_PARTS - EARLY else number - FF_PARTS + EARLY],
            rest.at[number],
            save_sem.at[number],
        )

    @pl.when(step == 0)
    def _():
        for load in loads:
            load.start()
        meet(place)
        loads[0].wait()

    @pl.when(step < chunks)
    def _():
        right = og[:, pl.ds(pl.multiple_of(step * 256, 256), 256)]
        for y in range(2):
            for x in range(2):
                first = (y * 2 + x) * 1024
                grad = dot_tn(acts[:, first : first + 1024], right).astype(BF16).reshape(4, 2, 4, 32, 256)
                for piece in range(2):
                    for group in range(4):
                        stage[2 * step + piece, y, x, :, :, :, group * 128 : group * 128 + 128] = grad[
                            :, :, group, :, piece * 128 : piece * 128 + 128
                        ]
        queue.tick(step)

    @pl.when(step >= chunks)
    def _():
        w1 = inner_w[...].reshape(width, PART)
        w2 = outer_w[...].reshape(PART, width)
        ib_grad[...] = jnp.zeros_like(ib_grad)
        for start in range(0, tokens, 512):
            rows = pl.ds(start, 512)
            piece = (dot_nt(og[rows, :], w2) * slope[rows, :].astype(F32)).astype(BF16)
            ig[rows, :] = piece
            ib_grad[0] += jnp.sum(piece.astype(F32), axis=0, keepdims=True)
        beat = chunks + lax.div(3 * part, 2)
        odd = lax.rem(part, 2)
        pl.when(odd == 1)(functools.partial(queue.tick, beat))
        stage[part] = dot_tn(low[...], ig[...]).astype(BF16).reshape(PIECE)
        for number in range(FF_PARTS - EARLY):
            pl.when(part == EARLY + number)(lambda number=number: keep(number).start())
        queue.tick(beat + odd)
        pl.when(part == 0)(loads[1].wait)
        for start in range(0, tokens, 512):
            rows = pl.ds(start, 512)
            total[rows, :] += dot_nt(ig[rows, :], w1)

    @pl.when(step == pl.num_programs(0) - 1)
    def _():
        for load in loads[2:]:
            load.wait()
        sums[...] = jnp.zeros_like(sums)
        matrix = wo[...].reshape(width, width)
        for start in range(0, tokens, 256):
            rows = pl.ds(start, 256)
            up = total[rows, :]
            centered = unit[rows, :]
            grad = layer_norm_back(up * vec[3:4, :], centered, scale[rows, :])
            total[rows, :] = grad
            rounded = grad.astype(BF16)
            acts[rows, :width] = rounded
            sums[0:1, :] += jnp.sum(rounded.astype(F32), axis=0, keepdims=True)
            sums[1:2, :] += jnp.sum(up * centered, axis=0, keepdims=True)
            sums[2:3, :] += jnp.sum(up, axis=0, keepdims=True)
            acts[rows, width : 2 * width] = dot_nt(rounded, matrix).astype(BF16)
            queue.tick(FF_PARTS + EARLY + 3 + start // 256)
        save_first = pltpu.make_async_copy(total, first_out, load_sem.at[0])
        save_gm = pltpu.make_async_copy(acts.at[:, pl.ds(width, width)], gm_out, load_sem.at[1])
        save_first.start()
        save_gm.start()
        for piece in range(2):
            columns = slice(piece * PART, piece * PART + PART)
            stage[piece] = dot_tn(mixed[...], acts[:, columns]).astype(BF16).reshape(PIECE)
            keep(FF_PARTS - EARLY + piece).start()
        save_first.wait()
        save_gm.wait()
        for number in range(FF_PARTS - EARLY + 2):
            keep(number).wait()
        queue.finish()


def feed_backward(active, slope, og, low, inner, outer, grad_second, unit, scale, mixed, weights, vec):
    tokens, width = og.shape
    part = lambda s: jnp.maximum(s - 4, 0)
    whole = lambda shape: pl.BlockSpec(shape, lambda s: (0,) * len(shape), pipeline_mode=pl.Buffered(1))
    kept = lambda shape: pl.BlockSpec(shape, lambda s: (0,) * len(shape))
    hbm = pl.BlockSpec(memory_space=pltpu.HBM)
    count = FF_PARTS + EARLY
    rest = FF_PARTS - EARLY + 2
    return pl.pallas_call(
        backward_kernel,
        grid=(4 + FF_PARTS,),
        out_shape=[
            jax.ShapeDtypeStruct(outer.shape[4:], F32),
            jax.ShapeDtypeStruct((32, EARLY * PART), F32),
            jax.ShapeDtypeStruct((rest,) + PIECE, BF16),
            jax.ShapeDtypeStruct((FF_PARTS, 1, PART), F32),
            jax.ShapeDtypeStruct((tokens, width), F32),
            jax.ShapeDtypeStruct((tokens, width), BF16),
            jax.ShapeDtypeStruct((8, width), F32),
        ],
        in_specs=[
            hbm, pl.BlockSpec((tokens, PART), lambda s: (0, part(s))), whole(og.shape), whole(low.shape),
            pl.BlockSpec(GRID + (32, PART), lambda s: (0, 0, 0, 0, 0, part(s))),
            pl.BlockSpec((4, outer.shape[4], width), lambda s: (part(s), 0, 0)),
            hbm, hbm, whole(scale.shape), hbm, hbm, whole(vec.shape),
        ],
        out_specs=[
            kept(outer.shape[4:]), kept((32, EARLY * PART)), hbm,
            pl.BlockSpec((1, 1, PART), lambda s: (part(s), 0, 0)), hbm, hbm, kept((8, width)),
        ],
        scratch_shapes=[
            pltpu.VMEM((tokens, FF_PARTS * PART), BF16),
            pltpu.VMEM((tokens, width), F32),
            pltpu.VMEM((tokens, width), F32),
            pltpu.VMEM((tokens, width), BF16),
            pltpu.VMEM(GRID + (32, width), BF16),
            pltpu.VMEM((tokens, PART), BF16),
            pltpu.VMEM((FF_PARTS,) + PIECE, BF16),
            pltpu.SemaphoreType.DMA((5,)),
            pltpu.SemaphoreType.DMA((rest,)),
        ]
        + sums_buffers(count),
        compiler_params=pltpu.CompilerParams(
            collective_id=3, has_side_effects=True, vmem_limit_bytes=VMEM
        ),
        name="feed_backward",
    )(
        active, slope, og, low, inner, outer.reshape((32,) + outer.shape[4:]), grad_second, unit, scale, mixed,
        weights, vec,
    )


LATE = FF_PARTS - EARLY + 2
BACK = LATE + 4


def attend_back_kernel(
    q, k, v, gm, mixed, lse, key_ids, query_ids, xt, rest, inner_early,
    dq_out, dk_out, dv_out, tail_out, sums, inner_sum, wo_sum, qkv_sum,
    bias, dq_all, dk_all, dv_all, dk_sum, dv_sum, stage, load_sem, *bufs,
):
    group, row, inner = pl.program_id(0), pl.program_id(1), pl.program_id(2)
    step = group * 4 + row * 2 + inner
    tokens = q.shape[1]
    place = Place()

    def load(j):
        return pltpu.make_async_copy(rest.at[j], stage.at[j], load_sem.at[j])

    def ready(j):
        pl.when(j < LATE)(lambda: load(j).wait())

    def store(j, half, value):
        rows = slice(half * 16, half * 16 + 16)
        for number in range(FF_PARTS - EARLY):

            @pl.when(j == number)
            def _():
                first = (EARLY + number) * PART
                inner_sum[rows, first : first + PART] = value

        for piece in range(2):

            @pl.when(j == LATE - 2 + piece)
            def _():
                wo_sum[rows, piece * PART : piece * PART + PART] = value

        @pl.when(j >= LATE)
        def _():
            qkv_sum[j - LATE, rows, :] = value

    def order(beat):
        j = jnp.where(beat <= LATE, beat, jnp.where(beat <= 8, beat - 7 + LATE + 1, LATE + 3))
        return j, ((beat >= 0) & (beat <= LATE)) | (beat == 7) | (beat == 8) | (beat == 11)

    queue = Sums(place, BACK, stage, lambda j: j, bufs, store, ready=ready, order=order)

    @pl.when(step == 0)
    def _():
        for j in range(LATE):
            load(j).start()
        meet(place)
        inner_sum[:, : EARLY * PART] = inner_early[...]

    @pl.when((group == 0) & (inner == 0))
    def _():
        bias[row] = mask_scores(key_ids[0], query_ids[0])

    k_t = k[0].T
    for start in range(0, tokens, 256):
        low_key = 0 if start == 0 else start
        queries = q[0, start : start + 256, :]
        grads = gm[0, start : start + 256, :]
        product = (grads.astype(F32) * mixed[0, start : start + 256, :].astype(F32)).T
        keys, values = k[0, low_key:, :], v[0, low_key:, :]
        parts = []
        dk, dv = 0.0, 0.0
        for head in range(2):
            one_q, one_g = one_head(queries, head), one_head(grads, head)
            delta = jnp.sum(product[head * HD : head * HD + HD, :], axis=0, keepdims=True)
            s = dot_nt(keys, one_q) * SCORE_SCALE + bias[row, low_key:, start : start + 256]
            probs = jnp.exp2(s - lse[0, 0, head : head + 1, start : start + 256])
            dprob = dot_nt(values, one_g)
            score_grad = (probs * (dprob - delta)).astype(BF16)
            dv = dv + dot(probs.astype(BF16), one_g)
            dk = dk + dot(score_grad, one_q)
            parts.append(dot(k_t[head * HD : head * HD + HD, low_key:], score_grad))
        dq = (jnp.concatenate(parts, axis=0) * 0.125).T.astype(BF16)
        dq_out[0, start : start + 256, :] = dq
        if start == 0:
            dk_sum[...] = dk
            dv_sum[...] = dv
        else:
            dk_sum[low_key:, :] += dk
            dv_sum[low_key:, :] += dv
    dk_out[0] = (dk_sum[...] * 0.125).astype(BF16)
    dv_out[0] = dv_sum[...].astype(BF16)
    columns = pl.ds(pl.multiple_of(inner * PAIR, PAIR), PAIR)
    dq_all[row, :, columns] = dq_out[0]
    dk_all[row, :, columns] = dk_out[0]
    dv_all[row, :, columns] = dv_out[0]

    @pl.when((row == 1) & (inner == 1))
    def _():
        span = 2 * PAIR
        pair_slot = jnp.where(group == 3, BACK, jnp.where(group == 2, LATE + 3, LATE + group))
        value_slot = jnp.where(group < 2, LATE + 2, BACK + 1)
        value_half = pl.ds(pl.multiple_of(lax.rem(group, 2) * span, span), span)
        for number, source in enumerate((dq_all, dk_all, dv_all)):
            first = SEGMAX if number == 0 else 0
            grad = dot_tn(xt[0, first:, :], source[0]) + dot_tn(xt[1, first:, :], source[1])
            grad = grad.astype(BF16).reshape(GRID + (32, span))
            if number < 2:
                stage[pair_slot, :, :, :, :, :, number * span : number * span + span] = grad
            else:
                stage[value_slot, :, :, :, :, :, value_half] = grad
        sums[...] = jnp.zeros_like(sums)
        for number, source in enumerate((dq_all, dv_all)):
            added = jnp.sum(source[0].astype(F32), axis=0, keepdims=True) + jnp.sum(
                source[1].astype(F32), axis=0, keepdims=True
            )
            sums[number : number + 1, :] = added

    queue.tick(step)

    @pl.when(step == 15)
    def _():
        saves = [pltpu.make_async_copy(stage.at[BACK + n], tail_out.at[n], load_sem.at[n]) for n in range(2)]
        for save in saves:
            save.start()
        for beat in range(16, 19):
            queue.tick(beat)
        queue.finish()
        for save in saves:
            save.wait()


def attend_back(q, k, v, gm, mixed, lse, key_ids, query_ids, xt, rest, inner_early):
    rows, tokens, width = q.shape
    window = k.shape[1]
    groups = width // (2 * PAIR)
    whole = lambda shape: pl.BlockSpec(shape, lambda g, r, i: (0,) * len(shape), pipeline_mode=pl.Buffered(1))
    kept = lambda shape: pl.BlockSpec(shape, lambda g, r, i: (0,) * len(shape))
    per_pair = lambda n: pl.BlockSpec((1, n, PAIR), lambda g, r, i: (r, 0, g * 2 + i))
    per_row = lambda *s: pl.BlockSpec((1,) + s, lambda g, r, i: (r, 0, 0))
    hbm = pl.BlockSpec(memory_space=pltpu.HBM)
    return pl.pallas_call(
        attend_back_kernel,
        grid=(groups, rows, 2),
        out_shape=[
            jax.ShapeDtypeStruct((rows, tokens, width), BF16),
            jax.ShapeDtypeStruct((rows, window, width), BF16),
            jax.ShapeDtypeStruct((rows, window, width), BF16),
            jax.ShapeDtypeStruct((2,) + PIECE, BF16),
            jax.ShapeDtypeStruct((8, width), F32),
            jax.ShapeDtypeStruct((32, FF_PARTS * PART), F32),
            jax.ShapeDtypeStruct((32, width), F32),
            jax.ShapeDtypeStruct((4, 32, PART), F32),
        ],
        in_specs=[
            per_pair(tokens), per_pair(window), per_pair(window), per_pair(tokens), per_pair(tokens),
            pl.BlockSpec((1, 1, 8, tokens), lambda g, r, i: (r, g * 2 + i, 0, 0)),
            per_row(window, 1), per_row(1, tokens), whole(xt.shape), hbm, whole(inner_early.shape),
        ],
        out_specs=[
            per_pair(tokens), per_pair(window), per_pair(window), hbm,
            pl.BlockSpec((8, 2 * PAIR), lambda g, r, i: (0, g)),
            kept((32, FF_PARTS * PART)), kept((32, width)), kept((4, 32, PART)),
        ],
        scratch_shapes=[
            pltpu.VMEM((rows, window, tokens), F32),
            pltpu.VMEM((rows, tokens, 2 * PAIR), BF16),
            pltpu.VMEM((rows, window, 2 * PAIR), BF16),
            pltpu.VMEM((rows, window, 2 * PAIR), BF16),
            pltpu.VMEM((window, PAIR), F32),
            pltpu.VMEM((window, PAIR), F32),
            pltpu.VMEM((BACK + 2,) + PIECE, BF16),
            pltpu.SemaphoreType.DMA((LATE,)),
        ]
        + sums_buffers(BACK),
        compiler_params=pltpu.CompilerParams(
            collective_id=4, has_side_effects=True, vmem_limit_bytes=VMEM
        ),
        name="attend_back",
    )(q, k, v, gm, mixed, lse, key_ids, query_ids, xt, rest, inner_early)


def shards(vector, base, width):
    count = vector.shape[1]
    device = lax.broadcasted_iota(jnp.int32, (32, count), 0)
    column = lax.broadcasted_iota(jnp.int32, (32, count), 1)
    rows = jnp.where(device == lax.div(column, width), vector, 0.0).astype(BF16)
    lane = lax.broadcasted_iota(jnp.int32, (count, 128), 1)
    place = lax.broadcasted_iota(jnp.int32, (count, 128), 0)
    pick = jnp.where(lane == base + lax.rem(place, width), 1.0, 0.0).astype(BF16)
    return dot(rows, pick)


def finish_kernel(
    tail_in, sums0, sums1, sums2, ib_grad, qkv_early, dq_in, dk_in, dv_in, weights_in, first_in,
    query_sum, key_sum, value_sum, small_sum, gh_out, tail_there,
    dq, dk, dv, weights, gh, tail_here, stage, small_stage, load_sem, tail_sem, *bufs,
):
    place = Place()
    loads = [
        pltpu.make_async_copy(source, target, load_sem.at[number])
        for number, (source, target) in enumerate(
            (
                (tail_in, stage),
                (weights_in.at[pl.ds(0, 3)], weights),
                (dk_in, dk),
                (dv_in, dv),
                (dq_in, dq),
                (first_in, gh),
            )
        )
    ]
    for load in loads:
        load.start()
    meet(place, -1)
    span = 2 * PAIR

    def store(j, half, value):
        rows = slice(half * 16, half * 16 + 16)
        if j == 0:
            query_sum[rows, 3 * span :] = value[:, :span]
            key_sum[rows, 3 * span :] = value[:, span:]
        else:
            value_sum[rows, 2 * span :] = value

    def store_small(j, half, value):
        small_sum[...] = value

    beats = (0, 1, 2, 3, 4)
    queue = Sums(place, 2, stage, lambda j: j, bufs[:6], store, offsets=beats)
    small = Sums(place, 1, small_stage, lambda j: j, bufs[6:], store_small, halves=1, offsets=beats)
    loads[0].wait()
    queue.tick(0)
    packed = []
    vectors = [sums0[0:1], sums0[1:2], sums1[0:1], sums1[1:2], sums1[2:3], sums2[0:1], sums2[1:2], sums2[2:3]]
    for first in (0, 4):
        packed.append(sum(shards(vectors[first + n], n * 32, 32) for n in range(4)))
    inner = [ib_grad[part][:, n * 128 : n * 128 + 128] for part in range(FF_PARTS) for n in range(4)]
    packed.append(jnp.concatenate(inner, axis=0))
    packed = [p.astype(BF16).astype(F32) for p in packed]
    at = lax.broadcasted_iota(jnp.int32, (32, 16, 128), 1)
    block = jnp.zeros((32, 16, 128), F32)
    for number, value in enumerate(packed):
        block = jnp.where(at == number, jnp.broadcast_to(value[:, None, :], (32, 16, 128)), block)
    small_stage[0] = block.astype(BF16).reshape(GRID + (16, 128))

    queue.tick(1)
    small.tick(0)
    tokens, width = dq.shape[1], dq.shape[2]
    for load in loads[1:4]:
        load.wait()
    matrix = [weights.at[m] for m in range(3)]
    send_tail, recv_tail = place.seq > 0, place.seq < 7
    tail = remote(
        tail_here, tail_there, tail_sem.at[0], tail_sem.at[1],
        place.device(z=lax.rem(place.z + 3 + place.c, 4), c=1 - place.c),
    )
    for row in range(2):
        tail_here[row] = (
            dot_nt(dk[row, :SEGMAX, :], matrix[1][...].reshape(width, width))
            + dot_nt(dv[row, :SEGMAX, :], matrix[2][...].reshape(width, width))
        ).astype(BF16)
    pl.when(send_tail)(tail.start)
    queue.tick(2)
    small.tick(1)
    for load in loads[4:]:
        load.wait()

    def own_rows(row):
        for column in range(0, width, 512):
            cols = slice(column, column + 512)
            total = gh[row, :, cols]
            for number, (source, first) in enumerate(((dq, 0), (dk, SEGMAX), (dv, SEGMAX))):
                part = weights[number, column // 512]
                total = total + dot_nt(source[row, first:, :], part.reshape(512, width))
            gh[row, :, cols] = total

    own_rows(0)
    queue.tick(3)
    small.tick(2)
    own_rows(1)
    save = pltpu.make_async_copy(gh, gh_out, load_sem.at[0])
    save.start()
    query_sum[:, : 3 * span] = jnp.concatenate([qkv_early[n, :, :span] for n in (0, 1, 3)], axis=1)
    key_sum[:, : 3 * span] = jnp.concatenate([qkv_early[n, :, span:] for n in (0, 1, 3)], axis=1)
    value_sum[:, : 2 * span] = qkv_early[2]
    for beat in (4, 5):
        queue.tick(beat)
        small.tick(beat - 1)
    queue.finish()
    small.finish()

    @pl.when(place.seq == 7)
    def _():
        tail_there[...] = jnp.zeros_like(tail_there)

    pl.when(recv_tail)(tail.wait_recv)
    pl.when(send_tail)(tail.wait_send)
    save.wait()


def finish(tail_in, sums0, sums1, sums2, ib_grad, qkv_early, dq, dk, dv, weights, grad_first):
    rows, tokens, width = dq.shape
    hbm = pl.BlockSpec(memory_space=pltpu.HBM)
    vmem = pl.BlockSpec(memory_space=pltpu.VMEM)
    return pl.pallas_call(
        finish_kernel,
        out_shape=[
            jax.ShapeDtypeStruct((32, width), F32),
            jax.ShapeDtypeStruct((32, width), F32),
            jax.ShapeDtypeStruct((32, width), F32),
            jax.ShapeDtypeStruct((16, 128), F32),
            jax.ShapeDtypeStruct((rows, tokens, width), F32),
            jax.ShapeDtypeStruct((rows, SEGMAX, width), BF16),
        ],
        in_specs=[hbm] + [vmem] * 5 + [hbm] * 5,
        out_specs=[vmem] * 4 + [hbm, vmem],
        scratch_shapes=[
            pltpu.VMEM(dq.shape, BF16),
            pltpu.VMEM(dk.shape, BF16),
            pltpu.VMEM(dv.shape, BF16),
            pltpu.VMEM((3,) + weights.shape[1:], BF16),
            pltpu.VMEM((rows, tokens, width), F32),
            pltpu.VMEM((rows, SEGMAX, width), BF16),
            pltpu.VMEM((2,) + PIECE, BF16),
            pltpu.VMEM((1,) + GRID + (16, 128), BF16),
            pltpu.SemaphoreType.DMA((6,)),
            pltpu.SemaphoreType.DMA((2,)),
        ]
        + sums_buffers(2)
        + sums_buffers(1, 128, 1),
        compiler_params=pltpu.CompilerParams(
            collective_id=5, has_side_effects=True, vmem_limit_bytes=VMEM
        ),
        name="sum_gradients",
    )(tail_in, sums0, sums1, sums2, ib_grad, qkv_early, dq, dk, dv, weights, grad_first)


def deliver_kernel(gh, returned, *refs):
    count = len(refs) // 2
    sources, out, targets = refs[:count], refs[count], refs[count + 1 :]
    late = lax.rem(pl.program_id(0), 2) == 1
    out[...] = gh[...] + jnp.where(late, returned[...].astype(F32), 0.0)

    @pl.when(pl.program_id(0) == 0)
    def _():
        for source, target in zip(sources, targets):
            target[...] = source[...]


def deliver(gh, returned, arrays):
    rows, tokens, width = gh.shape
    whole = lambda a: pl.BlockSpec(a.shape, lambda s: (0,) * a.ndim)
    block = pl.BlockSpec((1, SEGMAX, width), lambda s: (s // 2, s % 2, 0))
    back = pl.BlockSpec((1, SEGMAX, width), lambda s: (s // 2, 0, 0))
    return pl.pallas_call(
        deliver_kernel,
        grid=(2 * rows,),
        out_shape=[jax.ShapeDtypeStruct(gh.shape, F32)] + [jax.ShapeDtypeStruct(a.shape, a.dtype) for a in arrays],
        in_specs=[block, back] + [whole(a) for a in arrays],
        out_specs=[block] + [whole(a) for a in arrays],
        compiler_params=pltpu.CompilerParams(vmem_limit_bytes=VMEM),
        name="deliver",
    )(gh, returned, *arrays)


def local(
    hidden_in, segment_ids, query_weight, query_bias, key_weight, value_weight, value_bias, output_weight,
    output_bias, first_gain, first_shift, inner_weight, inner_bias, outer_weight, outer_bias, second_gain,
    second_shift, cotangent,
):
    rows, tokens, width = hidden_in.shape
    window = tokens + SEGMAX
    vectors = (query_bias, value_bias, output_bias, first_gain, first_shift, outer_bias, second_gain, second_shift, inner_bias)
    padded = jnp.concatenate([jnp.full((rows, SEGMAX), -1, jnp.int32), segment_ids], axis=1)
    key_ids = lax.dynamic_slice_in_dim(padded, lax.axis_index("seq") * tokens, window, 1)
    query_ids = key_ids[:, None, SEGMAX:]
    key_ids = key_ids[:, :, None]
    q, k, v, xt, weights, mixed, unit, low, inner, outer, lse, scale, vec, inner_b = encode(
        hidden_in, key_ids, query_ids, vectors, query_weight, key_weight, value_weight, output_weight,
        inner_weight, outer_weight,
    )
    flat = lambda a: a.reshape(rows * tokens, a.shape[-1])
    active, slope, layer_out, og, grad_second, sums2 = feed_forward(
        flat(low), flat(unit), flat(cotangent), inner, inner_b, outer, vec
    )
    outer_sum, inner_early, rest, ib_grad, grad_first, gm, sums1 = feed_backward(
        active, slope, og, flat(low), inner, outer, grad_second, flat(unit), flat(scale), flat(mixed), weights, vec
    )
    dq, dk, dv, tail, sums0, inner_sum, wo_sum, qkv_early = attend_back(
        q, k, v, gm.reshape(rows, tokens, width), mixed, lse, key_ids, query_ids, xt, rest, inner_early
    )
    query_sum, key_sum, value_sum, small_sum, grad_hidden, returned = finish(
        tail, sums0, sums1, sums2, ib_grad, qkv_early, dq, dk, dv, weights, grad_first.reshape(rows, tokens, width)
    )
    grad_hidden, query_sum, key_sum, value_sum, wo_sum, inner_sum, outer_sum, small_sum = deliver(
        grad_hidden, returned, (query_sum, key_sum, value_sum, wo_sum, inner_sum, outer_sum, small_sum)
    )
    vector = small_sum[:2].reshape(8, 32)
    return (
        layer_out.reshape(rows, tokens, width),
        grad_hidden,
        query_sum,
        vector[0],
        key_sum,
        value_sum,
        vector[1],
        wo_sum,
        vector[2],
        vector[3],
        vector[4],
        inner_sum,
        small_sum[2],
        outer_sum,
        vector[5],
        vector[6],
        vector[7],
    )


def solution(mesh):
    in_specs = (
        P("dp", "seq", None),
        P("dp", None),
        P(("dp", "seq"), None),
        P(("dp", "seq")),
        P(("dp", "seq"), None),
        P(("dp", "seq"), None),
        P(("dp", "seq")),
        P(("dp", "seq"), None),
        P(("dp", "seq")),
        P(("dp", "seq")),
        P(("dp", "seq")),
        P(("dp", "seq"), None),
        P(("dp", "seq")),
        P(("dp", "seq"), None),
        P(("dp", "seq")),
        P(("dp", "seq")),
        P(("dp", "seq")),
        P("dp", "seq", None),
    )
    out_specs = (
        P("dp", "seq", None),
        P("dp", "seq", None),
        P(("dp", "seq"), None),
        P(("dp", "seq")),
        P(("dp", "seq"), None),
        P(("dp", "seq"), None),
        P(("dp", "seq")),
        P(("dp", "seq"), None),
        P(("dp", "seq")),
        P(("dp", "seq")),
        P(("dp", "seq")),
        P(("dp", "seq"), None),
        P(("dp", "seq")),
        P(("dp", "seq"), None),
        P(("dp", "seq")),
        P(("dp", "seq")),
        P(("dp", "seq")),
    )
    fits = dict(mesh.shape) == {"dp": 4, "seq": 8}
    body = local if fits else plain
    return jax.shard_map(body, mesh=mesh, in_specs=in_specs, out_specs=out_specs, check_vma=False)
```

```python
import functools

import jax
import jax.numpy as jnp
from jax import lax
from jax.experimental import pallas as pl
from jax.experimental.pallas import tpu as pltpu
from jax.sharding import PartitionSpec as P

HD = 64
SEGMAX = 256
EPS = 1e-05
LOG2E = 1.4426950408889634
SCORE_SCALE = 0.125 * LOG2E
HIDDEN = -1e30
PAIR = 2 * HD
MESH = pl.DeviceIdType.MESH
BF16 = jnp.bfloat16
F32 = jnp.float32
VMEM = 64 * 2**20


group_heads = 4


def passed_along(block, axis, distance):
    devices = range(lax.axis_size(axis))
    route = [(i - distance, i) for i in devices if i - distance in devices]
    return lax.ppermute(block, axis, route)


def normalize(hidden, gain, shift):
    center = hidden - jnp.mean(hidden, axis=-1, keepdims=True)
    spread = jnp.mean(center * center, axis=-1, keepdims=True)
    return center * lax.rsqrt(spread + 1e-05) * gain + shift


def contract_rows(left, right):
    return lax.dot_general(
        left, right, (((0,), (0,)), ((), ())), preferred_element_type=jnp.float32
    )


def times_transposed(left, right):
    return lax.dot_general(
        left, right, (((1,), (1,)), ((), ())), preferred_element_type=jnp.float32
    )


def column_sum(values):
    return jnp.sum(values.astype(jnp.float32), axis=0)


def plain(
    hidden_in,
    segment_ids,
    query_weight,
    query_bias,
    key_weight,
    value_weight,
    value_bias,
    output_weight,
    output_bias,
    first_gain,
    first_shift,
    inner_weight,
    inner_bias,
    outer_weight,
    outer_bias,
    second_gain,
    second_shift,
    cotangent,
):
    rows_here, tokens, width = hidden_in.shape
    window = tokens + SEGMAX
    span = group_heads * HD
    groups = width // span
    items = jnp.arange(rows_here * groups, dtype=jnp.int32)
    (
        query_matrix,
        query_offset,
        key_matrix,
        value_matrix,
        value_offset,
        output_matrix,
        output_offset,
        first_scale,
        first_offset,
    ) = (
        lax.all_gather(query_weight, ("dp", "seq"), axis=0, tiled=True),
        lax.all_gather(query_bias, ("dp", "seq"), axis=0, tiled=True),
        lax.all_gather(key_weight, ("dp", "seq"), axis=0, tiled=True),
        lax.all_gather(value_weight, ("dp", "seq"), axis=0, tiled=True),
        lax.all_gather(value_bias, ("dp", "seq"), axis=0, tiled=True),
        lax.all_gather(output_weight, ("dp", "seq"), axis=0, tiled=True),
        lax.all_gather(output_bias, ("dp", "seq"), axis=0, tiled=True),
        lax.all_gather(first_gain, ("dp", "seq"), axis=0, tiled=True),
        lax.all_gather(first_shift, ("dp", "seq"), axis=0, tiled=True),
    )
    flat = hidden_in.reshape(rows_here * tokens, width)
    offset = lax.axis_index("seq") * tokens
    padded_ids = jnp.concatenate(
        [jnp.full((rows_here, SEGMAX), -1, jnp.int32), segment_ids], axis=1
    )
    key_ids = lax.dynamic_slice_in_dim(padded_ids, offset, window, 1)
    query_ids = key_ids[:, SEGMAX:]
    diagonal = jnp.arange(window)[None, :] == jnp.arange(tokens)[:, None] + SEGMAX
    visible = (query_ids[:, :, None] == key_ids[:, None, :]) & (
        query_ids[:, :, None] > 0
    ) | diagonal[None]
    queries = (
        (
            jnp.dot(flat, query_matrix, preferred_element_type=jnp.float32)
            + query_offset.astype(jnp.float32)
        )
        .astype(jnp.bfloat16)
        .reshape(rows_here, tokens, width)
    )
    keys_own = (
        jnp.dot(flat, key_matrix, preferred_element_type=jnp.float32)
        .astype(jnp.bfloat16)
        .reshape(rows_here, tokens, width)
    )
    values_own = (
        (
            jnp.dot(flat, value_matrix, preferred_element_type=jnp.float32)
            + value_offset.astype(jnp.float32)
        )
        .astype(jnp.bfloat16)
        .reshape(rows_here, tokens, width)
    )
    tails = passed_along(
        (keys_own[:, tokens - SEGMAX :], values_own[:, tokens - SEGMAX :]), "seq", 1
    )
    keys_all = jnp.concatenate([tails[0], keys_own], axis=1)
    values_all = jnp.concatenate([tails[1], values_own], axis=1)

    def pieces(item):
        row = item // groups
        column = item % groups * span
        query_part = lax.dynamic_slice(queries, (row, 0, column), (1, tokens, span))[0].reshape(
            tokens, group_heads, HD
        )
        key_part = lax.dynamic_slice(keys_all, (row, 0, column), (1, window, span))[0].reshape(
            window, group_heads, HD
        )
        value_part = lax.dynamic_slice(values_all, (row, 0, column), (1, window, span))[0].reshape(
            window, group_heads, HD
        )
        mask_row = lax.dynamic_index_in_dim(visible, row, 0, keepdims=False)
        scores = (
            jnp.einsum("qhd,khd->hqk", query_part, key_part, preferred_element_type=jnp.float32)
            * 0.125
        )
        scores = jnp.where(mask_row[None], scores, -1e30)
        return (row, column, query_part, key_part, value_part, scores)

    def attend(item):
        row, column, query_part, key_part, value_part, scores = pieces(item)
        highest = jnp.max(scores, axis=-1, keepdims=True)
        expo = jnp.exp(scores - highest)
        total = jnp.sum(expo, axis=-1, keepdims=True)
        probs = (expo / total).astype(jnp.bfloat16)
        mixed_part = jnp.einsum(
            "hqk,khd->qhd", probs, value_part, preferred_element_type=jnp.float32
        )
        return (
            mixed_part.astype(jnp.bfloat16).reshape(tokens, span),
            highest[..., 0] + jnp.log(total[..., 0]),
        )

    mixed_parts, logsums = lax.map(attend, items)
    mixed = (
        mixed_parts.reshape(rows_here, groups, tokens, span)
        .transpose(0, 2, 1, 3)
        .reshape(rows_here * tokens, width)
    )
    first_sum = (
        flat.astype(jnp.float32)
        + jnp.dot(mixed, output_matrix, preferred_element_type=jnp.float32)
        + output_offset.astype(jnp.float32)
    )
    normed = normalize(first_sum, first_scale.astype(jnp.float32), first_offset.astype(jnp.float32))
    normed_low = normed.astype(jnp.bfloat16)
    inner_matrix, inner_offset, outer_matrix, outer_offset, second_scale, second_offset = (
        lax.all_gather(inner_weight, ("dp", "seq"), axis=0, tiled=True),
        lax.all_gather(inner_bias, ("dp", "seq"), axis=0, tiled=True),
        lax.all_gather(outer_weight, ("dp", "seq"), axis=0, tiled=True),
        lax.all_gather(outer_bias, ("dp", "seq"), axis=0, tiled=True),
        lax.all_gather(second_gain, ("dp", "seq"), axis=0, tiled=True),
        lax.all_gather(second_shift, ("dp", "seq"), axis=0, tiled=True),
    )
    inner = jnp.dot(
        normed_low, inner_matrix, preferred_element_type=jnp.float32
    ) + inner_offset.astype(jnp.float32)
    active_low = jax.nn.gelu(inner, approximate=False).astype(jnp.bfloat16)
    second_sum = (
        normed
        + jnp.dot(active_low, outer_matrix, preferred_element_type=jnp.float32)
        + outer_offset.astype(jnp.float32)
    )
    layer_out = normalize(
        second_sum, second_scale.astype(jnp.float32), second_offset.astype(jnp.float32)
    )
    layer_out = layer_out.astype(jnp.bfloat16).reshape(rows_here, tokens, width)
    inner_matrix, inner_offset, outer_matrix, outer_offset, second_scale, second_offset = (
        lax.all_gather(inner_weight, ("dp", "seq"), axis=0, tiled=True),
        lax.all_gather(inner_bias, ("dp", "seq"), axis=0, tiled=True),
        lax.all_gather(outer_weight, ("dp", "seq"), axis=0, tiled=True),
        lax.all_gather(outer_bias, ("dp", "seq"), axis=0, tiled=True),
        lax.all_gather(second_gain, ("dp", "seq"), axis=0, tiled=True),
        lax.all_gather(second_shift, ("dp", "seq"), axis=0, tiled=True),
    )
    upstream = cotangent.reshape(rows_here * tokens, width).astype(jnp.float32)
    _, pull_second = jax.vjp(
        normalize, second_sum, second_scale.astype(jnp.float32), second_offset.astype(jnp.float32)
    )
    grad_second, second_gain_grad, second_shift_grad = pull_second(upstream)
    outer_grad = grad_second.astype(jnp.bfloat16)
    outer_weight_grad = contract_rows(active_low, outer_grad)
    outer_bias_grad = column_sum(outer_grad)
    _, pull_gelu = jax.vjp(lambda value: jax.nn.gelu(value, approximate=False), inner)
    (inner_grad_full,) = pull_gelu(times_transposed(outer_grad, outer_matrix))
    inner_grad = inner_grad_full.astype(jnp.bfloat16)
    inner_weight_grad = contract_rows(normed_low, inner_grad)
    inner_bias_grad = column_sum(inner_grad)
    grad_normed = grad_second + times_transposed(inner_grad, inner_matrix)
    (
        query_matrix,
        query_offset,
        key_matrix,
        value_matrix,
        value_offset,
        output_matrix,
        output_offset,
        first_scale,
        first_offset,
    ) = (
        lax.all_gather(query_weight, ("dp", "seq"), axis=0, tiled=True),
        lax.all_gather(query_bias, ("dp", "seq"), axis=0, tiled=True),
        lax.all_gather(key_weight, ("dp", "seq"), axis=0, tiled=True),
        lax.all_gather(value_weight, ("dp", "seq"), axis=0, tiled=True),
        lax.all_gather(value_bias, ("dp", "seq"), axis=0, tiled=True),
        lax.all_gather(output_weight, ("dp", "seq"), axis=0, tiled=True),
        lax.all_gather(output_bias, ("dp", "seq"), axis=0, tiled=True),
        lax.all_gather(first_gain, ("dp", "seq"), axis=0, tiled=True),
        lax.all_gather(first_shift, ("dp", "seq"), axis=0, tiled=True),
    )
    _, pull_first = jax.vjp(
        normalize, first_sum, first_scale.astype(jnp.float32), first_offset.astype(jnp.float32)
    )
    grad_first, first_gain_grad, first_shift_grad = pull_first(grad_normed)
    attn_grad = grad_first.astype(jnp.bfloat16)
    output_weight_grad = contract_rows(mixed, attn_grad)
    output_bias_grad = column_sum(attn_grad)
    grad_mixed = (
        times_transposed(attn_grad, output_matrix)
        .astype(jnp.bfloat16)
        .reshape(rows_here, tokens, width)
    )

    def attend_back(item):
        row, column, query_part, key_part, value_part, scores = pieces(item)
        logsum = lax.dynamic_index_in_dim(logsums, item, 0, keepdims=False)
        grad_part = lax.dynamic_slice(grad_mixed, (row, 0, column), (1, tokens, span))[0].reshape(
            tokens, group_heads, HD
        )
        probs = jnp.exp(scores - logsum[..., None])
        dprob = jnp.einsum(
            "qhd,khd->hqk", grad_part, value_part, preferred_element_type=jnp.float32
        )
        delta = jnp.sum(probs * dprob, axis=-1, keepdims=True)
        score_grad = (probs * (dprob - delta)).astype(jnp.bfloat16)
        query_part_grad = (
            jnp.einsum("hqk,khd->qhd", score_grad, key_part, preferred_element_type=jnp.float32)
            * 0.125
        )
        key_part_grad = (
            jnp.einsum("hqk,qhd->khd", score_grad, query_part, preferred_element_type=jnp.float32)
            * 0.125
        )
        value_part_grad = jnp.einsum(
            "hqk,qhd->khd",
            probs.astype(jnp.bfloat16),
            grad_part,
            preferred_element_type=jnp.float32,
        )
        return (
            query_part_grad.reshape(tokens, span),
            key_part_grad.reshape(window, span),
            value_part_grad.reshape(window, span),
        )

    query_parts, key_parts, value_parts = lax.map(attend_back, items)
    query_full = (
        query_parts.reshape(rows_here, groups, tokens, span)
        .transpose(0, 2, 1, 3)
        .reshape(rows_here * tokens, width)
    )
    key_window = (
        key_parts.reshape(rows_here, groups, window, span)
        .transpose(0, 2, 1, 3)
        .reshape(rows_here, window, width)
    )
    value_window = (
        value_parts.reshape(rows_here, groups, window, span)
        .transpose(0, 2, 1, 3)
        .reshape(rows_here, window, width)
    )
    returned = (
        passed_along(key_window[:, :SEGMAX].astype(jnp.bfloat16), "seq", -1).astype(jnp.float32),
        passed_along(value_window[:, :SEGMAX].astype(jnp.bfloat16), "seq", -1).astype(jnp.float32),
    )
    key_own = key_window[:, SEGMAX:]
    value_own = value_window[:, SEGMAX:]
    key_total = jnp.concatenate(
        [key_own[:, : tokens - SEGMAX], key_own[:, tokens - SEGMAX :] + returned[0]], axis=1
    )
    value_total = jnp.concatenate(
        [value_own[:, : tokens - SEGMAX], value_own[:, tokens - SEGMAX :] + returned[1]], axis=1
    )
    query_grad = query_full.astype(jnp.bfloat16)
    key_grad = key_total.reshape(rows_here * tokens, width).astype(jnp.bfloat16)
    value_grad = value_total.reshape(rows_here * tokens, width).astype(jnp.bfloat16)
    query_weight_grad = contract_rows(flat, query_grad)
    query_bias_grad = column_sum(query_grad)
    key_weight_grad = contract_rows(flat, key_grad)
    value_weight_grad = contract_rows(flat, value_grad)
    value_bias_grad = column_sum(value_grad)
    grad_hidden = (
        grad_first
        + times_transposed(query_grad, query_matrix)
        + times_transposed(key_grad, key_matrix)
        + times_transposed(value_grad, value_matrix)
    ).reshape(rows_here, tokens, width)
    shards = (
        lax.psum_scatter(query_weight_grad, ("dp", "seq"), scatter_dimension=0, tiled=True),
        lax.psum_scatter(query_bias_grad, ("dp", "seq"), scatter_dimension=0, tiled=True),
        lax.psum_scatter(key_weight_grad, ("dp", "seq"), scatter_dimension=0, tiled=True),
        lax.psum_scatter(value_weight_grad, ("dp", "seq"), scatter_dimension=0, tiled=True),
        lax.psum_scatter(value_bias_grad, ("dp", "seq"), scatter_dimension=0, tiled=True),
        lax.psum_scatter(output_weight_grad, ("dp", "seq"), scatter_dimension=0, tiled=True),
        lax.psum_scatter(output_bias_grad, ("dp", "seq"), scatter_dimension=0, tiled=True),
        lax.psum_scatter(first_gain_grad, ("dp", "seq"), scatter_dimension=0, tiled=True),
        lax.psum_scatter(first_shift_grad, ("dp", "seq"), scatter_dimension=0, tiled=True),
        lax.psum_scatter(inner_weight_grad, ("dp", "seq"), scatter_dimension=0, tiled=True),
        lax.psum_scatter(inner_bias_grad, ("dp", "seq"), scatter_dimension=0, tiled=True),
        lax.psum_scatter(outer_weight_grad, ("dp", "seq"), scatter_dimension=0, tiled=True),
        lax.psum_scatter(outer_bias_grad, ("dp", "seq"), scatter_dimension=0, tiled=True),
        lax.psum_scatter(second_gain_grad, ("dp", "seq"), scatter_dimension=0, tiled=True),
        lax.psum_scatter(second_shift_grad, ("dp", "seq"), scatter_dimension=0, tiled=True),
    )
    return (
        layer_out,
        grad_hidden,
        shards[0],
        shards[1],
        shards[2],
        shards[3],
        shards[4],
        shards[5],
        shards[6],
        shards[7],
        shards[8],
        shards[9],
        shards[10],
        shards[11],
        shards[12],
        shards[13],
        shards[14],
    )


GRID = (2, 2, 4, 2)
FF_PARTS = 8
PART = 512
EARLY = 5
PIECE = GRID + (32, PART)


class Place:
    def __init__(self):
        dp = lax.axis_index("dp")
        seq = lax.axis_index("seq")
        self.x = lax.rem(dp, 2)
        self.y = lax.div(dp, 2)
        self.z = lax.div(seq, 2)
        self.c = lax.rem(seq, 2)
        self.seq = seq

    def device(self, x=None, y=None, z=None, c=None):
        x = self.x if x is None else x
        y = self.y if y is None else y
        z = self.z if z is None else z
        c = self.c if c is None else c
        return (y * 2 + x, z * 2 + c)

    def peer(self, dim):
        if dim == "x":
            return self.device(x=1 - self.x)
        if dim == "y":
            return self.device(y=1 - self.y)
        if dim == "c":
            return self.device(c=1 - self.c)
        return self.device(z=lax.rem(self.z + dim, 4))


def signal(semaphore, device):
    pl.semaphore_signal(semaphore, inc=1, device_id=device, device_id_type=MESH)


def meet(place, along=0):
    barrier = pltpu.get_barrier_semaphore()
    for dim in ("x", "y", "c", 1, 2, 3):
        signal(barrier, place.peer(dim))
    extra = 0
    if along:
        up = (place.c == 1) & (place.z < 3)
        down = (place.c == 0) & (place.z > 0)
        receives, sends = (down, up) if along > 0 else (up, down)
        other = lax.rem(place.z + (3 if along > 0 else 1), 4)

        @pl.when(receives)
        def _():
            signal(barrier, place.device(z=other, c=1 - place.c))

        extra = sends.astype(jnp.int32)
    pl.semaphore_wait(barrier, 6 + extra)


def remote(src, dst, send, recv, device):
    return pltpu.make_async_remote_copy(
        src_ref=src, dst_ref=dst, send_sem=send, recv_sem=recv, device_id=device, device_id_type=MESH
    )


class Gather:
    def __init__(self, place, order, source, target, send, recv):
        held = {"x": False, "y": False, "z": False}

        def region():
            index = []
            for name, size in (("y", 2), ("x", 2), ("z", 4)):
                index.append(pl.ds(0, size) if held[name] else pl.ds(getattr(place, name), 1))
            return target(index[0], index[1], index[2], pl.ds(place.c, 1))

        self.own = pltpu.make_async_copy(source, region(), recv.at[6])
        self.phases = []
        for number, dim in enumerate(order):
            here = region()
            copies = []
            for partner in (1, 2, 3) if dim == "z" else (dim,):
                slot = partner - 1 if dim == "z" else {"x": 3, "y": 4}[dim]
                copies.append(
                    remote(
                        source if number == 0 else here,
                        here,
                        send.at[slot],
                        recv.at[slot],
                        place.peer(partner),
                    )
                )
            self.phases.append(copies)
            held[dim] = True
        here = region()
        self.phases.append([remote(here, here, send.at[5], recv.at[5], place.peer("c"))])

    def start(self, phase):
        if phase == 0:
            self.own.start()
        for copy in self.phases[phase]:
            copy.start()

    def arrive(self, phase):
        for copy in self.phases[phase]:
            copy.wait_recv()
        if phase == 0:
            self.own.wait()

    def step(self, phase):
        if phase > 0:
            self.arrive(phase - 1)
        if phase < 4:
            self.start(phase)

    def finish(self):
        for copies in self.phases:
            for copy in copies:
                copy.wait_send()


class Sums:
    def __init__(self, place, count, stage, slot, bufs, store, halves=2, ready=None, order=None, offsets=(0, 1, 3, 5, 7)):
        self.place, self.count, self.stage, self.slot = place, count, stage, slot
        self.order, self.offsets = order, offsets
        self.r0, self.r1, self.r2, self.r3, self.send, self.recv = bufs
        self.store, self.halves, self.ready = store, halves, ready

    def copies(self, j, half, phase):
        place = self.place
        send, recv = self.send.at[j, half], self.recv.at[j, half]
        r0, r1, r2, r3 = (ref.at[j, half] for ref in (self.r0, self.r1, self.r2, self.r3))
        if phase == 0:
            source = self.stage.at[self.slot(j), :, :, :, 1 - place.c, pl.ds(16 * half, 16)]
            return [remote(source, r0, send.at[0], recv.at[0], place.peer("c"))]
        if phase == 1:
            source, dim = (r0.at[1 - place.y], "y") if half == 0 else (r0.at[:, 1 - place.x], "x")
            return [remote(source, r1, send.at[1], recv.at[1], place.peer(dim))]
        if phase == 2:
            source, dim = (r1.at[1 - place.x], "x") if half == 0 else (r1.at[1 - place.y], "y")
            return [remote(source, r2, send.at[2], recv.at[2], place.peer(dim))]
        return [
            remote(r2.at[lax.rem(place.z + k, 4)], r3.at[k - 1], send.at[2 + k], recv.at[2 + k], place.peer(k))
            for k in (1, 2, 3)
        ]

    def step(self, j, phase):
        place = self.place
        if phase == 0 and self.ready is not None:
            self.ready(j)
        for half in range(self.halves):
            if phase > 0:
                for copy in self.copies(j, half, phase - 1):
                    copy.wait_recv()
            if phase == 1:
                self.copies(j, half, 0)[0].wait_send()
                mine = self.stage[self.slot(j), :, :, :, place.c, 16 * half : 16 * half + 16, :]
                self.r0[j, half] = self.r0[j, half] + mine
            elif phase == 2:
                mine = self.r0[j, half, place.y] if half == 0 else self.r0[j, half, :, place.x]
                self.r1[j, half] = self.r1[j, half] + mine
            elif phase == 3:
                mine = self.r1[j, half, place.x] if half == 0 else self.r1[j, half, place.y]
                self.r2[j, half] = self.r2[j, half] + mine
            elif phase == 4:
                total = self.r2[j, half, place.z].astype(F32)
                for k in range(3):
                    total = total + self.r3[j, half, k].astype(F32)
                self.store(j, half, total)
            if phase < 4:
                for copy in self.copies(j, half, phase):
                    copy.start()

    def tick(self, time):
        for phase, offset in enumerate(self.offsets):
            j = time - offset
            valid = (j >= 0) & (j < self.count)
            if self.order is not None:
                j, valid = self.order(j)
            if isinstance(valid, bool):
                if valid:
                    self.step(j, phase)
            else:
                pl.when(valid)(functools.partial(self.step, j, phase))

    def finish(self):
        def body(j, carry):
            for half in range(self.halves):
                for phase in (1, 2, 3):
                    for copy in self.copies(j, half, phase):
                        copy.wait_send()
            return carry

        lax.fori_loop(0, self.count, body, 0)


def sums_buffers(count, columns=512, halves=2):
    block = (16, columns)
    return [
        pltpu.VMEM((count, halves, 2, 2, 4) + block, BF16),
        pltpu.VMEM((count, halves, 2, 4) + block, BF16),
        pltpu.VMEM((count, halves, 4) + block, BF16),
        pltpu.VMEM((count, halves, 3) + block, BF16),
        pltpu.SemaphoreType.DMA((count, halves, 6)),
        pltpu.SemaphoreType.DMA((count, halves, 6)),
    ]


def advance(slots, time, offsets):
    for phase, offset in enumerate(offsets):
        number = time - offset
        if 0 <= number < len(slots):
            for part in slots[number]:
                part.step(phase)


def dot(left, right):
    return jnp.dot(left, right, preferred_element_type=F32)


def dot_nt(left, right):
    return lax.dot_general(left, right, (((1,), (1,)), ((), ())), preferred_element_type=F32)


def dot_tn(left, right):
    return lax.dot_general(left, right, (((0,), (0,)), ((), ())), preferred_element_type=F32)


def spread(blocks, row, base, shift, count):
    at = lax.broadcasted_iota(jnp.int32, (32, 16, 128), 1)
    rows = jnp.sum(jnp.where(at == row, blocks.reshape(32, 16, 128).astype(F32), 0.0), axis=1)
    lane = lax.broadcasted_iota(jnp.int32, (128, count), 0)
    column = lax.broadcasted_iota(jnp.int32, (128, count), 1)
    pick = jnp.where(lane == base + (column & (2**shift - 1)), 1.0, 0.0).astype(BF16)
    wide = dot(rows.astype(BF16), pick)
    device = lax.broadcasted_iota(jnp.int32, (32, count), 0)
    column = lax.broadcasted_iota(jnp.int32, (32, count), 1)
    return jnp.sum(jnp.where(device == column >> shift, wide, 0.0), axis=0, keepdims=True)


BEATS = (0, 1, 2, 3, 4)
ITEM_BEATS = {0: 11, 3: 12, 7: 13, 10: 14, 14: 15}
PART_BEATS = {1: 16, 4: 17, 7: 18}
EVEN = (("zxy", 4), ("zyx", 4))
MIXED = (("zxy", 3), ("zyx", 3), ("xzy", 1), ("yzx", 1))


def gather_slots(place, source, target, pieces, orders, send, recv):
    slots = []
    number = 0
    for rows, first, columns in pieces:
        slot = []
        for order, eighths in orders:
            cols = pl.ds(first, columns * eighths // 8)
            first += columns * eighths // 8
            slot.append(
                Gather(
                    place,
                    order,
                    source.at[:, :, :, :, rows, cols],
                    lambda y, x, z, c, rows=rows, cols=cols: target.at[y, x, z, c, rows, cols],
                    send.at[number],
                    recv.at[number],
                )
            )
            number += 1
        slots.append(slot)
    return slots


def finish_slots(slots):
    for slot in slots:
        for part in slot:
            part.finish()


def mask_scores(key_ids, query_ids):
    keys, queries = key_ids.shape[0], query_ids.shape[1]
    key_at = lax.broadcasted_iota(jnp.int32, (keys, queries), 0)
    query_at = lax.broadcasted_iota(jnp.int32, (keys, queries), 1)
    visible = ((key_ids == query_ids) & (query_ids > 0)) | (key_at == query_at + SEGMAX)
    return jnp.where(visible, 0.0, HIDDEN).astype(F32)


BLOCK = 128


def key_ranges(tokens):
    window = tokens + SEGMAX
    return [(start, min(start + BLOCK + 2 * SEGMAX, window)) for start in range(0, tokens, BLOCK)]


def one_head(block, head):
    lane = lax.broadcasted_iota(jnp.int32, block.shape, 1)
    return jnp.where((lane >= HD) == bool(head), block, jnp.zeros_like(block))


def both_heads(block):
    return jnp.concatenate([one_head(block, 0), one_head(block, 1)], axis=0)


def own_heads(value):
    return jnp.concatenate([value[:HD, :BLOCK], value[HD:, BLOCK:]], axis=0)


def layer_norm(value):
    center = value - jnp.mean(value, axis=-1, keepdims=True)
    scale = lax.rsqrt(jnp.mean(center * center, axis=-1, keepdims=True) + EPS)
    return center * scale, scale


def layer_norm_back(grad, unit, scale):
    return scale * (
        grad
        - jnp.mean(grad, axis=-1, keepdims=True)
        - unit * jnp.mean(grad * unit, axis=-1, keepdims=True)
    )


def gelu_both(value):
    bell = jnp.exp2(value * value * (-0.5 * LOG2E)) * 0.3989422804014327
    below = 0.5 + 0.5 * lax.erf(value * 0.7071067811865476)
    return value * below, below + value * bell


def encode_kernel(
    x_in, key_ids, query_ids, v0, v1, v2, v3, v4, v5, v6, v7, v8, wq_in, wk_in, wv_in, wo_in, inner_in, outer_in,
    q_out, k_out, v_out, xt_out, w_out, mixed_out, unit_out, low_out, inner_out, outer_out, active_out, slope_out,
    lse, scale, vec,
    weights, small, smalls, xt, q, k, v, mixed, unit, low, bias, inner, own_weights, inner_own, outer_own, inner_b, active, slope,
    send, recv, tail_sem, local_sem, part_sem, weight_sem,
):
    place = Place()
    tokens, width = x_in.shape[1], x_in.shape[2]
    own_x = pltpu.make_async_copy(x_in, xt.at[:, pl.ds(SEGMAX, tokens)], local_sem.at[0])
    own_x.start()
    own_ff = [
        pltpu.make_async_copy(inner_in, inner_own, local_sem.at[22]),
        pltpu.make_async_copy(outer_in, outer_own, local_sem.at[23]),
    ]
    own_w = [
        pltpu.make_async_copy(source, own_weights.at[number], local_sem.at[18 + number])
        for number, source in enumerate((wq_in, wk_in, wv_in, wo_in))
    ]
    for copy in own_w + own_ff:
        copy.start()
    at = lax.broadcasted_iota(jnp.int32, (16, 128), 0)
    block = jnp.zeros((16, 128), F32)
    for number, vector in enumerate((v0, v1, v2, v3, v4, v5, v6, v7, v8)):
        size = vector.shape[1]
        base, row = (number % 4 * 32, number // 4) if number < 8 else (0, 2)
        lane = lax.broadcasted_iota(jnp.int32, (size, 128), 1)
        index = lax.broadcasted_iota(jnp.int32, (size, 128), 0)
        pick = jnp.where(lane == base + index, 1.0, 0.0).astype(BF16)
        wide = dot(jnp.broadcast_to(vector[...], (16, size)), pick)
        block = block + jnp.where(at == row, wide, 0.0)
    small[0, 0, 0, 0] = block.astype(BF16)
    meet(place, 1)
    half = width // 2
    slots = []
    vectors = Gather(place, "zxy", small, lambda y, x, z, c: smalls.at[y, x, z, c], send.at[56], recv.at[56])
    everything, used = slice(None), 0

    def add(source, target, pieces, orders):
        nonlocal used, slots
        sems = pl.ds(used, len(orders) * len(pieces))
        used += len(orders) * len(pieces)
        slots += gather_slots(place, source, target, pieces, orders, send.at[sems], recv.at[sems])

    for copy in own_w:
        copy.wait()
    for matrix in range(3):
        add(own_weights.at[matrix], w_out.at[matrix], [(everything, part * half, half) for part in range(2)], EVEN)
    add(own_weights.at[3], w_out.at[3], [(everything, 0, width)], MIXED)
    slots[0].append(vectors)
    add(inner_own, inner_out, [(everything, part * width, width) for part in range(4)], MIXED)
    add(outer_own, outer_out, [(pl.ds(part * 32, 32), 0, width) for part in range(4)], MIXED)

    tails = []
    for row in range(2):
        for start in range(0, SEGMAX, 128):
            tails.append(
                remote(
                    x_in.at[row, pl.ds(tokens - SEGMAX + start, 128)],
                    xt.at[row, pl.ds(start, 128)],
                    tail_sem.at[0, len(tails)],
                    tail_sem.at[1, len(tails)],
                    place.device(z=lax.rem(place.z + place.c, 4), c=1 - place.c),
                )
            )
    has_next, has_last = place.seq < 7, place.seq > 0
    saves = []

    def save(source, target):
        copy = pltpu.make_async_copy(source, target, local_sem.at[1 + len(saves)])
        copy.start()
        saves.append(copy)

    def project(matrix, part):
        target, bias_row, first = ((q, 0, SEGMAX), (k, None, 0), (v, 1, 0))[matrix]
        columns = slice(part * half, part * half + half)
        right = weights[matrix, :, :, :, :, :, columns].reshape(width, half)
        for row in range(2):
            out = dot(xt[row, first:, :], right)
            if bias_row is not None:
                out = out + vec[bias_row : bias_row + 1, columns]
            target[row, :, columns] = out.astype(BF16)

    weight_loads = []
    for matrix in range(4):
        for start in range(0, width, half):
            columns = pl.ds(start, half) if matrix < 3 else pl.ds(0, width)
            if matrix < 3 or start == 0:
                weight_loads.append(
                    pltpu.make_async_copy(
                        w_out.at[matrix, :, :, :, :, :, columns],
                        weights.at[matrix, :, :, :, :, :, columns],
                        weight_sem.at[len(weight_loads)],
                    )
                )
    last = BEATS[-1]
    for time in range(last + 7):
        if 3 <= time <= 6:
            pl.when(has_next)(tails[time - 3].start)
        if time == 3:
            xt_zero = jnp.zeros((2, SEGMAX, width), BF16)

            @pl.when(place.seq == 0)
            def _():
                xt[:, :SEGMAX, :] = xt_zero

            own_x.wait()
            for copy in own_ff:
                copy.wait()
        advance(slots, time, BEATS)
        done = time - last
        if done == 0:
            for vector in range(8):
                vec[vector : vector + 1, :] = spread(smalls[...], vector // 4, vector % 4 * 32, 5, width)
            vec[8:, :] = jnp.zeros((8, width), F32)
            for part in range(FF_PARTS):
                for device in range(4):
                    index = part * 4 + device
                    row = smalls[index // 16, index // 8 % 2, index // 2 % 4, index % 2]
                    inner_b[part, :, device * 128 : device * 128 + 128] = row[2:3, :].astype(F32)
        if done >= 0:
            weight_loads[done].start()
        if done >= 1:
            matrix, part = (done - 1) // 2, (done - 1) % 2
            weight_loads[done - 1].wait()
            if matrix == 1 and part == 0:
                for tail in tails:
                    pl.when(has_last)(tail.wait_recv)
                save(xt, xt_out)
            project(matrix, part)
            if part == 1:
                save((q, k, v)[matrix], (q_out, k_out, v_out)[matrix])

    pairs = width // PAIR
    count = 2 * pairs
    item_beats = ITEM_BEATS
    part_beats = PART_BEATS

    def beat(time):
        advance(slots, time, BEATS)

    def inner_load(part):
        columns = pl.ds(part * PART if isinstance(part, int) else pl.multiple_of(part * PART, PART), PART)
        ring = part % 2
        return pltpu.make_async_copy(inner_out.at[:, :, :, :, :, columns], inner.at[ring], weight_sem.at[7 + ring])

    def attend(item, carry):
        row, pair = lax.div(item, pairs), lax.rem(item, pairs)
        for number, time in item_beats.items():
            pl.when(item == number)(functools.partial(beat, time))

        @pl.when(pair == 0)
        def _():
            bias[...] = mask_scores(key_ids[row], query_ids[row])

        columns = pl.ds(pl.multiple_of(pair * PAIR, PAIR), PAIR)
        v_t = v[row, :, columns].T
        for start, (low_key, high_key) in zip(range(0, tokens, BLOCK), key_ranges(tokens)):
            s = dot_nt(k[row, low_key:high_key, columns], both_heads(q[row, start : start + BLOCK, columns]))
            mask = bias[low_key:high_key, start : start + BLOCK]
            s = s * SCORE_SCALE + jnp.concatenate([mask, mask], axis=1)
            highest = jnp.max(s, axis=0, keepdims=True)
            expo = jnp.exp2(s - highest)
            total = jnp.sum(expo, axis=0, keepdims=True)
            out = dot(v_t[:, low_key:high_key], expo.astype(BF16)) * (1.0 / total)
            logs = highest + jnp.log2(total)
            for head in range(2):
                lse[row, pair, head : head + 1, start : start + BLOCK] = logs[:, head * BLOCK : head * BLOCK + BLOCK]
            mixed[row, start : start + BLOCK, columns] = own_heads(out).T.astype(BF16)

        @pl.when(pair == pairs - 1)
        def _():
            pl.when(row == 0)(weight_loads[6].wait)
            matrix = weights[3].reshape(width, width)
            for start in range(0, tokens, 256):
                rows = pl.ds(start, 256)
                residual = xt[row, SEGMAX + start : SEGMAX + start + 256, :].astype(F32)
                total = dot(mixed[row, rows, :], matrix) + residual + vec[2:3, :]
                centered, spread_ = layer_norm(total)
                unit[row, rows, :] = centered
                scale[row, rows, :] = spread_
                low[row, rows, :] = (centered * vec[3:4, :] + vec[4:5, :]).astype(BF16)

        return carry

    lax.fori_loop(0, count, attend, 0)
    for source, target in ((mixed, mixed_out), (unit, unit_out), (low, low_out)):
        save(source, target)

    def part_saves(part):
        columns = pl.ds(part * PART if isinstance(part, int) else pl.multiple_of(part * PART, PART), PART)
        ring = part % 2
        return [
            pltpu.make_async_copy(source.at[ring], target.at[:, columns], part_sem.at[number, ring])
            for number, (source, target) in enumerate(((active, active_out), (slope, slope_out)))
        ]

    def feed(part, carry):
        for number, time in part_beats.items():
            pl.when(part == number)(functools.partial(beat, time))

        @pl.when(part >= 2)
        def _():
            for copy in part_saves(part - 2):
                copy.wait()

        ring = lax.rem(part, 2)
        inner_load(part).wait()
        pl.when(part + 1 < FF_PARTS)(lambda: inner_load(part + 1).start())
        w1 = inner[ring].reshape(width, PART)
        for row in range(2):
            act, der = gelu_both(dot(low[row], w1) + inner_b[part])
            active[ring, row * tokens : row * tokens + tokens, :] = act.astype(BF16)
            slope[ring, row * tokens : row * tokens + tokens, :] = der.astype(BF16)
        for copy in part_saves(part):
            copy.start()
        return carry

    inner_load(0).start()
    lax.fori_loop(0, FF_PARTS, feed, 0)
    for part in (FF_PARTS - 2, FF_PARTS - 1):
        for copy in part_saves(part):
            copy.wait()
    finish_slots(slots)
    for tail in tails:
        pl.when(has_next)(tail.wait_send)
    for copy in saves:
        copy.wait()


def encode(hidden, key_ids, query_ids, vectors, wq, wk, wv, wo, inner, outer):
    rows, tokens, width = hidden.shape
    window = tokens + SEGMAX
    hbm = pl.BlockSpec(memory_space=pltpu.HBM)
    vmem = pl.BlockSpec(memory_space=pltpu.VMEM)
    lead = lambda a: a.reshape((1, 1, 1, 1) + a.shape)
    block = wq.shape
    own, wide = (rows, tokens, width), (rows, window, width)
    return pl.pallas_call(
        encode_kernel,
        out_shape=[
            jax.ShapeDtypeStruct(own, BF16),
            jax.ShapeDtypeStruct(wide, BF16),
            jax.ShapeDtypeStruct(wide, BF16),
            jax.ShapeDtypeStruct(wide, BF16),
            jax.ShapeDtypeStruct((4,) + GRID + block, BF16),
            jax.ShapeDtypeStruct(own, BF16),
            jax.ShapeDtypeStruct(own, F32),
            jax.ShapeDtypeStruct(own, BF16),
            jax.ShapeDtypeStruct(GRID + inner.shape, BF16),
            jax.ShapeDtypeStruct(GRID + outer.shape, BF16),
            jax.ShapeDtypeStruct((rows * tokens, inner.shape[1]), BF16),
            jax.ShapeDtypeStruct((rows * tokens, inner.shape[1]), BF16),
            jax.ShapeDtypeStruct((rows, width // PAIR, 8, tokens), F32),
            jax.ShapeDtypeStruct((rows, tokens, 1), F32),
            jax.ShapeDtypeStruct((16, width), F32),
        ],
        in_specs=[hbm] + [vmem] * 11 + [hbm] * 6,
        out_specs=[hbm] * 12 + [vmem] * 3,
        scratch_shapes=[
            pltpu.VMEM((4,) + GRID + block, BF16),
            pltpu.VMEM((1, 1, 1, 1, 16, 128), BF16),
            pltpu.VMEM(GRID + (16, 128), BF16),
            pltpu.VMEM(wide, BF16),
            pltpu.VMEM(own, BF16),
            pltpu.VMEM(wide, BF16),
            pltpu.VMEM(wide, BF16),
            pltpu.VMEM(own, BF16),
            pltpu.VMEM(own, F32),
            pltpu.VMEM(own, BF16),
            pltpu.VMEM((window, tokens), F32),
            pltpu.VMEM((2,) + PIECE, BF16),
            pltpu.VMEM((4, 1, 1, 1, 1) + block, BF16),
            pltpu.VMEM((1, 1, 1, 1) + inner.shape, BF16),
            pltpu.VMEM((1, 1, 1, 1) + outer.shape, BF16),
            pltpu.VMEM((FF_PARTS, 1, PART), F32),
            pltpu.VMEM((2, rows * tokens, PART), BF16),
            pltpu.VMEM((2, rows * tokens, PART), BF16),
            pltpu.SemaphoreType.DMA((57, 8)),
            pltpu.SemaphoreType.DMA((57, 8)),
            pltpu.SemaphoreType.DMA((2, 4)),
            pltpu.SemaphoreType.DMA((24,)),
            pltpu.SemaphoreType.DMA((2, 2)),
            pltpu.SemaphoreType.DMA((9,)),
        ],
        compiler_params=pltpu.CompilerParams(collective_id=0, has_side_effects=True, vmem_limit_bytes=VMEM),
        name="gather_encode",
    )(
        hidden, key_ids, query_ids, *[v.reshape(1, -1) for v in vectors],
        lead(wq), lead(wk), lead(wv), lead(wo), lead(inner), lead(outer),
    )


def forward_kernel(active, outer, unit, cot, vec, layer_out, og, grad_second, sums, total):
    step = pl.program_id(0)
    tokens = active.shape[0]

    @pl.when(step < FF_PARTS)
    def _():
        w2 = outer[...].reshape(PART, -1)
        for start in range(0, tokens, 512):
            rows = pl.ds(start, 512)
            out = dot(active[rows, :], w2)

            @pl.when(step == 0)
            def _():
                total[rows, :] = out

            @pl.when(step > 0)
            def _():
                total[rows, :] += out

    @pl.when(step == FF_PARTS)
    def _():
        sums[...] = jnp.zeros_like(sums)

    @pl.when(step >= FF_PARTS)
    def _():
        first = pl.multiple_of((step - FF_PARTS) * 256, 256)
        for start in range(0, 256, 128):
            rows = pl.ds(start, 128)
            normed = unit[rows, :] * vec[3:4, :] + vec[4:5, :]
            centered, scale = layer_norm(total[pl.ds(first + start, 128), :] + normed + vec[5:6, :])
            layer_out[rows, :] = (centered * vec[6:7, :] + vec[7:8, :]).astype(BF16)
            up = cot[rows, :].astype(F32)
            grad = layer_norm_back(up * vec[6:7, :], centered, scale)
            grad_second[rows, :] = grad
            rounded = grad.astype(BF16)
            og[rows, :] = rounded
            sums[0:1, :] += jnp.sum(rounded.astype(F32), axis=0, keepdims=True)
            sums[1:2, :] += jnp.sum(up * centered, axis=0, keepdims=True)
            sums[2:3, :] += jnp.sum(up, axis=0, keepdims=True)


def feed_forward(active, outer, unit, cot, vec):
    tokens, width = unit.shape
    first = lambda s: jnp.minimum(s, FF_PARTS - 1)
    second = lambda s: jnp.maximum(s - FF_PARTS, 0)
    whole = lambda shape: pl.BlockSpec(shape, lambda s: (0,) * len(shape))
    rows = pl.BlockSpec((256, width), lambda s: (second(s), 0))
    return pl.pallas_call(
        forward_kernel,
        grid=(FF_PARTS + tokens // 256,),
        out_shape=[
            jax.ShapeDtypeStruct((tokens, width), BF16),
            jax.ShapeDtypeStruct((tokens, width), BF16),
            jax.ShapeDtypeStruct((tokens, width), F32),
            jax.ShapeDtypeStruct((8, width), F32),
        ],
        in_specs=[
            pl.BlockSpec((tokens, PART), lambda s: (0, first(s))),
            pl.BlockSpec((4, outer.shape[4], width), lambda s: (first(s), 0, 0)),
            rows, rows, whole(vec.shape),
        ],
        out_specs=[rows, rows, rows, whole((8, width))],
        scratch_shapes=[pltpu.VMEM((tokens, width), F32)],
        compiler_params=pltpu.CompilerParams(vmem_limit_bytes=VMEM),
        name="feed_forward",
    )(active, outer.reshape((32,) + outer.shape[4:]), unit, cot, vec)


def backward_kernel(
    active_in, slope, og, low, inner_w, outer_w, second_in, unit_in, scale, mixed_in, weights_in, vec,
    outer_sum, inner_sum, rest, ib_grad, first_out, gm_out, sums,
    acts, total, unit, mixed, wo, ig, stage, load_sem, save_sem, *bufs,
):
    step = pl.program_id(0)
    chunks = 4
    part = step - chunks
    tokens, width = og.shape
    place = Place()

    def store(j, half, value):
        @pl.when(j < FF_PARTS)
        def _():
            for group in range(4):
                outer_sum[
                    group * 32 + half * 16 : group * 32 + half * 16 + 16,
                    pl.ds(pl.multiple_of(j * 128, 128), 128),
                ] = value[:, group * 128 : group * 128 + 128]

        @pl.when(j >= FF_PARTS)
        def _():
            columns = pl.ds(pl.multiple_of((j - FF_PARTS) * PART, PART), PART)
            inner_sum[half * 16 : half * 16 + 16, columns] = value

    queue = Sums(place, FF_PARTS + EARLY, stage, lambda j: lax.rem(j, FF_PARTS), bufs, store)
    loads = [
        pltpu.make_async_copy(source, target, load_sem.at[number])
        for number, (source, target) in enumerate(
            ((active_in, acts), (second_in, total), (unit_in, unit), (mixed_in, mixed), (weights_in.at[3], wo))
        )
    ]

    def keep(number):
        return pltpu.make_async_copy(
            stage.at[number + EARLY if number < FF_PARTS - EARLY else number - FF_PARTS + EARLY],
            rest.at[number],
            save_sem.at[number],
        )

    @pl.when(step == 0)
    def _():
        for load in loads:
            load.start()
        meet(place)
        loads[0].wait()

    @pl.when(step < chunks)
    def _():
        right = og[:, pl.ds(pl.multiple_of(step * 256, 256), 256)]
        for y in range(2):
            for x in range(2):
                first = (y * 2 + x) * 1024
                grad = dot_tn(acts[:, first : first + 1024], right).astype(BF16).reshape(4, 2, 4, 32, 256)
                for piece in range(2):
                    for group in range(4):
                        stage[2 * step + piece, y, x, :, :, :, group * 128 : group * 128 + 128] = grad[
                            :, :, group, :, piece * 128 : piece * 128 + 128
                        ]
        queue.tick(step)

    @pl.when(step >= chunks)
    def _():
        w1 = inner_w[...].reshape(width, PART)
        w2 = outer_w[...].reshape(PART, width)
        ib_grad[...] = jnp.zeros_like(ib_grad)
        for start in range(0, tokens, 512):
            rows = pl.ds(start, 512)
            piece = (dot_nt(og[rows, :], w2) * slope[rows, :].astype(F32)).astype(BF16)
            ig[rows, :] = piece
            ib_grad[0] += jnp.sum(piece.astype(F32), axis=0, keepdims=True)
        beat = chunks + lax.div(3 * part, 2)
        odd = lax.rem(part, 2)
        pl.when(odd == 1)(functools.partial(queue.tick, beat))
        stage[part] = dot_tn(low[...], ig[...]).astype(BF16).reshape(PIECE)
        for number in range(FF_PARTS - EARLY):
            pl.when(part == EARLY + number)(lambda number=number: keep(number).start())
        queue.tick(beat + odd)
        pl.when(part == 0)(loads[1].wait)
        for start in range(0, tokens, 512):
            rows = pl.ds(start, 512)
            total[rows, :] += dot_nt(ig[rows, :], w1)

    @pl.when(step == pl.num_programs(0) - 1)
    def _():
        for load in loads[2:]:
            load.wait()
        sums[...] = jnp.zeros_like(sums)
        matrix = wo[...].reshape(width, width)
        for start in range(0, tokens, 256):
            rows = pl.ds(start, 256)
            up = total[rows, :]
            centered = unit[rows, :]
            grad = layer_norm_back(up * vec[3:4, :], centered, scale[rows, :])
            total[rows, :] = grad
            rounded = grad.astype(BF16)
            acts[rows, :width] = rounded
            sums[0:1, :] += jnp.sum(rounded.astype(F32), axis=0, keepdims=True)
            sums[1:2, :] += jnp.sum(up * centered, axis=0, keepdims=True)
            sums[2:3, :] += jnp.sum(up, axis=0, keepdims=True)
            acts[rows, width : 2 * width] = dot_nt(rounded, matrix).astype(BF16)
            queue.tick(16 + start // 256)
        save_first = pltpu.make_async_copy(total, first_out, load_sem.at[0])
        save_gm = pltpu.make_async_copy(acts.at[:, pl.ds(width, width)], gm_out, load_sem.at[1])
        save_first.start()
        save_gm.start()
        for piece in range(2):
            columns = slice(piece * PART, piece * PART + PART)
            stage[piece] = dot_tn(mixed[...], acts[:, columns]).astype(BF16).reshape(PIECE)
            keep(FF_PARTS - EARLY + piece).start()
        save_first.wait()
        save_gm.wait()
        for number in range(FF_PARTS - EARLY + 2):
            keep(number).wait()
        queue.finish()


def feed_backward(active, slope, og, low, inner, outer, grad_second, unit, scale, mixed, weights, vec):
    tokens, width = og.shape
    part = lambda s: jnp.maximum(s - 4, 0)
    whole = lambda shape: pl.BlockSpec(shape, lambda s: (0,) * len(shape), pipeline_mode=pl.Buffered(1))
    kept = lambda shape: pl.BlockSpec(shape, lambda s: (0,) * len(shape))
    hbm = pl.BlockSpec(memory_space=pltpu.HBM)
    count = FF_PARTS + EARLY
    rest = FF_PARTS - EARLY + 2
    return pl.pallas_call(
        backward_kernel,
        grid=(4 + FF_PARTS,),
        out_shape=[
            jax.ShapeDtypeStruct(outer.shape[4:], F32),
            jax.ShapeDtypeStruct((32, EARLY * PART), F32),
            jax.ShapeDtypeStruct((rest,) + PIECE, BF16),
            jax.ShapeDtypeStruct((FF_PARTS, 1, PART), F32),
            jax.ShapeDtypeStruct((tokens, width), F32),
            jax.ShapeDtypeStruct((tokens, width), BF16),
            jax.ShapeDtypeStruct((8, width), F32),
        ],
        in_specs=[
            hbm, pl.BlockSpec((tokens, PART), lambda s: (0, part(s))), whole(og.shape), whole(low.shape),
            pl.BlockSpec(GRID + (32, PART), lambda s: (0, 0, 0, 0, 0, part(s))),
            pl.BlockSpec((4, outer.shape[4], width), lambda s: (part(s), 0, 0)),
            hbm, hbm, whole(scale.shape), hbm, hbm, whole(vec.shape),
        ],
        out_specs=[
            kept(outer.shape[4:]), kept((32, EARLY * PART)), hbm,
            pl.BlockSpec((1, 1, PART), lambda s: (part(s), 0, 0)), hbm, hbm, kept((8, width)),
        ],
        scratch_shapes=[
            pltpu.VMEM((tokens, FF_PARTS * PART), BF16),
            pltpu.VMEM((tokens, width), F32),
            pltpu.VMEM((tokens, width), F32),
            pltpu.VMEM((tokens, width), BF16),
            pltpu.VMEM(GRID + (32, width), BF16),
            pltpu.VMEM((tokens, PART), BF16),
            pltpu.VMEM((FF_PARTS,) + PIECE, BF16),
            pltpu.SemaphoreType.DMA((5,)),
            pltpu.SemaphoreType.DMA((rest,)),
        ]
        + sums_buffers(count),
        compiler_params=pltpu.CompilerParams(
            collective_id=3, has_side_effects=True, vmem_limit_bytes=VMEM
        ),
        name="feed_backward",
    )(
        active, slope, og, low, inner, outer.reshape((32,) + outer.shape[4:]), grad_second, unit, scale, mixed,
        weights, vec,
    )


LATE = FF_PARTS - EARLY + 2
BACK = LATE + 4


def attend_back_kernel(
    q, k, v, gm, mixed, lse, key_ids, query_ids, xt, rest, inner_early,
    dq_out, dk_out, dv_out, tail_out, sums, inner_sum, wo_sum, qkv_sum,
    bias, dq_all, dk_all, dv_all, dk_sum, dv_sum, stage, load_sem, *bufs,
):
    group, row, inner = pl.program_id(0), pl.program_id(1), pl.program_id(2)
    step = group * 4 + row * 2 + inner
    tokens = q.shape[1]
    place = Place()

    def load(j):
        return pltpu.make_async_copy(rest.at[j], stage.at[j], load_sem.at[j])

    def ready(j):
        pl.when(j < LATE)(lambda: load(j).wait())

    def store(j, half, value):
        rows = slice(half * 16, half * 16 + 16)
        for number in range(FF_PARTS - EARLY):

            @pl.when(j == number)
            def _():
                first = (EARLY + number) * PART
                inner_sum[rows, first : first + PART] = value

        for piece in range(2):

            @pl.when(j == LATE - 2 + piece)
            def _():
                wo_sum[rows, piece * PART : piece * PART + PART] = value

        @pl.when(j >= LATE)
        def _():
            qkv_sum[j - LATE, rows, :] = value

    def order(beat):
        j = jnp.where(beat <= LATE, beat, jnp.where(beat <= 8, beat - 7 + LATE + 1, LATE + 3))
        return j, ((beat >= 0) & (beat <= LATE)) | (beat == 7) | (beat == 8) | (beat == 11)

    queue = Sums(place, BACK, stage, lambda j: j, bufs, store, ready=ready, order=order)

    @pl.when(step == 0)
    def _():
        for j in range(LATE):
            load(j).start()
        meet(place)
        inner_sum[:, : EARLY * PART] = inner_early[...]

    @pl.when((group == 0) & (inner == 0))
    def _():
        bias[row] = mask_scores(key_ids[0], query_ids[0])

    k_t = k[0].T
    for start, (low_key, high_key) in zip(range(0, tokens, BLOCK), key_ranges(tokens)):
        rows = slice(start, start + BLOCK)
        both_q, both_g = both_heads(q[0, rows, :]), both_heads(gm[0, rows, :])
        product = (gm[0, rows, :].astype(F32) * mixed[0, rows, :].astype(F32)).T
        delta = jnp.concatenate(
            [jnp.sum(product[head * HD : head * HD + HD, :], axis=0, keepdims=True) for head in range(2)], axis=1
        )
        logs = jnp.concatenate([lse[0, 0, head : head + 1, rows] for head in range(2)], axis=1)
        mask = bias[row, low_key:high_key, rows]
        s = dot_nt(k[0, low_key:high_key, :], both_q) * SCORE_SCALE + jnp.concatenate([mask, mask], axis=1)
        probs = jnp.exp2(s - logs)
        dprob = dot_nt(v[0, low_key:high_key, :], both_g)
        score_grad = (probs * (dprob - delta)).astype(BF16)
        dv = dot(probs.astype(BF16), both_g)
        dk = dot(score_grad, both_q)
        dq_out[0, rows, :] = (own_heads(dot(k_t[:, low_key:high_key], score_grad)) * 0.125).T.astype(BF16)
        if start == 0:
            dk_sum[low_key:high_key, :] = dk
            dv_sum[low_key:high_key, :] = dv
            dk_sum[high_key:, :] = jnp.zeros((dk_sum.shape[0] - high_key, PAIR), F32)
            dv_sum[high_key:, :] = jnp.zeros((dk_sum.shape[0] - high_key, PAIR), F32)
        else:
            dk_sum[low_key:high_key, :] += dk
            dv_sum[low_key:high_key, :] += dv
    dk_out[0] = (dk_sum[...] * 0.125).astype(BF16)
    dv_out[0] = dv_sum[...].astype(BF16)
    columns = pl.ds(pl.multiple_of(inner * PAIR, PAIR), PAIR)
    dq_all[row, :, columns] = dq_out[0]
    dk_all[row, :, columns] = dk_out[0]
    dv_all[row, :, columns] = dv_out[0]

    @pl.when((row == 1) & (inner == 1))
    def _():
        span = 2 * PAIR
        pair_slot = jnp.where(group == 3, BACK, jnp.where(group == 2, LATE + 3, LATE + group))
        value_slot = jnp.where(group < 2, LATE + 2, BACK + 1)
        value_half = pl.ds(pl.multiple_of(lax.rem(group, 2) * span, span), span)
        for number, source in enumerate((dq_all, dk_all, dv_all)):
            first = SEGMAX if number == 0 else 0
            grad = dot_tn(xt[0, first:, :], source[0]) + dot_tn(xt[1, first:, :], source[1])
            grad = grad.astype(BF16).reshape(GRID + (32, span))
            if number < 2:
                stage[pair_slot, :, :, :, :, :, number * span : number * span + span] = grad
            else:
                stage[value_slot, :, :, :, :, :, value_half] = grad
        sums[...] = jnp.zeros_like(sums)
        for number, source in enumerate((dq_all, dv_all)):
            added = jnp.sum(source[0].astype(F32), axis=0, keepdims=True) + jnp.sum(
                source[1].astype(F32), axis=0, keepdims=True
            )
            sums[number : number + 1, :] = added

    queue.tick(step)

    @pl.when(step == 15)
    def _():
        saves = [pltpu.make_async_copy(stage.at[BACK + n], tail_out.at[n], load_sem.at[n]) for n in range(2)]
        for save in saves:
            save.start()
        for beat in range(16, 19):
            queue.tick(beat)
        queue.finish()
        for save in saves:
            save.wait()


def attend_back(q, k, v, gm, mixed, lse, key_ids, query_ids, xt, rest, inner_early):
    rows, tokens, width = q.shape
    window = k.shape[1]
    groups = width // (2 * PAIR)
    whole = lambda shape: pl.BlockSpec(shape, lambda g, r, i: (0,) * len(shape), pipeline_mode=pl.Buffered(1))
    kept = lambda shape: pl.BlockSpec(shape, lambda g, r, i: (0,) * len(shape))
    per_pair = lambda n: pl.BlockSpec((1, n, PAIR), lambda g, r, i: (r, 0, g * 2 + i))
    per_row = lambda *s: pl.BlockSpec((1,) + s, lambda g, r, i: (r, 0, 0))
    hbm = pl.BlockSpec(memory_space=pltpu.HBM)
    return pl.pallas_call(
        attend_back_kernel,
        grid=(groups, rows, 2),
        out_shape=[
            jax.ShapeDtypeStruct((rows, tokens, width), BF16),
            jax.ShapeDtypeStruct((rows, window, width), BF16),
            jax.ShapeDtypeStruct((rows, window, width), BF16),
            jax.ShapeDtypeStruct((2,) + PIECE, BF16),
            jax.ShapeDtypeStruct((8, width), F32),
            jax.ShapeDtypeStruct((32, FF_PARTS * PART), F32),
            jax.ShapeDtypeStruct((32, width), F32),
            jax.ShapeDtypeStruct((4, 32, PART), F32),
        ],
        in_specs=[
            per_pair(tokens), per_pair(window), per_pair(window), per_pair(tokens), per_pair(tokens),
            pl.BlockSpec((1, 1, 8, tokens), lambda g, r, i: (r, g * 2 + i, 0, 0)),
            per_row(window, 1), per_row(1, tokens), whole(xt.shape), hbm, whole(inner_early.shape),
        ],
        out_specs=[
            per_pair(tokens), per_pair(window), per_pair(window), hbm,
            pl.BlockSpec((8, 2 * PAIR), lambda g, r, i: (0, g)),
            kept((32, FF_PARTS * PART)), kept((32, width)), kept((4, 32, PART)),
        ],
        scratch_shapes=[
            pltpu.VMEM((rows, window, tokens), F32),
            pltpu.VMEM((rows, tokens, 2 * PAIR), BF16),
            pltpu.VMEM((rows, window, 2 * PAIR), BF16),
            pltpu.VMEM((rows, window, 2 * PAIR), BF16),
            pltpu.VMEM((window, PAIR), F32),
            pltpu.VMEM((window, PAIR), F32),
            pltpu.VMEM((BACK + 2,) + PIECE, BF16),
            pltpu.SemaphoreType.DMA((LATE,)),
        ]
        + sums_buffers(BACK),
        compiler_params=pltpu.CompilerParams(
            collective_id=4, has_side_effects=True, vmem_limit_bytes=VMEM
        ),
        name="attend_back",
    )(q, k, v, gm, mixed, lse, key_ids, query_ids, xt, rest, inner_early)


def shards(vector, base, shift):
    count = vector.shape[1]
    device = lax.broadcasted_iota(jnp.int32, (32, count), 0)
    column = lax.broadcasted_iota(jnp.int32, (32, count), 1)
    rows = jnp.where(device == column >> shift, vector, 0.0).astype(BF16)
    lane = lax.broadcasted_iota(jnp.int32, (count, 128), 1)
    place = lax.broadcasted_iota(jnp.int32, (count, 128), 0)
    pick = jnp.where(lane == base + (place & (2**shift - 1)), 1.0, 0.0).astype(BF16)
    return dot(rows, pick)


def finish_kernel(
    tail_in, sums0, sums1, sums2, ib_grad, qkv_early, dq_in, dk_in, dv_in, weights_in, first_in,
    query_sum, key_sum, value_sum, small_sum, gh_out, tail_there,
    dq, dk, dv, weights, gh, tail_here, stage, small_stage, load_sem, tail_sem, *bufs,
):
    place = Place()
    loads = [
        pltpu.make_async_copy(source, target, load_sem.at[number])
        for number, (source, target) in enumerate(
            (
                (tail_in, stage),
                (weights_in.at[pl.ds(0, 3)], weights),
                (dk_in, dk),
                (dv_in, dv),
                (dq_in, dq),
                (first_in, gh),
            )
        )
    ]
    for load in loads:
        load.start()
    meet(place, -1)
    span = 2 * PAIR

    def store(j, half, value):
        rows = slice(half * 16, half * 16 + 16)
        if j == 0:
            query_sum[rows, 3 * span :] = value[:, :span]
            key_sum[rows, 3 * span :] = value[:, span:]
        else:
            value_sum[rows, 2 * span :] = value

    def store_small(j, half, value):
        small_sum[...] = value

    beats = (0, 1, 2, 3, 4)
    queue = Sums(place, 2, stage, lambda j: j, bufs[:6], store, offsets=beats)
    small = Sums(place, 1, small_stage, lambda j: j, bufs[6:], store_small, halves=1, offsets=beats)
    loads[0].wait()
    queue.tick(0)
    tokens, width = dq.shape[1], dq.shape[2]
    for load in loads[1:4]:
        load.wait()
    matrix = [weights.at[m] for m in range(3)]
    send_tail, recv_tail = place.seq > 0, place.seq < 7
    tails = [
        remote(
            tail_here.at[row], tail_there.at[row], tail_sem.at[0, row], tail_sem.at[1, row],
            place.device(z=lax.rem(place.z + 3 + place.c, 4), c=1 - place.c),
        )
        for row in range(2)
    ]
    for row in range(2):
        tail_here[row] = (
            dot_nt(dk[row, :SEGMAX, :], matrix[1][...].reshape(width, width))
            + dot_nt(dv[row, :SEGMAX, :], matrix[2][...].reshape(width, width))
        ).astype(BF16)
        pl.when(send_tail)(tails[row].start)
        if row == 0:
            queue.tick(1)
    packed = []
    vectors = [sums0[0:1], sums0[1:2], sums1[0:1], sums1[1:2], sums1[2:3], sums2[0:1], sums2[1:2], sums2[2:3]]
    for first in (0, 4):
        packed.append(sum(shards(vectors[first + n], n * 32, 5) for n in range(4)))
    inner = [ib_grad[part][:, n * 128 : n * 128 + 128] for part in range(FF_PARTS) for n in range(4)]
    packed.append(jnp.concatenate(inner, axis=0))
    packed = [p.astype(BF16).astype(F32) for p in packed]
    at = lax.broadcasted_iota(jnp.int32, (32, 16, 128), 1)
    block = jnp.zeros((32, 16, 128), F32)
    for number, value in enumerate(packed):
        block = jnp.where(at == number, jnp.broadcast_to(value[:, None, :], (32, 16, 128)), block)
    small_stage[0] = block.astype(BF16).reshape(GRID + (16, 128))

    small.tick(0)
    queue.tick(2)
    small.tick(1)
    for load in loads[4:]:
        load.wait()

    def own_rows(row):
        for column in range(0, width, 512):
            cols = slice(column, column + 512)
            total = gh[row, :, cols]
            for number, (source, first) in enumerate(((dq, 0), (dk, SEGMAX), (dv, SEGMAX))):
                part = weights[number, column // 512]
                total = total + dot_nt(source[row, first:, :], part.reshape(512, width))
            gh[row, :, cols] = total

    own_rows(0)
    queue.tick(3)
    small.tick(2)
    own_rows(1)
    save = pltpu.make_async_copy(gh, gh_out, load_sem.at[0])
    save.start()
    query_sum[:, : 3 * span] = jnp.concatenate([qkv_early[n, :, :span] for n in (0, 1, 3)], axis=1)
    key_sum[:, : 3 * span] = jnp.concatenate([qkv_early[n, :, span:] for n in (0, 1, 3)], axis=1)
    value_sum[:, : 2 * span] = qkv_early[2]
    for beat in (4, 5):
        queue.tick(beat)
        small.tick(beat - 1)
    queue.finish()
    small.finish()

    @pl.when(place.seq == 7)
    def _():
        tail_there[...] = jnp.zeros_like(tail_there)

    for tail in tails:
        pl.when(recv_tail)(tail.wait_recv)
        pl.when(send_tail)(tail.wait_send)
    save.wait()


def finish(tail_in, sums0, sums1, sums2, ib_grad, qkv_early, dq, dk, dv, weights, grad_first):
    rows, tokens, width = dq.shape
    hbm = pl.BlockSpec(memory_space=pltpu.HBM)
    vmem = pl.BlockSpec(memory_space=pltpu.VMEM)
    return pl.pallas_call(
        finish_kernel,
        out_shape=[
            jax.ShapeDtypeStruct((32, width), F32),
            jax.ShapeDtypeStruct((32, width), F32),
            jax.ShapeDtypeStruct((32, width), F32),
            jax.ShapeDtypeStruct((16, 128), F32),
            jax.ShapeDtypeStruct((rows, tokens, width), F32),
            jax.ShapeDtypeStruct((rows, SEGMAX, width), BF16),
        ],
        in_specs=[hbm] + [vmem] * 5 + [hbm] * 5,
        out_specs=[vmem] * 4 + [hbm, vmem],
        scratch_shapes=[
            pltpu.VMEM(dq.shape, BF16),
            pltpu.VMEM(dk.shape, BF16),
            pltpu.VMEM(dv.shape, BF16),
            pltpu.VMEM((3,) + weights.shape[1:], BF16),
            pltpu.VMEM((rows, tokens, width), F32),
            pltpu.VMEM((rows, SEGMAX, width), BF16),
            pltpu.VMEM((2,) + PIECE, BF16),
            pltpu.VMEM((1,) + GRID + (16, 128), BF16),
            pltpu.SemaphoreType.DMA((6,)),
            pltpu.SemaphoreType.DMA((2, 2)),
        ]
        + sums_buffers(2)
        + sums_buffers(1, 128, 1),
        compiler_params=pltpu.CompilerParams(
            collective_id=5, has_side_effects=True, vmem_limit_bytes=VMEM
        ),
        name="sum_gradients",
    )(tail_in, sums0, sums1, sums2, ib_grad, qkv_early, dq, dk, dv, weights, grad_first)


def deliver_kernel(gh, returned, *refs):
    count = len(refs) // 2
    sources, out, targets = refs[:count], refs[count], refs[count + 1 :]
    late = lax.rem(pl.program_id(0), 2) == 1
    out[...] = gh[...] + jnp.where(late, returned[...].astype(F32), 0.0)

    @pl.when(pl.program_id(0) == 0)
    def _():
        for source, target in zip(sources, targets):
            target[...] = source[...]


def deliver(gh, returned, arrays):
    rows, tokens, width = gh.shape
    whole = lambda a: pl.BlockSpec(a.shape, lambda s: (0,) * a.ndim)
    block = pl.BlockSpec((1, SEGMAX, width), lambda s: (s // 2, s % 2, 0))
    back = pl.BlockSpec((1, SEGMAX, width), lambda s: (s // 2, 0, 0))
    return pl.pallas_call(
        deliver_kernel,
        grid=(2 * rows,),
        out_shape=[jax.ShapeDtypeStruct(gh.shape, F32)] + [jax.ShapeDtypeStruct(a.shape, a.dtype) for a in arrays],
        in_specs=[block, back] + [whole(a) for a in arrays],
        out_specs=[block] + [whole(a) for a in arrays],
        compiler_params=pltpu.CompilerParams(vmem_limit_bytes=VMEM),
        name="deliver",
    )(gh, returned, *arrays)


def local(
    hidden_in, segment_ids, query_weight, query_bias, key_weight, value_weight, value_bias, output_weight,
    output_bias, first_gain, first_shift, inner_weight, inner_bias, outer_weight, outer_bias, second_gain,
    second_shift, cotangent,
):
    rows, tokens, width = hidden_in.shape
    window = tokens + SEGMAX
    vectors = (query_bias, value_bias, output_bias, first_gain, first_shift, outer_bias, second_gain, second_shift, inner_bias)
    padded = jnp.concatenate([jnp.full((rows, SEGMAX), -1, jnp.int32), segment_ids], axis=1)
    key_ids = lax.dynamic_slice_in_dim(padded, lax.axis_index("seq") * tokens, window, 1)
    query_ids = key_ids[:, None, SEGMAX:]
    key_ids = key_ids[:, :, None]
    q, k, v, xt, weights, mixed, unit, low, inner, outer, active, slope, lse, scale, vec = encode(
        hidden_in, key_ids, query_ids, vectors, query_weight, key_weight, value_weight, output_weight,
        inner_weight, outer_weight,
    )
    flat = lambda a: a.reshape(rows * tokens, a.shape[-1])
    layer_out, og, grad_second, sums2 = feed_forward(active, outer, flat(unit), flat(cotangent), vec)
    outer_sum, inner_early, rest, ib_grad, grad_first, gm, sums1 = feed_backward(
        active, slope, og, flat(low), inner, outer, grad_second, flat(unit), flat(scale), flat(mixed), weights, vec
    )
    dq, dk, dv, tail, sums0, inner_sum, wo_sum, qkv_early = attend_back(
        q, k, v, gm.reshape(rows, tokens, width), mixed, lse, key_ids, query_ids, xt, rest, inner_early
    )
    query_sum, key_sum, value_sum, small_sum, grad_hidden, returned = finish(
        tail, sums0, sums1, sums2, ib_grad, qkv_early, dq, dk, dv, weights, grad_first.reshape(rows, tokens, width)
    )
    grad_hidden, query_sum, key_sum, value_sum, wo_sum, inner_sum, outer_sum, small_sum = deliver(
        grad_hidden, returned, (query_sum, key_sum, value_sum, wo_sum, inner_sum, outer_sum, small_sum)
    )
    vector = small_sum[:2].reshape(8, 32)
    return (
        layer_out.reshape(rows, tokens, width),
        grad_hidden,
        query_sum,
        vector[0],
        key_sum,
        value_sum,
        vector[1],
        wo_sum,
        vector[2],
        vector[3],
        vector[4],
        inner_sum,
        small_sum[2],
        outer_sum,
        vector[5],
        vector[6],
        vector[7],
    )


def solution(mesh):
    in_specs = (
        P("dp", "seq", None),
        P("dp", None),
        P(("dp", "seq"), None),
        P(("dp", "seq")),
        P(("dp", "seq"), None),
        P(("dp", "seq"), None),
        P(("dp", "seq")),
        P(("dp", "seq"), None),
        P(("dp", "seq")),
        P(("dp", "seq")),
        P(("dp", "seq")),
        P(("dp", "seq"), None),
        P(("dp", "seq")),
        P(("dp", "seq"), None),
        P(("dp", "seq")),
        P(("dp", "seq")),
        P(("dp", "seq")),
        P("dp", "seq", None),
    )
    out_specs = (
        P("dp", "seq", None),
        P("dp", "seq", None),
        P(("dp", "seq"), None),
        P(("dp", "seq")),
        P(("dp", "seq"), None),
        P(("dp", "seq"), None),
        P(("dp", "seq")),
        P(("dp", "seq"), None),
        P(("dp", "seq")),
        P(("dp", "seq")),
        P(("dp", "seq")),
        P(("dp", "seq"), None),
        P(("dp", "seq")),
        P(("dp", "seq"), None),
        P(("dp", "seq")),
        P(("dp", "seq")),
        P(("dp", "seq")),
    )
    fits = dict(mesh.shape) == {"dp": 4, "seq": 8}
    body = local if fits else plain
    return jax.shard_map(body, mesh=mesh, in_specs=in_specs, out_specs=out_specs, check_vma=False)
```

```python
import functools

import jax
import jax.numpy as jnp
from jax import lax
from jax.experimental import pallas as pl
from jax.experimental.pallas import tpu as pltpu
from jax.sharding import PartitionSpec as P

HD = 64
SEGMAX = 256
EPS = 1e-05
LOG2E = 1.4426950408889634
SCORE_SCALE = 0.125 * LOG2E
HIDDEN = -1e30
PAIR = 2 * HD
MESH = pl.DeviceIdType.MESH
BF16 = jnp.bfloat16
F32 = jnp.float32
VMEM = 64 * 2**20


group_heads = 4


def passed_along(block, axis, distance):
    devices = range(lax.axis_size(axis))
    route = [(i - distance, i) for i in devices if i - distance in devices]
    return lax.ppermute(block, axis, route)


def normalize(hidden, gain, shift):
    center = hidden - jnp.mean(hidden, axis=-1, keepdims=True)
    spread = jnp.mean(center * center, axis=-1, keepdims=True)
    return center * lax.rsqrt(spread + 1e-05) * gain + shift


def contract_rows(left, right):
    return lax.dot_general(
        left, right, (((0,), (0,)), ((), ())), preferred_element_type=jnp.float32
    )


def times_transposed(left, right):
    return lax.dot_general(
        left, right, (((1,), (1,)), ((), ())), preferred_element_type=jnp.float32
    )


def column_sum(values):
    return jnp.sum(values.astype(jnp.float32), axis=0)


def plain(
    hidden_in,
    segment_ids,
    query_weight,
    query_bias,
    key_weight,
    value_weight,
    value_bias,
    output_weight,
    output_bias,
    first_gain,
    first_shift,
    inner_weight,
    inner_bias,
    outer_weight,
    outer_bias,
    second_gain,
    second_shift,
    cotangent,
):
    rows_here, tokens, width = hidden_in.shape
    window = tokens + SEGMAX
    span = group_heads * HD
    groups = width // span
    items = jnp.arange(rows_here * groups, dtype=jnp.int32)
    (
        query_matrix,
        query_offset,
        key_matrix,
        value_matrix,
        value_offset,
        output_matrix,
        output_offset,
        first_scale,
        first_offset,
    ) = (
        lax.all_gather(query_weight, ("dp", "seq"), axis=0, tiled=True),
        lax.all_gather(query_bias, ("dp", "seq"), axis=0, tiled=True),
        lax.all_gather(key_weight, ("dp", "seq"), axis=0, tiled=True),
        lax.all_gather(value_weight, ("dp", "seq"), axis=0, tiled=True),
        lax.all_gather(value_bias, ("dp", "seq"), axis=0, tiled=True),
        lax.all_gather(output_weight, ("dp", "seq"), axis=0, tiled=True),
        lax.all_gather(output_bias, ("dp", "seq"), axis=0, tiled=True),
        lax.all_gather(first_gain, ("dp", "seq"), axis=0, tiled=True),
        lax.all_gather(first_shift, ("dp", "seq"), axis=0, tiled=True),
    )
    flat = hidden_in.reshape(rows_here * tokens, width)
    offset = lax.axis_index("seq") * tokens
    padded_ids = jnp.concatenate(
        [jnp.full((rows_here, SEGMAX), -1, jnp.int32), segment_ids], axis=1
    )
    key_ids = lax.dynamic_slice_in_dim(padded_ids, offset, window, 1)
    query_ids = key_ids[:, SEGMAX:]
    diagonal = jnp.arange(window)[None, :] == jnp.arange(tokens)[:, None] + SEGMAX
    visible = (query_ids[:, :, None] == key_ids[:, None, :]) & (
        query_ids[:, :, None] > 0
    ) | diagonal[None]
    queries = (
        (
            jnp.dot(flat, query_matrix, preferred_element_type=jnp.float32)
            + query_offset.astype(jnp.float32)
        )
        .astype(jnp.bfloat16)
        .reshape(rows_here, tokens, width)
    )
    keys_own = (
        jnp.dot(flat, key_matrix, preferred_element_type=jnp.float32)
        .astype(jnp.bfloat16)
        .reshape(rows_here, tokens, width)
    )
    values_own = (
        (
            jnp.dot(flat, value_matrix, preferred_element_type=jnp.float32)
            + value_offset.astype(jnp.float32)
        )
        .astype(jnp.bfloat16)
        .reshape(rows_here, tokens, width)
    )
    tails = passed_along(
        (keys_own[:, tokens - SEGMAX :], values_own[:, tokens - SEGMAX :]), "seq", 1
    )
    keys_all = jnp.concatenate([tails[0], keys_own], axis=1)
    values_all = jnp.concatenate([tails[1], values_own], axis=1)

    def pieces(item):
        row = item // groups
        column = item % groups * span
        query_part = lax.dynamic_slice(queries, (row, 0, column), (1, tokens, span))[0].reshape(
            tokens, group_heads, HD
        )
        key_part = lax.dynamic_slice(keys_all, (row, 0, column), (1, window, span))[0].reshape(
            window, group_heads, HD
        )
        value_part = lax.dynamic_slice(values_all, (row, 0, column), (1, window, span))[0].reshape(
            window, group_heads, HD
        )
        mask_row = lax.dynamic_index_in_dim(visible, row, 0, keepdims=False)
        scores = (
            jnp.einsum("qhd,khd->hqk", query_part, key_part, preferred_element_type=jnp.float32)
            * 0.125
        )
        scores = jnp.where(mask_row[None], scores, -1e30)
        return (row, column, query_part, key_part, value_part, scores)

    def attend(item):
        row, column, query_part, key_part, value_part, scores = pieces(item)
        highest = jnp.max(scores, axis=-1, keepdims=True)
        expo = jnp.exp(scores - highest)
        total = jnp.sum(expo, axis=-1, keepdims=True)
        probs = (expo / total).astype(jnp.bfloat16)
        mixed_part = jnp.einsum(
            "hqk,khd->qhd", probs, value_part, preferred_element_type=jnp.float32
        )
        return (
            mixed_part.astype(jnp.bfloat16).reshape(tokens, span),
            highest[..., 0] + jnp.log(total[..., 0]),
        )

    mixed_parts, logsums = lax.map(attend, items)
    mixed = (
        mixed_parts.reshape(rows_here, groups, tokens, span)
        .transpose(0, 2, 1, 3)
        .reshape(rows_here * tokens, width)
    )
    first_sum = (
        flat.astype(jnp.float32)
        + jnp.dot(mixed, output_matrix, preferred_element_type=jnp.float32)
        + output_offset.astype(jnp.float32)
    )
    normed = normalize(first_sum, first_scale.astype(jnp.float32), first_offset.astype(jnp.float32))
    normed_low = normed.astype(jnp.bfloat16)
    inner_matrix, inner_offset, outer_matrix, outer_offset, second_scale, second_offset = (
        lax.all_gather(inner_weight, ("dp", "seq"), axis=0, tiled=True),
        lax.all_gather(inner_bias, ("dp", "seq"), axis=0, tiled=True),
        lax.all_gather(outer_weight, ("dp", "seq"), axis=0, tiled=True),
        lax.all_gather(outer_bias, ("dp", "seq"), axis=0, tiled=True),
        lax.all_gather(second_gain, ("dp", "seq"), axis=0, tiled=True),
        lax.all_gather(second_shift, ("dp", "seq"), axis=0, tiled=True),
    )
    inner = jnp.dot(
        normed_low, inner_matrix, preferred_element_type=jnp.float32
    ) + inner_offset.astype(jnp.float32)
    active_low = jax.nn.gelu(inner, approximate=False).astype(jnp.bfloat16)
    second_sum = (
        normed
        + jnp.dot(active_low, outer_matrix, preferred_element_type=jnp.float32)
        + outer_offset.astype(jnp.float32)
    )
    layer_out = normalize(
        second_sum, second_scale.astype(jnp.float32), second_offset.astype(jnp.float32)
    )
    layer_out = layer_out.astype(jnp.bfloat16).reshape(rows_here, tokens, width)
    inner_matrix, inner_offset, outer_matrix, outer_offset, second_scale, second_offset = (
        lax.all_gather(inner_weight, ("dp", "seq"), axis=0, tiled=True),
        lax.all_gather(inner_bias, ("dp", "seq"), axis=0, tiled=True),
        lax.all_gather(outer_weight, ("dp", "seq"), axis=0, tiled=True),
        lax.all_gather(outer_bias, ("dp", "seq"), axis=0, tiled=True),
        lax.all_gather(second_gain, ("dp", "seq"), axis=0, tiled=True),
        lax.all_gather(second_shift, ("dp", "seq"), axis=0, tiled=True),
    )
    upstream = cotangent.reshape(rows_here * tokens, width).astype(jnp.float32)
    _, pull_second = jax.vjp(
        normalize, second_sum, second_scale.astype(jnp.float32), second_offset.astype(jnp.float32)
    )
    grad_second, second_gain_grad, second_shift_grad = pull_second(upstream)
    outer_grad = grad_second.astype(jnp.bfloat16)
    outer_weight_grad = contract_rows(active_low, outer_grad)
    outer_bias_grad = column_sum(outer_grad)
    _, pull_gelu = jax.vjp(lambda value: jax.nn.gelu(value, approximate=False), inner)
    (inner_grad_full,) = pull_gelu(times_transposed(outer_grad, outer_matrix))
    inner_grad = inner_grad_full.astype(jnp.bfloat16)
    inner_weight_grad = contract_rows(normed_low, inner_grad)
    inner_bias_grad = column_sum(inner_grad)
    grad_normed = grad_second + times_transposed(inner_grad, inner_matrix)
    (
        query_matrix,
        query_offset,
        key_matrix,
        value_matrix,
        value_offset,
        output_matrix,
        output_offset,
        first_scale,
        first_offset,
    ) = (
        lax.all_gather(query_weight, ("dp", "seq"), axis=0, tiled=True),
        lax.all_gather(query_bias, ("dp", "seq"), axis=0, tiled=True),
        lax.all_gather(key_weight, ("dp", "seq"), axis=0, tiled=True),
        lax.all_gather(value_weight, ("dp", "seq"), axis=0, tiled=True),
        lax.all_gather(value_bias, ("dp", "seq"), axis=0, tiled=True),
        lax.all_gather(output_weight, ("dp", "seq"), axis=0, tiled=True),
        lax.all_gather(output_bias, ("dp", "seq"), axis=0, tiled=True),
        lax.all_gather(first_gain, ("dp", "seq"), axis=0, tiled=True),
        lax.all_gather(first_shift, ("dp", "seq"), axis=0, tiled=True),
    )
    _, pull_first = jax.vjp(
        normalize, first_sum, first_scale.astype(jnp.float32), first_offset.astype(jnp.float32)
    )
    grad_first, first_gain_grad, first_shift_grad = pull_first(grad_normed)
    attn_grad = grad_first.astype(jnp.bfloat16)
    output_weight_grad = contract_rows(mixed, attn_grad)
    output_bias_grad = column_sum(attn_grad)
    grad_mixed = (
        times_transposed(attn_grad, output_matrix)
        .astype(jnp.bfloat16)
        .reshape(rows_here, tokens, width)
    )

    def attend_back(item):
        row, column, query_part, key_part, value_part, scores = pieces(item)
        logsum = lax.dynamic_index_in_dim(logsums, item, 0, keepdims=False)
        grad_part = lax.dynamic_slice(grad_mixed, (row, 0, column), (1, tokens, span))[0].reshape(
            tokens, group_heads, HD
        )
        probs = jnp.exp(scores - logsum[..., None])
        dprob = jnp.einsum(
            "qhd,khd->hqk", grad_part, value_part, preferred_element_type=jnp.float32
        )
        delta = jnp.sum(probs * dprob, axis=-1, keepdims=True)
        score_grad = (probs * (dprob - delta)).astype(jnp.bfloat16)
        query_part_grad = (
            jnp.einsum("hqk,khd->qhd", score_grad, key_part, preferred_element_type=jnp.float32)
            * 0.125
        )
        key_part_grad = (
            jnp.einsum("hqk,qhd->khd", score_grad, query_part, preferred_element_type=jnp.float32)
            * 0.125
        )
        value_part_grad = jnp.einsum(
            "hqk,qhd->khd",
            probs.astype(jnp.bfloat16),
            grad_part,
            preferred_element_type=jnp.float32,
        )
        return (
            query_part_grad.reshape(tokens, span),
            key_part_grad.reshape(window, span),
            value_part_grad.reshape(window, span),
        )

    query_parts, key_parts, value_parts = lax.map(attend_back, items)
    query_full = (
        query_parts.reshape(rows_here, groups, tokens, span)
        .transpose(0, 2, 1, 3)
        .reshape(rows_here * tokens, width)
    )
    key_window = (
        key_parts.reshape(rows_here, groups, window, span)
        .transpose(0, 2, 1, 3)
        .reshape(rows_here, window, width)
    )
    value_window = (
        value_parts.reshape(rows_here, groups, window, span)
        .transpose(0, 2, 1, 3)
        .reshape(rows_here, window, width)
    )
    returned = (
        passed_along(key_window[:, :SEGMAX].astype(jnp.bfloat16), "seq", -1).astype(jnp.float32),
        passed_along(value_window[:, :SEGMAX].astype(jnp.bfloat16), "seq", -1).astype(jnp.float32),
    )
    key_own = key_window[:, SEGMAX:]
    value_own = value_window[:, SEGMAX:]
    key_total = jnp.concatenate(
        [key_own[:, : tokens - SEGMAX], key_own[:, tokens - SEGMAX :] + returned[0]], axis=1
    )
    value_total = jnp.concatenate(
        [value_own[:, : tokens - SEGMAX], value_own[:, tokens - SEGMAX :] + returned[1]], axis=1
    )
    query_grad = query_full.astype(jnp.bfloat16)
    key_grad = key_total.reshape(rows_here * tokens, width).astype(jnp.bfloat16)
    value_grad = value_total.reshape(rows_here * tokens, width).astype(jnp.bfloat16)
    query_weight_grad = contract_rows(flat, query_grad)
    query_bias_grad = column_sum(query_grad)
    key_weight_grad = contract_rows(flat, key_grad)
    value_weight_grad = contract_rows(flat, value_grad)
    value_bias_grad = column_sum(value_grad)
    grad_hidden = (
        grad_first
        + times_transposed(query_grad, query_matrix)
        + times_transposed(key_grad, key_matrix)
        + times_transposed(value_grad, value_matrix)
    ).reshape(rows_here, tokens, width)
    shards = (
        lax.psum_scatter(query_weight_grad, ("dp", "seq"), scatter_dimension=0, tiled=True),
        lax.psum_scatter(query_bias_grad, ("dp", "seq"), scatter_dimension=0, tiled=True),
        lax.psum_scatter(key_weight_grad, ("dp", "seq"), scatter_dimension=0, tiled=True),
        lax.psum_scatter(value_weight_grad, ("dp", "seq"), scatter_dimension=0, tiled=True),
        lax.psum_scatter(value_bias_grad, ("dp", "seq"), scatter_dimension=0, tiled=True),
        lax.psum_scatter(output_weight_grad, ("dp", "seq"), scatter_dimension=0, tiled=True),
        lax.psum_scatter(output_bias_grad, ("dp", "seq"), scatter_dimension=0, tiled=True),
        lax.psum_scatter(first_gain_grad, ("dp", "seq"), scatter_dimension=0, tiled=True),
        lax.psum_scatter(first_shift_grad, ("dp", "seq"), scatter_dimension=0, tiled=True),
        lax.psum_scatter(inner_weight_grad, ("dp", "seq"), scatter_dimension=0, tiled=True),
        lax.psum_scatter(inner_bias_grad, ("dp", "seq"), scatter_dimension=0, tiled=True),
        lax.psum_scatter(outer_weight_grad, ("dp", "seq"), scatter_dimension=0, tiled=True),
        lax.psum_scatter(outer_bias_grad, ("dp", "seq"), scatter_dimension=0, tiled=True),
        lax.psum_scatter(second_gain_grad, ("dp", "seq"), scatter_dimension=0, tiled=True),
        lax.psum_scatter(second_shift_grad, ("dp", "seq"), scatter_dimension=0, tiled=True),
    )
    return (
        layer_out,
        grad_hidden,
        shards[0],
        shards[1],
        shards[2],
        shards[3],
        shards[4],
        shards[5],
        shards[6],
        shards[7],
        shards[8],
        shards[9],
        shards[10],
        shards[11],
        shards[12],
        shards[13],
        shards[14],
    )


GRID = (2, 2, 4, 2)
FF_PARTS = 8
PART = 512
EARLY = 5
PIECE = GRID + (32, PART)


class Place:
    def __init__(self):
        dp = lax.axis_index("dp")
        seq = lax.axis_index("seq")
        self.x = lax.rem(dp, 2)
        self.y = lax.div(dp, 2)
        self.z = lax.div(seq, 2)
        self.c = lax.rem(seq, 2)
        self.seq = seq

    def device(self, x=None, y=None, z=None, c=None):
        x = self.x if x is None else x
        y = self.y if y is None else y
        z = self.z if z is None else z
        c = self.c if c is None else c
        return (y * 2 + x, z * 2 + c)

    def peer(self, dim):
        if dim == "x":
            return self.device(x=1 - self.x)
        if dim == "y":
            return self.device(y=1 - self.y)
        if dim == "c":
            return self.device(c=1 - self.c)
        return self.device(z=lax.rem(self.z + dim, 4))


def signal(semaphore, device):
    pl.semaphore_signal(semaphore, inc=1, device_id=device, device_id_type=MESH)


def meet(place, along=0):
    barrier = pltpu.get_barrier_semaphore()
    for dim in ("x", "y", "c", 1, 2, 3):
        signal(barrier, place.peer(dim))
    extra = 0
    if along:
        up = (place.c == 1) & (place.z < 3)
        down = (place.c == 0) & (place.z > 0)
        receives, sends = (down, up) if along > 0 else (up, down)
        other = lax.rem(place.z + (3 if along > 0 else 1), 4)

        @pl.when(receives)
        def _():
            signal(barrier, place.device(z=other, c=1 - place.c))

        extra = sends.astype(jnp.int32)
    pl.semaphore_wait(barrier, 6 + extra)


def remote(src, dst, send, recv, device):
    return pltpu.make_async_remote_copy(
        src_ref=src, dst_ref=dst, send_sem=send, recv_sem=recv, device_id=device, device_id_type=MESH
    )


class Gather:
    def __init__(self, place, order, source, target, send, recv):
        held = {"x": False, "y": False, "z": False}

        def region():
            index = []
            for name, size in (("y", 2), ("x", 2), ("z", 4)):
                index.append(pl.ds(0, size) if held[name] else pl.ds(getattr(place, name), 1))
            return target(index[0], index[1], index[2], pl.ds(place.c, 1))

        self.own = pltpu.make_async_copy(source, region(), recv.at[6])
        self.phases = []
        for number, dim in enumerate(order):
            here = region()
            copies = []
            for partner in (1, 2, 3) if dim == "z" else (dim,):
                slot = partner - 1 if dim == "z" else {"x": 3, "y": 4}[dim]
                copies.append(
                    remote(
                        source if number == 0 else here,
                        here,
                        send.at[slot],
                        recv.at[slot],
                        place.peer(partner),
                    )
                )
            self.phases.append(copies)
            held[dim] = True
        here = region()
        self.phases.append([remote(here, here, send.at[5], recv.at[5], place.peer("c"))])

    def start(self, phase):
        if phase == 0:
            self.own.start()
        for copy in self.phases[phase]:
            copy.start()

    def arrive(self, phase):
        for copy in self.phases[phase]:
            copy.wait_recv()
        if phase == 0:
            self.own.wait()

    def step(self, phase):
        if phase > 0:
            self.arrive(phase - 1)
        if phase < 4:
            self.start(phase)

    def finish(self):
        for copies in self.phases:
            for copy in copies:
                copy.wait_send()


LAGS = (0, 1, 4, 7, 9)


class Sums:
    def __init__(self, place, count, stage, slot, bufs, store, halves=2, ready=None, order=None, offsets=LAGS):
        self.place, self.count, self.stage, self.slot = place, count, stage, slot
        self.order, self.offsets = order, offsets
        self.r0, self.r1, self.r2, self.r3, self.send, self.recv = bufs
        self.store, self.halves, self.ready = store, halves, ready

    def copies(self, j, half, phase):
        place = self.place
        send, recv = self.send.at[j, half], self.recv.at[j, half]
        r0, r1, r2, r3 = (ref.at[j, half] for ref in (self.r0, self.r1, self.r2, self.r3))
        if phase == 0:
            source = self.stage.at[self.slot(j), :, :, :, 1 - place.c, pl.ds(16 * half, 16)]
            return [remote(source, r0, send.at[0], recv.at[0], place.peer("c"))]
        if phase == 1:
            source, dim = (r0.at[1 - place.y], "y") if half == 0 else (r0.at[:, 1 - place.x], "x")
            return [remote(source, r1, send.at[1], recv.at[1], place.peer(dim))]
        if phase == 2:
            source, dim = (r1.at[1 - place.x], "x") if half == 0 else (r1.at[1 - place.y], "y")
            return [remote(source, r2, send.at[2], recv.at[2], place.peer(dim))]
        return [
            remote(r2.at[lax.rem(place.z + k, 4)], r3.at[k - 1], send.at[2 + k], recv.at[2 + k], place.peer(k))
            for k in (1, 2, 3)
        ]

    def step(self, j, phase):
        place = self.place
        if phase == 0 and self.ready is not None:
            self.ready(j)
        for half in range(self.halves):
            if phase > 0:
                for copy in self.copies(j, half, phase - 1):
                    copy.wait_recv()
            if phase == 1:
                self.copies(j, half, 0)[0].wait_send()
                mine = self.stage[self.slot(j), :, :, :, place.c, 16 * half : 16 * half + 16, :]
                self.r0[j, half] = self.r0[j, half] + mine
            elif phase == 2:
                mine = self.r0[j, half, place.y] if half == 0 else self.r0[j, half, :, place.x]
                self.r1[j, half] = self.r1[j, half] + mine
            elif phase == 3:
                mine = self.r1[j, half, place.x] if half == 0 else self.r1[j, half, place.y]
                self.r2[j, half] = self.r2[j, half] + mine
            elif phase == 4:
                total = self.r2[j, half, place.z].astype(F32)
                for k in range(3):
                    total = total + self.r3[j, half, k].astype(F32)
                self.store(j, half, total)
            if phase < 4:
                for copy in self.copies(j, half, phase):
                    copy.start()

    def tick(self, time):
        for phase, offset in enumerate(self.offsets):
            j = time - offset
            valid = (j >= 0) & (j < self.count)
            if self.order is not None:
                j, valid = self.order(j)
            if isinstance(valid, bool):
                if valid:
                    self.step(j, phase)
            else:
                pl.when(valid)(functools.partial(self.step, j, phase))

    def finish(self):
        def body(j, carry):
            for half in range(self.halves):
                for phase in (1, 2, 3):
                    for copy in self.copies(j, half, phase):
                        copy.wait_send()
            return carry

        lax.fori_loop(0, self.count, body, 0)


def sums_buffers(count, columns=512, halves=2):
    block = (16, columns)
    return [
        pltpu.VMEM((count, halves, 2, 2, 4) + block, BF16),
        pltpu.VMEM((count, halves, 2, 4) + block, BF16),
        pltpu.VMEM((count, halves, 4) + block, BF16),
        pltpu.VMEM((count, halves, 3) + block, BF16),
        pltpu.SemaphoreType.DMA((count, halves, 6)),
        pltpu.SemaphoreType.DMA((count, halves, 6)),
    ]


def advance(slots, time, offsets):
    for phase, offset in enumerate(offsets):
        number = time - offset
        if 0 <= number < len(slots):
            for part in slots[number]:
                part.step(phase)


def dot(left, right):
    return jnp.dot(left, right, preferred_element_type=F32)


def dot_nt(left, right):
    return lax.dot_general(left, right, (((1,), (1,)), ((), ())), preferred_element_type=F32)


def dot_tn(left, right):
    return lax.dot_general(left, right, (((0,), (0,)), ((), ())), preferred_element_type=F32)


def spread(blocks, row, base, shift, count):
    at = lax.broadcasted_iota(jnp.int32, (32, 16, 128), 1)
    rows = jnp.sum(jnp.where(at == row, blocks.reshape(32, 16, 128).astype(F32), 0.0), axis=1)
    lane = lax.broadcasted_iota(jnp.int32, (128, count), 0)
    column = lax.broadcasted_iota(jnp.int32, (128, count), 1)
    pick = jnp.where(lane == base + (column & (2**shift - 1)), 1.0, 0.0).astype(BF16)
    wide = dot(rows.astype(BF16), pick)
    device = lax.broadcasted_iota(jnp.int32, (32, count), 0)
    column = lax.broadcasted_iota(jnp.int32, (32, count), 1)
    return jnp.sum(jnp.where(device == column >> shift, wide, 0.0), axis=0, keepdims=True)


BEATS = (0, 1, 2, 3, 4)
ITEM_BEATS = {0: 11, 3: 12, 7: 13, 10: 14, 14: 15}
PART_BEATS = {1: 16, 4: 17, 7: 18}
EVEN = (("zxy", 4), ("zyx", 4))
MIXED = (("zxy", 3), ("zyx", 3), ("xzy", 1), ("yzx", 1))


def gather_slots(place, source, target, pieces, orders, send, recv):
    slots = []
    number = 0
    for rows, first, columns in pieces:
        slot = []
        for order, eighths in orders:
            cols = pl.ds(first, columns * eighths // 8)
            first += columns * eighths // 8
            slot.append(
                Gather(
                    place,
                    order,
                    source.at[:, :, :, :, rows, cols],
                    lambda y, x, z, c, rows=rows, cols=cols: target.at[y, x, z, c, rows, cols],
                    send.at[number],
                    recv.at[number],
                )
            )
            number += 1
        slots.append(slot)
    return slots


def finish_slots(slots):
    for slot in slots:
        for part in slot:
            part.finish()


def mask_scores(key_ids, query_ids):
    keys, queries = key_ids.shape[0], query_ids.shape[1]
    key_at = lax.broadcasted_iota(jnp.int32, (keys, queries), 0)
    query_at = lax.broadcasted_iota(jnp.int32, (keys, queries), 1)
    visible = ((key_ids == query_ids) & (query_ids > 0)) | (key_at == query_at + SEGMAX)
    return jnp.where(visible, 0.0, HIDDEN).astype(F32)


BLOCK = 128


def key_ranges(tokens):
    window = tokens + SEGMAX
    return [(start, min(start + BLOCK + 2 * SEGMAX, window)) for start in range(0, tokens, BLOCK)]


def one_head(block, head):
    lane = lax.broadcasted_iota(jnp.int32, block.shape, 1)
    return jnp.where((lane >= HD) == bool(head), block, jnp.zeros_like(block))


def both_heads(block):
    return jnp.concatenate([one_head(block, 0), one_head(block, 1)], axis=0)


def own_heads(value):
    return jnp.concatenate([value[:HD, :BLOCK], value[HD:, BLOCK:]], axis=0)


def layer_norm(value):
    center = value - jnp.mean(value, axis=-1, keepdims=True)
    scale = lax.rsqrt(jnp.mean(center * center, axis=-1, keepdims=True) + EPS)
    return center * scale, scale


def layer_norm_back(grad, unit, scale):
    return scale * (
        grad
        - jnp.mean(grad, axis=-1, keepdims=True)
        - unit * jnp.mean(grad * unit, axis=-1, keepdims=True)
    )


def gelu_both(value):
    bell = jnp.exp2(value * value * (-0.5 * LOG2E)) * 0.3989422804014327
    below = 0.5 + 0.5 * lax.erf(value * 0.7071067811865476)
    return value * below, below + value * bell


def encode_kernel(
    x_in, key_ids, query_ids, v0, v1, v2, v3, v4, v5, v6, v7, v8, wq_in, wk_in, wv_in, wo_in, inner_in, outer_in,
    q_out, k_out, v_out, xt_out, w_out, mixed_out, unit_out, low_out, inner_out, outer_out, active_out, slope_out,
    lse, scale, vec,
    weights, small, smalls, xt, q, k, v, mixed, unit, low, bias, inner, own_weights, inner_own, outer_own, inner_b, active, slope,
    send, recv, tail_sem, local_sem, part_sem, weight_sem,
):
    place = Place()
    tokens, width = x_in.shape[1], x_in.shape[2]
    own_x = pltpu.make_async_copy(x_in, xt.at[:, pl.ds(SEGMAX, tokens)], local_sem.at[0])
    own_x.start()
    own_ff = [
        pltpu.make_async_copy(inner_in, inner_own, local_sem.at[22]),
        pltpu.make_async_copy(outer_in, outer_own, local_sem.at[23]),
    ]
    own_w = [
        pltpu.make_async_copy(source, own_weights.at[number], local_sem.at[18 + number])
        for number, source in enumerate((wq_in, wk_in, wv_in, wo_in))
    ]
    for copy in own_w + own_ff:
        copy.start()
    at = lax.broadcasted_iota(jnp.int32, (16, 128), 0)
    block = jnp.zeros((16, 128), F32)
    for number, vector in enumerate((v0, v1, v2, v3, v4, v5, v6, v7, v8)):
        size = vector.shape[1]
        base, row = (number % 4 * 32, number // 4) if number < 8 else (0, 2)
        lane = lax.broadcasted_iota(jnp.int32, (size, 128), 1)
        index = lax.broadcasted_iota(jnp.int32, (size, 128), 0)
        pick = jnp.where(lane == base + index, 1.0, 0.0).astype(BF16)
        wide = dot(jnp.broadcast_to(vector[...], (16, size)), pick)
        block = block + jnp.where(at == row, wide, 0.0)
    small[0, 0, 0, 0] = block.astype(BF16)
    meet(place, 1)
    half = width // 2
    slots = []
    vectors = Gather(place, "zxy", small, lambda y, x, z, c: smalls.at[y, x, z, c], send.at[56], recv.at[56])
    everything, used = slice(None), 0

    def add(source, target, pieces, orders):
        nonlocal used, slots
        sems = pl.ds(used, len(orders) * len(pieces))
        used += len(orders) * len(pieces)
        slots += gather_slots(place, source, target, pieces, orders, send.at[sems], recv.at[sems])

    for copy in own_w:
        copy.wait()
    for matrix in range(3):
        add(own_weights.at[matrix], w_out.at[matrix], [(everything, part * half, half) for part in range(2)], EVEN)
    add(own_weights.at[3], w_out.at[3], [(everything, 0, width)], MIXED)
    slots[0].append(vectors)
    add(inner_own, inner_out, [(everything, part * width, width) for part in range(4)], MIXED)
    add(outer_own, outer_out, [(pl.ds(part * 32, 32), 0, width) for part in range(4)], MIXED)

    tails = []
    for row in range(2):
        for start in range(0, SEGMAX, 128):
            tails.append(
                remote(
                    x_in.at[row, pl.ds(tokens - SEGMAX + start, 128)],
                    xt.at[row, pl.ds(start, 128)],
                    tail_sem.at[0, len(tails)],
                    tail_sem.at[1, len(tails)],
                    place.device(z=lax.rem(place.z + place.c, 4), c=1 - place.c),
                )
            )
    has_next, has_last = place.seq < 7, place.seq > 0
    saves = []

    def save(source, target):
        copy = pltpu.make_async_copy(source, target, local_sem.at[1 + len(saves)])
        copy.start()
        saves.append(copy)

    def project(matrix, part):
        target, bias_row, first = ((q, 0, SEGMAX), (k, None, 0), (v, 1, 0))[matrix]
        columns = slice(part * half, part * half + half)
        right = weights[matrix, :, :, :, :, :, columns].reshape(width, half)
        for row in range(2):
            out = dot(xt[row, first:, :], right)
            if bias_row is not None:
                out = out + vec[bias_row : bias_row + 1, columns]
            target[row, :, columns] = out.astype(BF16)

    weight_loads = []
    for matrix in range(4):
        for start in range(0, width, half):
            columns = pl.ds(start, half) if matrix < 3 else pl.ds(0, width)
            if matrix < 3 or start == 0:
                weight_loads.append(
                    pltpu.make_async_copy(
                        w_out.at[matrix, :, :, :, :, :, columns],
                        weights.at[matrix, :, :, :, :, :, columns],
                        weight_sem.at[len(weight_loads)],
                    )
                )
    last = BEATS[-1]
    for time in range(last + 7):
        if 3 <= time <= 6:
            pl.when(has_next)(tails[time - 3].start)
        if time == 3:
            xt_zero = jnp.zeros((2, SEGMAX, width), BF16)

            @pl.when(place.seq == 0)
            def _():
                xt[:, :SEGMAX, :] = xt_zero

            own_x.wait()
            for copy in own_ff:
                copy.wait()
        advance(slots, time, BEATS)
        done = time - last
        if done == 0:
            for vector in range(8):
                vec[vector : vector + 1, :] = spread(smalls[...], vector // 4, vector % 4 * 32, 5, width)
            vec[8:, :] = jnp.zeros((8, width), F32)
            for part in range(FF_PARTS):
                for device in range(4):
                    index = part * 4 + device
                    row = smalls[index // 16, index // 8 % 2, index // 2 % 4, index % 2]
                    inner_b[part, :, device * 128 : device * 128 + 128] = row[2:3, :].astype(F32)
        if done >= 0:
            weight_loads[done].start()
        if done >= 1:
            matrix, part = (done - 1) // 2, (done - 1) % 2
            weight_loads[done - 1].wait()
            if matrix == 1 and part == 0:
                for tail in tails:
                    pl.when(has_last)(tail.wait_recv)
                save(xt, xt_out)
            project(matrix, part)
            if part == 1:
                save((q, k, v)[matrix], (q_out, k_out, v_out)[matrix])

    pairs = width // PAIR
    count = 2 * pairs
    item_beats = ITEM_BEATS
    part_beats = PART_BEATS

    def beat(time):
        advance(slots, time, BEATS)

    def inner_load(part):
        columns = pl.ds(part * PART if isinstance(part, int) else pl.multiple_of(part * PART, PART), PART)
        ring = part % 2
        return pltpu.make_async_copy(inner_out.at[:, :, :, :, :, columns], inner.at[ring], weight_sem.at[7 + ring])

    def attend(item, carry):
        row, pair = lax.div(item, pairs), lax.rem(item, pairs)
        for number, time in item_beats.items():
            pl.when(item == number)(functools.partial(beat, time))

        @pl.when(pair == 0)
        def _():
            bias[...] = mask_scores(key_ids[row], query_ids[row])

        columns = pl.ds(pl.multiple_of(pair * PAIR, PAIR), PAIR)
        v_t = v[row, :, columns].T
        for start, (low_key, high_key) in zip(range(0, tokens, BLOCK), key_ranges(tokens)):
            s = dot_nt(k[row, low_key:high_key, columns], both_heads(q[row, start : start + BLOCK, columns]))
            mask = bias[low_key:high_key, start : start + BLOCK]
            s = s * SCORE_SCALE + jnp.concatenate([mask, mask], axis=1)
            highest = jnp.max(s, axis=0, keepdims=True)
            expo = jnp.exp2(s - highest)
            total = jnp.sum(expo, axis=0, keepdims=True)
            out = dot(v_t[:, low_key:high_key], expo.astype(BF16)) * (1.0 / total)
            logs = highest + jnp.log2(total)
            for head in range(2):
                lse[row, pair, head : head + 1, start : start + BLOCK] = logs[:, head * BLOCK : head * BLOCK + BLOCK]
            mixed[row, start : start + BLOCK, columns] = own_heads(out).T.astype(BF16)

        @pl.when(pair == pairs - 1)
        def _():
            pl.when(row == 0)(weight_loads[6].wait)
            matrix = weights[3].reshape(width, width)
            for start in range(0, tokens, 256):
                rows = pl.ds(start, 256)
                residual = xt[row, SEGMAX + start : SEGMAX + start + 256, :].astype(F32)
                total = dot(mixed[row, rows, :], matrix) + residual + vec[2:3, :]
                centered, spread_ = layer_norm(total)
                unit[row, rows, :] = centered
                scale[row, rows, :] = spread_
                low[row, rows, :] = (centered * vec[3:4, :] + vec[4:5, :]).astype(BF16)

        return carry

    lax.fori_loop(0, count, attend, 0)
    for source, target in ((mixed, mixed_out), (unit, unit_out), (low, low_out)):
        save(source, target)

    def part_saves(part):
        columns = pl.ds(part * PART if isinstance(part, int) else pl.multiple_of(part * PART, PART), PART)
        ring = part % 2
        return [
            pltpu.make_async_copy(source.at[ring], target.at[:, columns], part_sem.at[number, ring])
            for number, (source, target) in enumerate(((active, active_out), (slope, slope_out)))
        ]

    def feed(part, carry):
        for number, time in part_beats.items():
            pl.when(part == number)(functools.partial(beat, time))

        @pl.when(part >= 2)
        def _():
            for copy in part_saves(part - 2):
                copy.wait()

        ring = lax.rem(part, 2)
        inner_load(part).wait()
        pl.when(part + 1 < FF_PARTS)(lambda: inner_load(part + 1).start())
        w1 = inner[ring].reshape(width, PART)
        for row in range(2):
            act, der = gelu_both(dot(low[row], w1) + inner_b[part])
            active[ring, row * tokens : row * tokens + tokens, :] = act.astype(BF16)
            slope[ring, row * tokens : row * tokens + tokens, :] = der.astype(BF16)
        for copy in part_saves(part):
            copy.start()
        return carry

    inner_load(0).start()
    lax.fori_loop(0, FF_PARTS, feed, 0)
    for part in (FF_PARTS - 2, FF_PARTS - 1):
        for copy in part_saves(part):
            copy.wait()
    finish_slots(slots)
    for tail in tails:
        pl.when(has_next)(tail.wait_send)
    for copy in saves:
        copy.wait()


def encode(hidden, key_ids, query_ids, vectors, wq, wk, wv, wo, inner, outer):
    rows, tokens, width = hidden.shape
    window = tokens + SEGMAX
    hbm = pl.BlockSpec(memory_space=pltpu.HBM)
    vmem = pl.BlockSpec(memory_space=pltpu.VMEM)
    lead = lambda a: a.reshape((1, 1, 1, 1) + a.shape)
    block = wq.shape
    own, wide = (rows, tokens, width), (rows, window, width)
    return pl.pallas_call(
        encode_kernel,
        out_shape=[
            jax.ShapeDtypeStruct(own, BF16),
            jax.ShapeDtypeStruct(wide, BF16),
            jax.ShapeDtypeStruct(wide, BF16),
            jax.ShapeDtypeStruct(wide, BF16),
            jax.ShapeDtypeStruct((4,) + GRID + block, BF16),
            jax.ShapeDtypeStruct(own, BF16),
            jax.ShapeDtypeStruct(own, F32),
            jax.ShapeDtypeStruct(own, BF16),
            jax.ShapeDtypeStruct(GRID + inner.shape, BF16),
            jax.ShapeDtypeStruct(GRID + outer.shape, BF16),
            jax.ShapeDtypeStruct((rows * tokens, inner.shape[1]), BF16),
            jax.ShapeDtypeStruct((rows * tokens, inner.shape[1]), BF16),
            jax.ShapeDtypeStruct((rows, width // PAIR, 8, tokens), F32),
            jax.ShapeDtypeStruct((rows, tokens, 1), F32),
            jax.ShapeDtypeStruct((16, width), F32),
        ],
        in_specs=[hbm] + [vmem] * 11 + [hbm] * 6,
        out_specs=[hbm] * 12 + [vmem] * 3,
        scratch_shapes=[
            pltpu.VMEM((4,) + GRID + block, BF16),
            pltpu.VMEM((1, 1, 1, 1, 16, 128), BF16),
            pltpu.VMEM(GRID + (16, 128), BF16),
            pltpu.VMEM(wide, BF16),
            pltpu.VMEM(own, BF16),
            pltpu.VMEM(wide, BF16),
            pltpu.VMEM(wide, BF16),
            pltpu.VMEM(own, BF16),
            pltpu.VMEM(own, F32),
            pltpu.VMEM(own, BF16),
            pltpu.VMEM((window, tokens), F32),
            pltpu.VMEM((2,) + PIECE, BF16),
            pltpu.VMEM((4, 1, 1, 1, 1) + block, BF16),
            pltpu.VMEM((1, 1, 1, 1) + inner.shape, BF16),
            pltpu.VMEM((1, 1, 1, 1) + outer.shape, BF16),
            pltpu.VMEM((FF_PARTS, 1, PART), F32),
            pltpu.VMEM((2, rows * tokens, PART), BF16),
            pltpu.VMEM((2, rows * tokens, PART), BF16),
            pltpu.SemaphoreType.DMA((57, 8)),
            pltpu.SemaphoreType.DMA((57, 8)),
            pltpu.SemaphoreType.DMA((2, 4)),
            pltpu.SemaphoreType.DMA((24,)),
            pltpu.SemaphoreType.DMA((2, 2)),
            pltpu.SemaphoreType.DMA((9,)),
        ],
        compiler_params=pltpu.CompilerParams(collective_id=0, has_side_effects=True, vmem_limit_bytes=VMEM),
        name="gather_encode",
    )(
        hidden, key_ids, query_ids, *[v.reshape(1, -1) for v in vectors],
        lead(wq), lead(wk), lead(wv), lead(wo), lead(inner), lead(outer),
    )


FORWARD = 4


def forward_kernel(active, outer, unit, cot, vec, layer_out, og, grad_second, sums, total):
    step = pl.program_id(0)
    tokens = active.shape[0]

    @pl.when(step < FORWARD)
    def _():
        w2 = outer[...].reshape(-1, total.shape[1])
        for start in range(0, tokens, 512):
            rows = pl.ds(start, 512)
            out = dot(active[rows, :], w2)

            @pl.when(step == 0)
            def _():
                total[rows, :] = out

            @pl.when(step > 0)
            def _():
                total[rows, :] += out

    @pl.when(step == FORWARD)
    def _():
        sums[...] = jnp.zeros_like(sums)

    @pl.when(step >= FORWARD)
    def _():
        first = pl.multiple_of((step - FORWARD) * 256, 256)
        for start in range(0, 256, 128):
            rows = pl.ds(start, 128)
            normed = unit[rows, :] * vec[3:4, :] + vec[4:5, :]
            centered, scale = layer_norm(total[pl.ds(first + start, 128), :] + normed + vec[5:6, :])
            layer_out[rows, :] = (centered * vec[6:7, :] + vec[7:8, :]).astype(BF16)
            up = cot[rows, :].astype(F32)
            grad = layer_norm_back(up * vec[6:7, :], centered, scale)
            grad_second[rows, :] = grad
            rounded = grad.astype(BF16)
            og[rows, :] = rounded
            sums[0:1, :] += jnp.sum(rounded.astype(F32), axis=0, keepdims=True)
            sums[1:2, :] += jnp.sum(up * centered, axis=0, keepdims=True)
            sums[2:3, :] += jnp.sum(up, axis=0, keepdims=True)


def feed_forward(active, outer, unit, cot, vec):
    tokens, width = unit.shape
    first = lambda s: jnp.minimum(s, FORWARD - 1)
    second = lambda s: jnp.maximum(s - FORWARD, 0)
    whole = lambda shape: pl.BlockSpec(shape, lambda s: (0,) * len(shape))
    rows = pl.BlockSpec((256, width), lambda s: (second(s), 0))
    return pl.pallas_call(
        forward_kernel,
        grid=(FORWARD + tokens // 256,),
        out_shape=[
            jax.ShapeDtypeStruct((tokens, width), BF16),
            jax.ShapeDtypeStruct((tokens, width), BF16),
            jax.ShapeDtypeStruct((tokens, width), F32),
            jax.ShapeDtypeStruct((8, width), F32),
        ],
        in_specs=[
            pl.BlockSpec((tokens, active.shape[1] // FORWARD), lambda s: (0, first(s))),
            pl.BlockSpec((32 // FORWARD, outer.shape[4], width), lambda s: (first(s), 0, 0)),
            rows, rows, whole(vec.shape),
        ],
        out_specs=[rows, rows, rows, whole((8, width))],
        scratch_shapes=[pltpu.VMEM((tokens, width), F32)],
        compiler_params=pltpu.CompilerParams(vmem_limit_bytes=VMEM),
        name="feed_forward",
    )(active, outer.reshape((32,) + outer.shape[4:]), unit, cot, vec)


def backward_kernel(
    active_in, slope, og, low, inner_w, outer_w, second_in, unit_in, scale, mixed_in, weights_in, vec,
    outer_sum, inner_sum, rest, ib_grad, first_out, gm_out, sums,
    acts, total, unit, mixed, wo, ig, stage, load_sem, save_sem, *bufs,
):
    step = pl.program_id(0)
    chunks = 4
    part = step - chunks
    tokens, width = og.shape
    place = Place()

    def store(j, half, value):
        @pl.when(j < FF_PARTS)
        def _():
            for group in range(4):
                outer_sum[
                    group * 32 + half * 16 : group * 32 + half * 16 + 16,
                    pl.ds(pl.multiple_of(j * 128, 128), 128),
                ] = value[:, group * 128 : group * 128 + 128]

        @pl.when(j >= FF_PARTS)
        def _():
            columns = pl.ds(pl.multiple_of((j - FF_PARTS) * PART, PART), PART)
            inner_sum[half * 16 : half * 16 + 16, columns] = value

    queue = Sums(place, FF_PARTS + EARLY, stage, lambda j: lax.rem(j, FF_PARTS), bufs, store)
    loads = [
        pltpu.make_async_copy(source, target, load_sem.at[number])
        for number, (source, target) in enumerate(
            ((active_in, acts), (second_in, total), (unit_in, unit), (mixed_in, mixed), (weights_in.at[3], wo))
        )
    ]

    def keep(number):
        return pltpu.make_async_copy(
            stage.at[number + EARLY if number < FF_PARTS - EARLY else number - FF_PARTS + EARLY],
            rest.at[number],
            save_sem.at[number],
        )

    @pl.when(step == 0)
    def _():
        for load in loads:
            load.start()
        meet(place)
        loads[0].wait()

    beat, odd = lax.div(3 * step, 2), lax.rem(step, 2)

    @pl.when(step < chunks)
    def _():
        pl.when(odd == 1)(functools.partial(queue.tick, beat))
        right = og[:, pl.ds(pl.multiple_of(step * 256, 256), 256)]
        for y in range(2):
            for x in range(2):
                first = (y * 2 + x) * 1024
                grad = dot_tn(acts[:, first : first + 1024], right).astype(BF16).reshape(4, 2, 4, 32, 256)
                for piece in range(2):
                    for group in range(4):
                        stage[2 * step + piece, y, x, :, :, :, group * 128 : group * 128 + 128] = grad[
                            :, :, group, :, piece * 128 : piece * 128 + 128
                        ]
        queue.tick(beat + odd)

    @pl.when(step >= chunks)
    def _():
        w1 = inner_w[...].reshape(width, PART)
        w2 = outer_w[...].reshape(PART, width)
        ib_grad[...] = jnp.zeros_like(ib_grad)
        for start in range(0, tokens, 512):
            rows = pl.ds(start, 512)
            piece = (dot_nt(og[rows, :], w2) * slope[rows, :].astype(F32)).astype(BF16)
            ig[rows, :] = piece
            ib_grad[0] += jnp.sum(piece.astype(F32), axis=0, keepdims=True)
        pl.when(odd == 1)(functools.partial(queue.tick, beat))
        stage[part] = dot_tn(low[...], ig[...]).astype(BF16).reshape(PIECE)
        for number in range(FF_PARTS - EARLY):
            pl.when(part == EARLY + number)(lambda number=number: keep(number).start())
        queue.tick(beat + odd)
        pl.when(part == 0)(loads[1].wait)
        for start in range(0, tokens, 512):
            rows = pl.ds(start, 512)
            total[rows, :] += dot_nt(ig[rows, :], w1)

    @pl.when(step == pl.num_programs(0) - 1)
    def _():
        for load in loads[2:]:
            load.wait()
        sums[...] = jnp.zeros_like(sums)
        matrix = wo[...].reshape(width, width)
        for start in range(0, tokens, 256):
            rows = pl.ds(start, 256)
            up = total[rows, :]
            centered = unit[rows, :]
            grad = layer_norm_back(up * vec[3:4, :], centered, scale[rows, :])
            total[rows, :] = grad
            rounded = grad.astype(BF16)
            acts[rows, :width] = rounded
            sums[0:1, :] += jnp.sum(rounded.astype(F32), axis=0, keepdims=True)
            sums[1:2, :] += jnp.sum(up * centered, axis=0, keepdims=True)
            sums[2:3, :] += jnp.sum(up, axis=0, keepdims=True)
            acts[rows, width : 2 * width] = dot_nt(rounded, matrix).astype(BF16)
            queue.tick(18 + start // 256)
        for late in range(22, FF_PARTS + EARLY + LAGS[-1]):
            queue.tick(late)
        save_first = pltpu.make_async_copy(total, first_out, load_sem.at[0])
        save_gm = pltpu.make_async_copy(acts.at[:, pl.ds(width, width)], gm_out, load_sem.at[1])
        save_first.start()
        save_gm.start()
        for piece in range(2):
            columns = slice(piece * PART, piece * PART + PART)
            stage[piece] = dot_tn(mixed[...], acts[:, columns]).astype(BF16).reshape(PIECE)
            keep(FF_PARTS - EARLY + piece).start()
        save_first.wait()
        save_gm.wait()
        for number in range(FF_PARTS - EARLY + 2):
            keep(number).wait()
        queue.finish()


def feed_backward(active, slope, og, low, inner, outer, grad_second, unit, scale, mixed, weights, vec):
    tokens, width = og.shape
    part = lambda s: jnp.maximum(s - 4, 0)
    whole = lambda shape: pl.BlockSpec(shape, lambda s: (0,) * len(shape), pipeline_mode=pl.Buffered(1))
    kept = lambda shape: pl.BlockSpec(shape, lambda s: (0,) * len(shape))
    hbm = pl.BlockSpec(memory_space=pltpu.HBM)
    count = FF_PARTS + EARLY
    rest = FF_PARTS - EARLY + 2
    return pl.pallas_call(
        backward_kernel,
        grid=(4 + FF_PARTS,),
        out_shape=[
            jax.ShapeDtypeStruct(outer.shape[4:], F32),
            jax.ShapeDtypeStruct((32, EARLY * PART), F32),
            jax.ShapeDtypeStruct((rest,) + PIECE, BF16),
            jax.ShapeDtypeStruct((FF_PARTS, 1, PART), F32),
            jax.ShapeDtypeStruct((tokens, width), F32),
            jax.ShapeDtypeStruct((tokens, width), BF16),
            jax.ShapeDtypeStruct((8, width), F32),
        ],
        in_specs=[
            hbm, pl.BlockSpec((tokens, PART), lambda s: (0, part(s))), whole(og.shape), whole(low.shape),
            pl.BlockSpec(GRID + (32, PART), lambda s: (0, 0, 0, 0, 0, part(s))),
            pl.BlockSpec((4, outer.shape[4], width), lambda s: (part(s), 0, 0)),
            hbm, hbm, whole(scale.shape), hbm, hbm, whole(vec.shape),
        ],
        out_specs=[
            kept(outer.shape[4:]), kept((32, EARLY * PART)), hbm,
            pl.BlockSpec((1, 1, PART), lambda s: (part(s), 0, 0)), hbm, hbm, kept((8, width)),
        ],
        scratch_shapes=[
            pltpu.VMEM((tokens, FF_PARTS * PART), BF16),
            pltpu.VMEM((tokens, width), F32),
            pltpu.VMEM((tokens, width), F32),
            pltpu.VMEM((tokens, width), BF16),
            pltpu.VMEM(GRID + (32, width), BF16),
            pltpu.VMEM((tokens, PART), BF16),
            pltpu.VMEM((FF_PARTS,) + PIECE, BF16),
            pltpu.SemaphoreType.DMA((5,)),
            pltpu.SemaphoreType.DMA((rest,)),
        ]
        + sums_buffers(count),
        compiler_params=pltpu.CompilerParams(
            collective_id=3, has_side_effects=True, vmem_limit_bytes=VMEM
        ),
        name="feed_backward",
    )(
        active, slope, og, low, inner, outer.reshape((32,) + outer.shape[4:]), grad_second, unit, scale, mixed,
        weights, vec,
    )


LATE = FF_PARTS - EARLY + 2
BACK = LATE + 4


def attend_back_kernel(
    q, k, v, gm, mixed, lse, key_ids, query_ids, xt, rest, inner_early,
    dq_out, dk_out, dv_out, tail_out, sums, inner_sum, wo_sum, qkv_sum,
    bias, dq_all, dk_all, dv_all, dk_sum, dv_sum, stage, load_sem, *bufs,
):
    group, row, inner = pl.program_id(0), pl.program_id(1), pl.program_id(2)
    step = group * 4 + row * 2 + inner
    tokens = q.shape[1]
    place = Place()

    def load(j):
        return pltpu.make_async_copy(rest.at[j], stage.at[j], load_sem.at[j])

    def ready(j):
        pl.when(j < LATE)(lambda: load(j).wait())

    def store(j, half, value):
        rows = slice(half * 16, half * 16 + 16)
        for number in range(FF_PARTS - EARLY):

            @pl.when(j == number)
            def _():
                first = (EARLY + number) * PART
                inner_sum[rows, first : first + PART] = value

        for piece in range(2):

            @pl.when(j == LATE - 2 + piece)
            def _():
                wo_sum[rows, piece * PART : piece * PART + PART] = value

        @pl.when(j >= LATE)
        def _():
            qkv_sum[j - LATE, rows, :] = value

    def order(beat):
        j = jnp.where(beat <= LATE, beat, jnp.where(beat <= 8, beat - 7 + LATE + 1, LATE + 3))
        return j, ((beat >= 0) & (beat <= LATE)) | (beat == 7) | (beat == 8) | (beat == 11)

    queue = Sums(place, BACK, stage, lambda j: j, bufs, store, ready=ready, order=order)

    @pl.when(step == 0)
    def _():
        for j in range(LATE):
            load(j).start()
        meet(place)
        inner_sum[:, : EARLY * PART] = inner_early[...]

    @pl.when((group == 0) & (inner == 0))
    def _():
        bias[row] = mask_scores(key_ids[0], query_ids[0])

    k_t = k[0].T
    for start, (low_key, high_key) in zip(range(0, tokens, BLOCK), key_ranges(tokens)):
        rows = slice(start, start + BLOCK)
        both_q, both_g = both_heads(q[0, rows, :]), both_heads(gm[0, rows, :])
        product = (gm[0, rows, :].astype(F32) * mixed[0, rows, :].astype(F32)).T
        delta = jnp.concatenate(
            [jnp.sum(product[head * HD : head * HD + HD, :], axis=0, keepdims=True) for head in range(2)], axis=1
        )
        logs = jnp.concatenate([lse[0, 0, head : head + 1, rows] for head in range(2)], axis=1)
        mask = bias[row, low_key:high_key, rows]
        s = dot_nt(k[0, low_key:high_key, :], both_q) * SCORE_SCALE + jnp.concatenate([mask, mask], axis=1)
        probs = jnp.exp2(s - logs)
        dprob = dot_nt(v[0, low_key:high_key, :], both_g)
        score_grad = (probs * (dprob - delta)).astype(BF16)
        dv = dot(probs.astype(BF16), both_g)
        dk = dot(score_grad, both_q)
        dq_out[0, rows, :] = (own_heads(dot(k_t[:, low_key:high_key], score_grad)) * 0.125).T.astype(BF16)
        if start == 0:
            dk_sum[low_key:high_key, :] = dk
            dv_sum[low_key:high_key, :] = dv
            dk_sum[high_key:, :] = jnp.zeros((dk_sum.shape[0] - high_key, PAIR), F32)
            dv_sum[high_key:, :] = jnp.zeros((dk_sum.shape[0] - high_key, PAIR), F32)
        else:
            dk_sum[low_key:high_key, :] += dk
            dv_sum[low_key:high_key, :] += dv
    dk_out[0] = (dk_sum[...] * 0.125).astype(BF16)
    dv_out[0] = dv_sum[...].astype(BF16)
    columns = pl.ds(pl.multiple_of(inner * PAIR, PAIR), PAIR)
    dq_all[row, :, columns] = dq_out[0]
    dk_all[row, :, columns] = dk_out[0]
    dv_all[row, :, columns] = dv_out[0]

    @pl.when((row == 1) & (inner == 1))
    def _():
        span = 2 * PAIR
        pair_slot = jnp.where(group == 3, BACK, jnp.where(group == 2, LATE + 3, LATE + group))
        value_slot = jnp.where(group < 2, LATE + 2, BACK + 1)
        value_half = pl.ds(pl.multiple_of(lax.rem(group, 2) * span, span), span)
        for number, source in enumerate((dq_all, dk_all, dv_all)):
            first = SEGMAX if number == 0 else 0
            grad = dot_tn(xt[0, first:, :], source[0]) + dot_tn(xt[1, first:, :], source[1])
            grad = grad.astype(BF16).reshape(GRID + (32, span))
            if number < 2:
                stage[pair_slot, :, :, :, :, :, number * span : number * span + span] = grad
            else:
                stage[value_slot, :, :, :, :, :, value_half] = grad
        sums[...] = jnp.zeros_like(sums)
        for number, source in enumerate((dq_all, dv_all)):
            added = jnp.sum(source[0].astype(F32), axis=0, keepdims=True) + jnp.sum(
                source[1].astype(F32), axis=0, keepdims=True
            )
            sums[number : number + 1, :] = added

    queue.tick(step)

    @pl.when(step == 15)
    def _():
        saves = [pltpu.make_async_copy(stage.at[BACK + n], tail_out.at[n], load_sem.at[n]) for n in range(2)]
        for save in saves:
            save.start()
        for beat in range(16, 12 + LAGS[-1]):
            queue.tick(beat)
        queue.finish()
        for save in saves:
            save.wait()


def attend_back(q, k, v, gm, mixed, lse, key_ids, query_ids, xt, rest, inner_early):
    rows, tokens, width = q.shape
    window = k.shape[1]
    groups = width // (2 * PAIR)
    whole = lambda shape: pl.BlockSpec(shape, lambda g, r, i: (0,) * len(shape), pipeline_mode=pl.Buffered(1))
    kept = lambda shape: pl.BlockSpec(shape, lambda g, r, i: (0,) * len(shape))
    per_pair = lambda n: pl.BlockSpec((1, n, PAIR), lambda g, r, i: (r, 0, g * 2 + i))
    per_row = lambda *s: pl.BlockSpec((1,) + s, lambda g, r, i: (r, 0, 0))
    hbm = pl.BlockSpec(memory_space=pltpu.HBM)
    return pl.pallas_call(
        attend_back_kernel,
        grid=(groups, rows, 2),
        out_shape=[
            jax.ShapeDtypeStruct((rows, tokens, width), BF16),
            jax.ShapeDtypeStruct((rows, window, width), BF16),
            jax.ShapeDtypeStruct((rows, window, width), BF16),
            jax.ShapeDtypeStruct((2,) + PIECE, BF16),
            jax.ShapeDtypeStruct((8, width), F32),
            jax.ShapeDtypeStruct((32, FF_PARTS * PART), F32),
            jax.ShapeDtypeStruct((32, width), F32),
            jax.ShapeDtypeStruct((4, 32, PART), F32),
        ],
        in_specs=[
            per_pair(tokens), per_pair(window), per_pair(window), per_pair(tokens), per_pair(tokens),
            pl.BlockSpec((1, 1, 8, tokens), lambda g, r, i: (r, g * 2 + i, 0, 0)),
            per_row(window, 1), per_row(1, tokens), whole(xt.shape), hbm, whole(inner_early.shape),
        ],
        out_specs=[
            per_pair(tokens), per_pair(window), per_pair(window), hbm,
            pl.BlockSpec((8, 2 * PAIR), lambda g, r, i: (0, g)),
            kept((32, FF_PARTS * PART)), kept((32, width)), kept((4, 32, PART)),
        ],
        scratch_shapes=[
            pltpu.VMEM((rows, window, tokens), F32),
            pltpu.VMEM((rows, tokens, 2 * PAIR), BF16),
            pltpu.VMEM((rows, window, 2 * PAIR), BF16),
            pltpu.VMEM((rows, window, 2 * PAIR), BF16),
            pltpu.VMEM((window, PAIR), F32),
            pltpu.VMEM((window, PAIR), F32),
            pltpu.VMEM((BACK + 2,) + PIECE, BF16),
            pltpu.SemaphoreType.DMA((LATE,)),
        ]
        + sums_buffers(BACK),
        compiler_params=pltpu.CompilerParams(
            collective_id=4, has_side_effects=True, vmem_limit_bytes=VMEM
        ),
        name="attend_back",
    )(q, k, v, gm, mixed, lse, key_ids, query_ids, xt, rest, inner_early)


def shards(vector, base, shift):
    count = vector.shape[1]
    device = lax.broadcasted_iota(jnp.int32, (32, count), 0)
    column = lax.broadcasted_iota(jnp.int32, (32, count), 1)
    rows = jnp.where(device == column >> shift, vector, 0.0).astype(BF16)
    lane = lax.broadcasted_iota(jnp.int32, (count, 128), 1)
    place = lax.broadcasted_iota(jnp.int32, (count, 128), 0)
    pick = jnp.where(lane == base + (place & (2**shift - 1)), 1.0, 0.0).astype(BF16)
    return dot(rows, pick)


def finish_kernel(
    tail_in, sums0, sums1, sums2, ib_grad, qkv_early, dq_in, dk_in, dv_in, weights_in, first_in,
    query_sum, key_sum, value_sum, small_sum, gh_out, tail_there,
    dq, dk, dv, weights, gh, tail_here, stage, small_stage, load_sem, tail_sem, *bufs,
):
    place = Place()
    loads = [
        pltpu.make_async_copy(source, target, load_sem.at[number])
        for number, (source, target) in enumerate(
            (
                (tail_in, stage),
                (weights_in.at[pl.ds(0, 3)], weights),
                (dk_in, dk),
                (dv_in, dv),
                (dq_in, dq),
                (first_in, gh),
            )
        )
    ]
    for load in loads:
        load.start()
    meet(place, -1)
    span = 2 * PAIR

    def store(j, half, value):
        rows = slice(half * 16, half * 16 + 16)
        if j == 0:
            query_sum[rows, 3 * span :] = value[:, :span]
            key_sum[rows, 3 * span :] = value[:, span:]
        else:
            value_sum[rows, 2 * span :] = value

    def store_small(j, half, value):
        small_sum[...] = value

    beats = (0, 1, 2, 3, 4)
    queue = Sums(place, 2, stage, lambda j: j, bufs[:6], store, offsets=beats)
    small = Sums(place, 1, small_stage, lambda j: j, bufs[6:], store_small, halves=1, offsets=beats)
    loads[0].wait()
    queue.tick(0)
    tokens, width = dq.shape[1], dq.shape[2]
    for load in loads[1:4]:
        load.wait()
    matrix = [weights.at[m] for m in range(3)]
    send_tail, recv_tail = place.seq > 0, place.seq < 7
    tails = [
        remote(
            tail_here.at[row], tail_there.at[row], tail_sem.at[0, row], tail_sem.at[1, row],
            place.device(z=lax.rem(place.z + 3 + place.c, 4), c=1 - place.c),
        )
        for row in range(2)
    ]
    for row in range(2):
        tail_here[row] = (
            dot_nt(dk[row, :SEGMAX, :], matrix[1][...].reshape(width, width))
            + dot_nt(dv[row, :SEGMAX, :], matrix[2][...].reshape(width, width))
        ).astype(BF16)
        pl.when(send_tail)(tails[row].start)
        if row == 0:
            queue.tick(1)
    packed = []
    vectors = [sums0[0:1], sums0[1:2], sums1[0:1], sums1[1:2], sums1[2:3], sums2[0:1], sums2[1:2], sums2[2:3]]
    for first in (0, 4):
        packed.append(sum(shards(vectors[first + n], n * 32, 5) for n in range(4)))
    inner = [ib_grad[part][:, n * 128 : n * 128 + 128] for part in range(FF_PARTS) for n in range(4)]
    packed.append(jnp.concatenate(inner, axis=0))
    packed = [p.astype(BF16).astype(F32) for p in packed]
    at = lax.broadcasted_iota(jnp.int32, (32, 16, 128), 1)
    block = jnp.zeros((32, 16, 128), F32)
    for number, value in enumerate(packed):
        block = jnp.where(at == number, jnp.broadcast_to(value[:, None, :], (32, 16, 128)), block)
    small_stage[0] = block.astype(BF16).reshape(GRID + (16, 128))

    small.tick(0)
    queue.tick(2)
    small.tick(1)
    for load in loads[4:]:
        load.wait()

    def own_rows(row):
        for column in range(0, width, 512):
            cols = slice(column, column + 512)
            total = gh[row, :, cols]
            for number, (source, first) in enumerate(((dq, 0), (dk, SEGMAX), (dv, SEGMAX))):
                part = weights[number, column // 512]
                total = total + dot_nt(source[row, first:, :], part.reshape(512, width))
            gh[row, :, cols] = total

    own_rows(0)
    queue.tick(3)
    small.tick(2)
    own_rows(1)
    save = pltpu.make_async_copy(gh, gh_out, load_sem.at[0])
    save.start()
    query_sum[:, : 3 * span] = jnp.concatenate([qkv_early[n, :, :span] for n in (0, 1, 3)], axis=1)
    key_sum[:, : 3 * span] = jnp.concatenate([qkv_early[n, :, span:] for n in (0, 1, 3)], axis=1)
    value_sum[:, : 2 * span] = qkv_early[2]
    for beat in (4, 5):
        queue.tick(beat)
        small.tick(beat - 1)
    queue.finish()
    small.finish()

    @pl.when(place.seq == 7)
    def _():
        tail_there[...] = jnp.zeros_like(tail_there)

    for tail in tails:
        pl.when(recv_tail)(tail.wait_recv)
        pl.when(send_tail)(tail.wait_send)
    save.wait()


def finish(tail_in, sums0, sums1, sums2, ib_grad, qkv_early, dq, dk, dv, weights, grad_first):
    rows, tokens, width = dq.shape
    hbm = pl.BlockSpec(memory_space=pltpu.HBM)
    vmem = pl.BlockSpec(memory_space=pltpu.VMEM)
    return pl.pallas_call(
        finish_kernel,
        out_shape=[
            jax.ShapeDtypeStruct((32, width), F32),
            jax.ShapeDtypeStruct((32, width), F32),
            jax.ShapeDtypeStruct((32, width), F32),
            jax.ShapeDtypeStruct((16, 128), F32),
            jax.ShapeDtypeStruct((rows, tokens, width), F32),
            jax.ShapeDtypeStruct((rows, SEGMAX, width), BF16),
        ],
        in_specs=[hbm] + [vmem] * 5 + [hbm] * 5,
        out_specs=[vmem] * 4 + [hbm, vmem],
        scratch_shapes=[
            pltpu.VMEM(dq.shape, BF16),
            pltpu.VMEM(dk.shape, BF16),
            pltpu.VMEM(dv.shape, BF16),
            pltpu.VMEM((3,) + weights.shape[1:], BF16),
            pltpu.VMEM((rows, tokens, width), F32),
            pltpu.VMEM((rows, SEGMAX, width), BF16),
            pltpu.VMEM((2,) + PIECE, BF16),
            pltpu.VMEM((1,) + GRID + (16, 128), BF16),
            pltpu.SemaphoreType.DMA((6,)),
            pltpu.SemaphoreType.DMA((2, 2)),
        ]
        + sums_buffers(2)
        + sums_buffers(1, 128, 1),
        compiler_params=pltpu.CompilerParams(
            collective_id=5, has_side_effects=True, vmem_limit_bytes=VMEM
        ),
        name="sum_gradients",
    )(tail_in, sums0, sums1, sums2, ib_grad, qkv_early, dq, dk, dv, weights, grad_first)


def deliver_kernel(gh, returned, *refs):
    count = len(refs) // 2
    sources, out, targets = refs[:count], refs[count], refs[count + 1 :]
    late = lax.rem(pl.program_id(0), 2) == 1
    out[...] = gh[...] + jnp.where(late, returned[...].astype(F32), 0.0)

    @pl.when(pl.program_id(0) == 0)
    def _():
        for source, target in zip(sources, targets):
            target[...] = source[...]


def deliver(gh, returned, arrays):
    rows, tokens, width = gh.shape
    whole = lambda a: pl.BlockSpec(a.shape, lambda s: (0,) * a.ndim)
    block = pl.BlockSpec((1, SEGMAX, width), lambda s: (s // 2, s % 2, 0))
    back = pl.BlockSpec((1, SEGMAX, width), lambda s: (s // 2, 0, 0))
    return pl.pallas_call(
        deliver_kernel,
        grid=(2 * rows,),
        out_shape=[jax.ShapeDtypeStruct(gh.shape, F32)] + [jax.ShapeDtypeStruct(a.shape, a.dtype) for a in arrays],
        in_specs=[block, back] + [whole(a) for a in arrays],
        out_specs=[block] + [whole(a) for a in arrays],
        compiler_params=pltpu.CompilerParams(vmem_limit_bytes=VMEM),
        name="deliver",
    )(gh, returned, *arrays)


def local(
    hidden_in, segment_ids, query_weight, query_bias, key_weight, value_weight, value_bias, output_weight,
    output_bias, first_gain, first_shift, inner_weight, inner_bias, outer_weight, outer_bias, second_gain,
    second_shift, cotangent,
):
    rows, tokens, width = hidden_in.shape
    window = tokens + SEGMAX
    vectors = (query_bias, value_bias, output_bias, first_gain, first_shift, outer_bias, second_gain, second_shift, inner_bias)
    padded = jnp.concatenate([jnp.full((rows, SEGMAX), -1, jnp.int32), segment_ids], axis=1)
    key_ids = lax.dynamic_slice_in_dim(padded, lax.axis_index("seq") * tokens, window, 1)
    query_ids = key_ids[:, None, SEGMAX:]
    key_ids = key_ids[:, :, None]
    q, k, v, xt, weights, mixed, unit, low, inner, outer, active, slope, lse, scale, vec = encode(
        hidden_in, key_ids, query_ids, vectors, query_weight, key_weight, value_weight, output_weight,
        inner_weight, outer_weight,
    )
    flat = lambda a: a.reshape(rows * tokens, a.shape[-1])
    layer_out, og, grad_second, sums2 = feed_forward(active, outer, flat(unit), flat(cotangent), vec)
    outer_sum, inner_early, rest, ib_grad, grad_first, gm, sums1 = feed_backward(
        active, slope, og, flat(low), inner, outer, grad_second, flat(unit), flat(scale), flat(mixed), weights, vec
    )
    dq, dk, dv, tail, sums0, inner_sum, wo_sum, qkv_early = attend_back(
        q, k, v, gm.reshape(rows, tokens, width), mixed, lse, key_ids, query_ids, xt, rest, inner_early
    )
    query_sum, key_sum, value_sum, small_sum, grad_hidden, returned = finish(
        tail, sums0, sums1, sums2, ib_grad, qkv_early, dq, dk, dv, weights, grad_first.reshape(rows, tokens, width)
    )
    grad_hidden, query_sum, key_sum, value_sum, wo_sum, inner_sum, outer_sum, small_sum = deliver(
        grad_hidden, returned, (query_sum, key_sum, value_sum, wo_sum, inner_sum, outer_sum, small_sum)
    )
    vector = small_sum[:2].reshape(8, 32)
    return (
        layer_out.reshape(rows, tokens, width),
        grad_hidden,
        query_sum,
        vector[0],
        key_sum,
        value_sum,
        vector[1],
        wo_sum,
        vector[2],
        vector[3],
        vector[4],
        inner_sum,
        small_sum[2],
        outer_sum,
        vector[5],
        vector[6],
        vector[7],
    )


def solution(mesh):
    in_specs = (
        P("dp", "seq", None),
        P("dp", None),
        P(("dp", "seq"), None),
        P(("dp", "seq")),
        P(("dp", "seq"), None),
        P(("dp", "seq"), None),
        P(("dp", "seq")),
        P(("dp", "seq"), None),
        P(("dp", "seq")),
        P(("dp", "seq")),
        P(("dp", "seq")),
        P(("dp", "seq"), None),
        P(("dp", "seq")),
        P(("dp", "seq"), None),
        P(("dp", "seq")),
        P(("dp", "seq")),
        P(("dp", "seq")),
        P("dp", "seq", None),
    )
    out_specs = (
        P("dp", "seq", None),
        P("dp", "seq", None),
        P(("dp", "seq"), None),
        P(("dp", "seq")),
        P(("dp", "seq"), None),
        P(("dp", "seq"), None),
        P(("dp", "seq")),
        P(("dp", "seq"), None),
        P(("dp", "seq")),
        P(("dp", "seq")),
        P(("dp", "seq")),
        P(("dp", "seq"), None),
        P(("dp", "seq")),
        P(("dp", "seq"), None),
        P(("dp", "seq")),
        P(("dp", "seq")),
        P(("dp", "seq")),
    )
    fits = dict(mesh.shape) == {"dp": 4, "seq": 8}
    body = local if fits else plain
    return jax.shard_map(body, mesh=mesh, in_specs=in_specs, out_specs=out_specs, check_vma=False)
```
